32 devices in a mesh: img: 8 (over z, y), win: 4 (over x, core).
Axes of the slice: x: 2, y: 2, z: 4, core: 2. Of those that a mesh axis runs over, the one named last changes fastest.
Arguments:
- tokens: bfloat16 [64, 4, 49, 768], P('img', 'win'), may hold values from -6 to 6
- crop_count: int32 [8], P('img'), may hold values from 1 to 8, 40 in all
- ln1_gain: float32 [2, 768], replicated, may hold values from 0.1 to 1.9
- ln1_bias: float32 [2, 768], replicated, may hold values from -1.75 to 1.75
- w_qkv: bfloat16 [2, 768, 2304], replicated, may hold values from -0.21875 to 0.21875
- b_query: float32 [2, 768], replicated, may hold values from -1.75 to 1.75
- b_value: float32 [2, 768], replicated, may hold values from -1.75 to 1.75
- bias_table: float32 [2, 169, 24], replicated, may hold values from -4 to 4
- w_out: bfloat16 [2, 768, 768], replicated, may hold values from -0.875 to 0.875
- b_out: float32 [2, 768], replicated, may hold values from -1.75 to 1.75
- ln2_gain: float32 [2, 768], replicated, may hold values from 0.1 to 1.9
- ln2_bias: float32 [2, 768], replicated, may hold values from -1.75 to 1.75
- w_up: bfloat16 [2, 768, 3072], replicated, may hold values from -0.21875 to 0.21875
- b_up: float32 [2, 3072], replicated, may hold values from -1.75 to 1.75
- w_down: bfloat16 [2, 3072, 768], replicated, may hold values from -0.109375 to 0.109375
- b_down: float32 [2, 768], replicated, may hold values from -1.75 to 1.75
- cotangent: bfloat16 [64, 4, 49, 768], P('img', 'win'), may hold values from -6 to 6
Outputs:
- block_out: bfloat16 [64, 4, 49, 768], P('img', 'win')
- grad_tokens: float32 [64, 4, 49, 768], P('img', 'win')
- grad_ln1_gain: float32 [2, 768], P(None, 'img')
- grad_ln1_bias: float32 [2, 768], P(None, 'img')
- grad_w_qkv: float32 [2, 768, 2304], P(None, 'img', 'win')
- grad_b_query: float32 [2, 768], P(None, 'img')
- grad_b_value: float32 [2, 768], P(None, 'img')
- grad_bias_table: float32 [2, 169, 24], replicated
- grad_w_out: float32 [2, 768, 768], P(None, 'img', 'win')
- grad_b_out: float32 [2, 768], P(None, 'img')
- grad_ln2_gain: float32 [2, 768], P(None, 'img')
- grad_ln2_bias: float32 [2, 768], P(None, 'img')
- grad_w_up: float32 [2, 768, 3072], P(None, 'img', 'win')
- grad_b_up: float32 [2, 3072], P(None, 'img')
- grad_w_down: float32 [2, 3072, 768], P(None, 'img', 'win')
- grad_b_down: float32 [2, 768], P(None, 'img')
The draws below stay inside these ranges and needn't reach their ends.
Inputs may be any that keep to these rules, and one draw needn't show every extreme that they name: Crop slots 0 to crop_count[i] - 1 of image group i hold crops, the others are padding; some group is full (8) in every draw.
All inputs are finite; a program needn't handle non-finite values.
Results may differ from the reference program's by a relative error of at most 0.018.
Values sent between devices are 32-bit elements; how exact they have to be, the bound alone decides.
No kernel may reach another device: no remote copies, remote signals or barrier semaphores. Data moves between devices by JAX's collectives and lax.ppermute only.
A program may use at most 576 MiB of HBM per device.

```python
import math
import jax
import jax.numpy as jnp
import numpy as np
from jax import lax

D = 768
HEADS = 24
HD = 32
FF = 3072
CAP = 8
CROPS = 64
N_IMG = 8


def block_levels(stream_key, extent, pieces, smallest, top_value):
    factor_of, own = 1.0, jax.random.fold_in(stream_key, 6)
    for position, shards_of in pieces:
        steps = jnp.exp(jax.random.uniform(jax.random.fold_in(own, position), (shards_of,), jnp.float32, smallest / len(pieces), top_value / len(pieces)))
        factor_of = factor_of * jnp.repeat(steps, extent[position] // shards_of).reshape([-1 if axis == position else 1 for axis in range(len(extent))])
    return factor_of


def length_profile(amount, total, reach, skew):
    portions = [(1 << 20) // math.isqrt(rank ** skew) + 1 for rank in range(2, amount + 1)]
    surplus, given = total - reach - (amount - 1), [1] * (amount - 1)
    while surplus > 0:
        movable = [i for i in range(amount - 1) if given[i] < reach]
        whole, remaining = sum([portions[i] for i in movable]), surplus
        for i in movable:
            more = min(reach - given[i], max(1, remaining * portions[i] // whole), surplus)
            given[i] = given[i] + more
            surplus = surplus - more
    return np.array([reach] + given)


def ragged_sizes(key, count, total, reach, lean):
    if count == 2:
        one = jax.random.randint(key, (), max(1, total - reach), min(reach, total - 1) + 1)
        return jnp.stack([one, total - one])
    sizes = jnp.asarray(length_profile(count, total, reach, lean), jnp.int32)
    pairs = (count - 1) // 2
    donor, receiver = sizes[1:1 + 2 * pairs:2], sizes[2:2 + 2 * pairs:2]
    room = jnp.minimum(donor - 1, reach - receiver)
    passed = jax.random.randint(jax.random.fold_in(key, 1), (pairs,), 0, 1 << 20) % (room + 1)
    sizes = sizes.at[1:1 + 2 * pairs:2].set(donor - passed).at[2:2 + 2 * pairs:2].set(receiver + passed)
    return sizes[jax.random.permutation(jax.random.fold_in(key, 2), count)]


def gaussian(own_key, extent, spread, most, pieces=(), kind=jnp.bfloat16):
    factor_of = block_levels(own_key, extent, pieces, -0.22, 0.18) if pieces else 1.0
    entries = jax.random.normal(own_key, extent, jnp.float32) * spread * factor_of
    return jnp.minimum(jnp.maximum(entries, -most), most).astype(kind)


def setup_inputs(seed: int = 0) -> dict:
    seeds = jax.random.split(jax.random.key(seed), 18)
    tokens = gaussian(seeds[0], (CROPS, 4, 49, D), 1.0, 6.0, ((0, 8), (1, 4)))
    crop_count = ragged_sizes(seeds[1], N_IMG, CAP * N_IMG * 5 // 8, CAP, 2).astype(jnp.int32)
    ln1_gain = jnp.clip(1.0 + 0.18 * jax.random.normal(seeds[2], (2, D), jnp.float32), 0.1, 1.9)
    ln1_bias = gaussian(seeds[3], (2, D), 0.3, 1.75, (), jnp.float32)
    w_qkv = gaussian(seeds[4], (2, D, 3 * D), D ** -0.5, 0.21875)
    b_query = gaussian(seeds[5], (2, D), 0.3, 1.75, (), jnp.float32)
    b_value = gaussian(seeds[6], (2, D), 0.3, 1.75, (), jnp.float32)
    bias_table = gaussian(seeds[7], (2, 169, HEADS), 1.0, 4.0, (), jnp.float32)
    w_out = gaussian(seeds[8], (2, D, D), (D // 16) ** -0.5, 0.875)
    b_out = gaussian(seeds[9], (2, D), 0.3, 1.75, (), jnp.float32)
    ln2_gain = jnp.clip(1.0 + 0.18 * jax.random.normal(seeds[10], (2, D), jnp.float32), 0.1, 1.9)
    ln2_bias = gaussian(seeds[11], (2, D), 0.3, 1.75, (), jnp.float32)
    w_up = gaussian(seeds[12], (2, D, FF), D ** -0.5, 0.21875)
    b_up = gaussian(seeds[13], (2, FF), 0.3, 1.75, (), jnp.float32)
    w_down = gaussian(seeds[14], (2, FF, D), FF ** -0.5, 0.109375)
    b_down = gaussian(seeds[15], (2, D), 0.3, 1.75, (), jnp.float32)
    cotangent = gaussian(seeds[16], (CROPS, 4, 49, D), 1.0, 6.0, ((0, 8), (1, 4)))
    return dict(tokens=tokens, crop_count=crop_count, ln1_gain=ln1_gain, ln1_bias=ln1_bias, w_qkv=w_qkv, b_query=b_query, b_value=b_value, bias_table=bias_table, w_out=w_out, b_out=b_out, ln2_gain=ln2_gain, ln2_bias=ln2_bias, w_up=w_up, b_up=b_up, w_down=w_down, b_down=b_down, cotangent=cotangent)


@jax.custom_vjp
def low(v):
    return lax.optimization_barrier(v.astype(jnp.bfloat16)).astype(jnp.float32)

@jax.custom_vjp
def low_back(v):
    return v

def low_keep(v):
    return (low(v), None)

def low_pass(kept, grad):
    return (grad,)

def back_keep(v):
    return (v, None)

def back_low(kept, grad):
    return (low(grad),)
low.defvjp(low_keep, low_pass)
low_back.defvjp(back_keep, back_low)
EPSILON = 1e-05

def matmul(left, right):
    return jnp.dot(left, right, precision=lax.Precision.HIGHEST, preferred_element_type=jnp.float32)

def layer_norm(values, gain_vec, shift_vec):
    average = lax.optimization_barrier(jnp.mean(values, axis=-1, keepdims=True))
    centered = values - average
    variance = lax.optimization_barrier(jnp.mean(centered * centered, axis=-1, keepdims=True))
    return centered * lax.rsqrt(variance + EPSILON) * gain_vec + shift_vec

def to_grid(windows):
    crops = windows.shape[0]
    return windows.reshape(crops, 2, 2, 7, 7, -1).transpose(0, 1, 3, 2, 4, 5).reshape(crops, 14, 14, -1)

def to_windows(grid):
    crops = grid.shape[0]
    return grid.reshape(crops, 2, 7, 2, 7, -1).transpose(0, 1, 3, 2, 4, 5).reshape(crops, 4, 49, -1)

def relative_index():
    places = jnp.arange(49, dtype=jnp.int32)
    rows_at = places // 7
    cols_at = places % 7
    return (rows_at[:, None] - rows_at[None, :] + 6) * 13 + cols_at[:, None] - cols_at[None, :] + 6

def shift_mask():
    coords = jnp.arange(14, dtype=jnp.int32)
    region = jnp.where(coords < 7, 0, jnp.where(coords < 11, 1, 2))
    labels = region[:, None] * 3 + region[None, :]
    labels = labels.reshape(2, 7, 2, 7).transpose(0, 2, 1, 3).reshape(4, 49)
    return jnp.where(labels[:, :, None] == labels[:, None, :], 0.0, -100.0).astype(jnp.float32)

def block(windows, params, index, mask):
    crops = windows.shape[0]
    hidden = low(layer_norm(windows, params['ln1_gain'][index], params['ln1_bias'][index]))
    bias_row = jnp.concatenate([params['b_query'][index], jnp.zeros((D,), jnp.float32), params['b_value'][index]])
    joint = low_back(matmul(hidden, params['w_qkv'][index]) + bias_row)
    query = low(joint[..., :D] * HD ** (-0.5)).reshape(crops, 4, 49, HEADS, HD)
    keys_in = low(joint[..., D:2 * D]).reshape(crops, 4, 49, HEADS, HD)
    vals_in = low(joint[..., 2 * D:]).reshape(crops, 4, 49, HEADS, HD)
    scores = low_back(jnp.einsum('cwthe,cwuhe->cwhtu', query, keys_in, precision=lax.Precision.HIGHEST))
    bias_heads = params['bias_table'][index][relative_index()].transpose(2, 0, 1)
    scores = scores + bias_heads[None, None] + mask[None, :, None]
    probs = jax.nn.softmax(scores, axis=-1)
    attended = jnp.einsum('cwhtu,cwuhe->cwthe', low(probs), vals_in, precision=lax.Precision.HIGHEST)
    attended = low(low_back(attended.reshape(crops, 4, 49, D)))
    middle = windows + low_back(matmul(attended, params['w_out'][index]) + params['b_out'][index])
    hidden_two = low(layer_norm(middle, params['ln2_gain'][index], params['ln2_bias'][index]))
    upward = low_back(matmul(hidden_two, params['w_up'][index]) + params['b_up'][index])
    active = low(jax.nn.gelu(upward, approximate=False))
    return middle + low_back(matmul(active, params['w_down'][index]) + params['b_down'][index])

def forward(params, windows, valid):
    first = block(windows, params, 0, jnp.zeros((4, 49, 49), jnp.float32))
    rolled = to_windows(jnp.roll(to_grid(first), (-3, -3), (1, 2)))
    second = block(rolled, params, 1, shift_mask())
    second = to_windows(jnp.roll(to_grid(second), (3, 3), (1, 2)))
    return second * valid[:, None, None, None]

def reference(tokens, crop_count, ln1_gain, ln1_bias, w_qkv, b_query, b_value, bias_table, w_out, b_out, ln2_gain, ln2_bias, w_up, b_up, w_down, b_down, cotangent):
    params = {'ln1_gain': ln1_gain.astype(jnp.float32), 'ln1_bias': ln1_bias.astype(jnp.float32), 'w_qkv': w_qkv.astype(jnp.float32), 'b_query': b_query.astype(jnp.float32), 'b_value': b_value.astype(jnp.float32), 'bias_table': bias_table.astype(jnp.float32), 'w_out': w_out.astype(jnp.float32), 'b_out': b_out.astype(jnp.float32), 'ln2_gain': ln2_gain.astype(jnp.float32), 'ln2_bias': ln2_bias.astype(jnp.float32), 'w_up': w_up.astype(jnp.float32), 'b_up': b_up.astype(jnp.float32), 'w_down': w_down.astype(jnp.float32), 'b_down': b_down.astype(jnp.float32)}
    slots = jnp.arange(CAP, dtype=jnp.int32)
    valid_all = (slots[None, :] < crop_count[:, None]).astype(jnp.float32)
    inputs = tokens.astype(jnp.float32).reshape(N_IMG, CAP, 4, 49, D)
    cotangents = cotangent.astype(jnp.float32).reshape(N_IMG, CAP, 4, 49, D)

    def one_group(carry, group):
        windows, grad_top, valid = group
        result, pullback = jax.vjp(lambda prm, xin: forward(prm, xin, valid), params, windows)
        grad_params, grad_input = pullback(grad_top)
        carry = jax.tree.map(jnp.add, carry, grad_params)
        return (carry, (result.astype(jnp.bfloat16), grad_input))
    start = jax.tree.map(jnp.zeros_like, params)
    grads, (results, grad_inputs) = lax.scan(one_group, start, (inputs, cotangents, valid_all))
    block_out = results.reshape(CROPS, 4, 49, D)
    grad_tokens = grad_inputs.reshape(CROPS, 4, 49, D)
    return (block_out, grad_tokens, grads['ln1_gain'], grads['ln1_bias'], grads['w_qkv'], grads['b_query'], grads['b_value'], grads['bias_table'], grads['w_out'], grads['b_out'], grads['ln2_gain'], grads['ln2_bias'], grads['w_up'], grads['b_up'], grads['w_down'], grads['b_down'])
```

```python
import functools

import jax
import jax.numpy as jnp
from jax import lax
from jax.experimental import pallas as pl
from jax.experimental.pallas import tpu as pltpu
from jax.sharding import PartitionSpec as P

HEADS = 24
HD = 32
SIDE = 7
T = SIDE * SIDE
TP = 56
D = 768
FF = 3072
C = 8
ROWS = T * C
PAD_ROWS = TP * C
LANE = 128
NG = D // LANE
PER = LANE // HD
GT = PER * TP
EPSILON = 1e-05
SCALE = HD ** (-0.5)
NEG = -1e30
QCH = 384
FCH = 512
N_Q = 3 * D // QCH
N_F = FF // FCH
VMEM_LIMIT = 58 << 20
F32 = jnp.float32
BF16 = jnp.bfloat16

TAIL_K = 0.3
TAIL = (
    0.11963200491345692,
    0.12071217642148169,
    0.10017566554041868,
    0.12769280877164998,
    -0.052036176065482394,
    0.20455934198696718,
    -0.15616004916725648,
    0.035424145900813254,
)
INV_SQRT_2PI = 0.3989422804014327

LOW, HIGH = range(0, 3), range(3, 7)


def cells(rows, cols):
    return [SIDE * i + j for i in rows for j in cols]


FWD_SEND = (cells(LOW, HIGH), cells(HIGH, LOW), cells(LOW, LOW))
FWD_KEEP = cells(HIGH, HIGH)
FWD_PUT = (cells(range(4, 7), range(0, 4)), cells(range(0, 4), range(4, 7)), cells(range(4, 7), range(4, 7)))
FWD_STAY = cells(range(0, 4), range(0, 4))
BACK_SEND, BACK_KEEP, BACK_PUT, BACK_STAY = FWD_PUT, FWD_STAY, FWD_SEND, FWD_KEEP
N_SEND = (12, 12, 9)


def nt(left, right):
    return lax.dot_general(left, right, (((1,), (1,)), ((), ())), preferred_element_type=F32)


def tn(left, right):
    return lax.dot_general(left, right, (((0,), (0,)), ((), ())), preferred_element_type=F32)


def nn(left, right):
    return jnp.dot(left, right, preferred_element_type=F32)


def norm_parts(values):
    average = jnp.mean(values, axis=-1, keepdims=True)
    centered = values - average
    inverse = lax.rsqrt(jnp.mean(centered * centered, axis=-1, keepdims=True) + EPSILON)
    return centered * inverse, inverse


def norm_back(grad_out, normed, inverse, gain):
    scaled = grad_out * gain
    return inverse * (
        scaled
        - jnp.mean(scaled, axis=-1, keepdims=True)
        - normed * jnp.mean(scaled * normed, axis=-1, keepdims=True)
    )


def gelu_parts(a):
    bell = jnp.exp(-0.5 * a * a)
    size = jnp.abs(a)
    t = 1.0 / (1.0 + TAIL_K * size)
    poly = jnp.full_like(t, TAIL[-1])
    for coef in TAIL[-2::-1]:
        poly = poly * t + coef
    tail = bell * (t * poly)
    phi = jnp.where(a < 0, tail, 1.0 - tail)
    return a * phi, phi + a * (INV_SQRT_2PI * bell)


def head_masks():
    lanes = lax.broadcasted_iota(jnp.int32, (TP, LANE), 1)
    return [(lanes >= HD * h) & (lanes < HD * (h + 1)) for h in range(PER)]


def spread(values, masks):
    return jnp.concatenate([jnp.where(m, values, 0.0) for m in masks], axis=0).astype(BF16)


def gather_heads(stacked, masks):
    out = stacked[(PER - 1) * TP :]
    for h in range(PER - 2, -1, -1):
        out = jnp.where(masks[h], stacked[h * TP : (h + 1) * TP], out)
    return out


def soft(scores):
    e = jnp.exp(scores - jnp.max(scores, axis=0, keepdims=True))
    return e * (1.0 / jnp.sum(e, axis=0, keepdims=True))


def colsum(values):
    return jnp.sum(values, axis=0, keepdims=True)


def crop_rows(c):
    return pl.ds(c, T, stride=C)


def pad_rows(c):
    return pl.ds(c, TP, stride=C)


def lanes_at(n, width):
    return pl.ds(pl.multiple_of(n * width, width), width)


def put_pieces(dest, own, pieces, stay, keep, put):
    for to, src in zip(stay, keep):
        dest[pl.ds(C * to, C), :] = own[src]
    for piece, places in zip(pieces, put):
        for k, to in enumerate(places):
            dest[pl.ds(C * to, C), :] = piece[k]


def take_pieces(values_ref, outs, places):
    for out, tokens in zip(outs, places):
        for k, t in enumerate(tokens):
            out[k] = values_ref[pl.ds(C * t, C), :]


def fwd_body(b, *refs):
    if b == 0:
        (tok, *rest) = refs
    else:
        (own, rx, rc, rd, *rest) = refs
    (
        bias, ln1g, ln1b, bq, bv, bout, ln2g, ln2b, bup, bdown,
        wqkv_h, wout_h, wup_h, wdown_h,
        z_o, h_o, qkvc_o, o_o, y_o, h2_o, g_o, gp_o, zn_o, sx_o, sc_o, sd_o,
        wqkv, wout, wup, wdown, qkv_s, o_s, bqkv, acc, sem_q, sem_o, sem_u, sem_d,
    ) = rest

    def cp_q(n):
        return pltpu.make_async_copy(
            wqkv_h.at[b, :, lanes_at(n, QCH)], wqkv.at[:, lanes_at(n, QCH)], sem_q.at[n]
        )

    def cp_u(n):
        return pltpu.make_async_copy(
            wup_h.at[b, :, lanes_at(n, FCH)], wup.at[:, lanes_at(n, FCH)], sem_u.at[n]
        )

    def cp_d(n):
        return pltpu.make_async_copy(
            wdown_h.at[b, lanes_at(n, FCH), :], wdown.at[lanes_at(n, FCH), :], sem_d.at[n]
        )

    cp_o = pltpu.make_async_copy(wout_h.at[b], wout, sem_o)
    for n in range(N_Q):
        cp_q(n).start()
    cp_o.start()
    for n in range(N_F):
        cp_u(n).start()
        cp_d(n).start()

    if b == 0:
        for c in range(C):
            v = tok[c].astype(F32)
            for g in range(NG):
                o_s[g, crop_rows(c), :] = v[:, LANE * g : LANE * (g + 1)]
        for g in range(NG):
            z_o[:, LANE * g : LANE * (g + 1)] = o_s[g, 0:ROWS, :]
    else:
        put_pieces(z_o, own, (rx, rc, rd), FWD_STAY, FWD_KEEP, FWD_PUT)
    normed, _ = norm_parts(z_o[...])
    h_o[...] = (normed * ln1g[b : b + 1, :] + ln1b[b : b + 1, :]).astype(BF16)
    bqkv[:, 0:D] = bq[b : b + 1, :]
    bqkv[:, D : 2 * D] = jnp.zeros((1, D), F32)
    bqkv[:, 2 * D :] = bv[b : b + 1, :]
    qkv_s[:, ROWS:, :] = jnp.zeros((3 * NG, PAD_ROWS - ROWS, LANE), F32)

    def qkv_step(n, _):
        cp_q(n).wait()
        joint = nn(h_o[...], wqkv[:, lanes_at(n, QCH)]) + bqkv[:, lanes_at(n, QCH)]
        joint = joint * jnp.where(n < D // QCH, SCALE, 1.0)
        joint = joint.astype(BF16).astype(F32)
        for k in range(QCH // LANE):
            qkv_s[n * (QCH // LANE) + k, 0:ROWS, :] = joint[:, LANE * k : LANE * (k + 1)]
        return 0

    lax.fori_loop(0, N_Q, qkv_step, 0)
    masks = head_masks()

    def attend(c, _):
        for g in range(NG):
            q = qkv_s[g, pad_rows(c), :]
            k = qkv_s[NG + g, pad_rows(c), :].astype(BF16)
            v = qkv_s[2 * NG + g, pad_rows(c), :].astype(BF16)
            qkvc_o[c, g] = q.astype(BF16)
            qkvc_o[c, NG + g] = k
            qkvc_o[c, 2 * NG + g] = v
            probs = soft(nt(k, spread(q, masks)) + bias[g])
            o_s[g, pad_rows(c), :] = gather_heads(tn(probs.astype(BF16), v), masks)
        return 0

    lax.fori_loop(0, C, attend, 0)
    for g in range(NG):
        o_o[:, LANE * g : LANE * (g + 1)] = o_s[g, 0:ROWS, :].astype(BF16)
    cp_o.wait()
    y = z_o[...] + (nn(o_o[...], wout[...]) + bout[b : b + 1, :])
    y_o[...] = y
    normed, _ = norm_parts(y)
    h2_o[...] = (normed * ln2g[b : b + 1, :] + ln2b[b : b + 1, :]).astype(BF16)
    acc[...] = jnp.zeros_like(acc)

    def mlp_step(n, _):
        cp_u(n).wait()
        a = nn(h2_o[...], wup[:, lanes_at(n, FCH)]) + bup[b : b + 1, lanes_at(n, FCH)]
        act, slope = gelu_parts(a)
        act = act.astype(BF16)
        g_o[:, lanes_at(n, FCH)] = act
        gp_o[:, lanes_at(n, FCH)] = slope.astype(BF16)
        cp_d(n).wait()
        acc[...] += nn(act, wdown[lanes_at(n, FCH), :])
        return 0

    lax.fori_loop(0, N_F, mlp_step, 0)
    acc[...] = y_o[...] + (acc[...] + bdown[b : b + 1, :])
    zn_o[...] = acc[...].reshape(T, C, D)
    take_pieces(acc, (sx_o, sc_o, sd_o), FWD_SEND if b == 0 else BACK_SEND)


ANY = pl.BlockSpec(memory_space=pl.ANY)
VM = pl.BlockSpec(memory_space=pltpu.VMEM)
SM = pl.BlockSpec(memory_space=pltpu.SMEM)


def params_of():
    return pltpu.CompilerParams(vmem_limit_bytes=VMEM_LIMIT)


def cost(flops, nbytes):
    return pl.CostEstimate(flops=int(flops), bytes_accessed=int(nbytes), transcendentals=0)


def shape(dims, dtype):
    return jax.ShapeDtypeStruct(dims, dtype)


PIECES = [shape((T, C, D), F32)] + [shape((n, C, D), F32) for n in N_SEND]


def block_fwd(b, sources, bias, p):
    outs = [
        shape((ROWS, D), F32),
        shape((ROWS, D), BF16),
        shape((C, 3 * NG, TP, LANE), BF16),
        shape((ROWS, D), BF16),
        shape((ROWS, D), F32),
        shape((ROWS, D), BF16),
        shape((ROWS, FF), BF16),
        shape((ROWS, FF), BF16),
    ] + PIECES
    small = (bias, p["ln1_gain"], p["ln1_bias"], p["b_query"], p["b_value"], p["b_out"],
             p["ln2_gain"], p["ln2_bias"], p["b_up"], p["b_down"])
    big = (p["w_qkv"], p["w_out"], p["w_up"], p["w_down"])
    return pl.pallas_call(
        functools.partial(fwd_body, b),
        in_specs=[VM] * (len(sources) + len(small)) + [ANY] * 4,
        out_specs=[VM] * len(outs),
        out_shape=outs,
        scratch_shapes=[
            pltpu.VMEM((D, 3 * D), BF16),
            pltpu.VMEM((D, D), BF16),
            pltpu.VMEM((D, FF), BF16),
            pltpu.VMEM((FF, D), BF16),
            pltpu.VMEM((3 * NG, PAD_ROWS, LANE), F32),
            pltpu.VMEM((NG, PAD_ROWS, LANE), F32),
            pltpu.VMEM((1, 3 * D), F32),
            pltpu.VMEM((ROWS, D), F32),
            pltpu.SemaphoreType.DMA((N_Q,)),
            pltpu.SemaphoreType.DMA,
            pltpu.SemaphoreType.DMA((N_F,)),
            pltpu.SemaphoreType.DMA((N_F,)),
        ],
        compiler_params=params_of(),
        cost_estimate=cost(2 * ROWS * 12 * D * D, 30e6),
        name=f"forward_{b}",
    )(*sources, *small, *big)


def cot_body(count, ct, own_o, sx_o, sc_o, sd_o, s, full):
    for c in range(C):
        keep = jnp.where(c < count[0], 1.0, 0.0).astype(F32)
        v = ct[c].astype(F32) * keep
        for g in range(NG):
            s[g, crop_rows(c), :] = v[:, LANE * g : LANE * (g + 1)]
    for g in range(NG):
        full[:, LANE * g : LANE * (g + 1)] = s[g]
    own_o[...] = full[...].reshape(T, C, D)
    take_pieces(full, (sx_o, sc_o, sd_o), FWD_SEND)


def cotangent_pieces(count, ct):
    return pl.pallas_call(
        cot_body,
        in_specs=[SM, VM],
        out_specs=[VM] * 4,
        out_shape=PIECES,
        scratch_shapes=[pltpu.VMEM((NG, ROWS, LANE), F32), pltpu.VMEM((ROWS, D), F32)],
        compiler_params=params_of(),
        cost_estimate=cost(0, 6e6),
        name="cotangent_pieces",
    )(count, ct)


def join_body(forward, own, rx, rc, rd, dz_o, dd_o, db_o):
    ways = (FWD_STAY, FWD_KEEP, FWD_PUT) if forward else (BACK_STAY, BACK_KEEP, BACK_PUT)
    put_pieces(dz_o, own, (rx, rc, rd), *ways)
    dd = dz_o[...].astype(BF16)
    db_o[...] = colsum(dd.astype(F32))
    w = D // 4
    for c in range(2):
        dd_o[c] = jnp.concatenate(
            [dd[:, w * c : w * (c + 1)], dd[:, w * (2 + c) : w * (3 + c)]], axis=1
        )


def join_grad(forward, own, received):
    return pl.pallas_call(
        functools.partial(join_body, forward),
        in_specs=[VM] * 4,
        out_specs=[VM] * 3,
        out_shape=[shape((ROWS, D), F32), shape((2, ROWS, D // 2), BF16), shape((1, D), F32)],
        compiler_params=params_of(),
        cost_estimate=cost(0, 5e6),
        name="join_grad",
    )(own, *received)


def block_out_body(count, own, rx, rc, rd, out, full, s):
    put_pieces(full, own, (rx, rc, rd), BACK_STAY, BACK_KEEP, BACK_PUT)
    for g in range(NG):
        s[g] = full[:, LANE * g : LANE * (g + 1)]
    for c in range(C):
        keep = jnp.where(c < count[0], 1.0, 0.0).astype(F32)
        for g in range(NG):
            out[c, :, LANE * g : LANE * (g + 1)] = (s[g, crop_rows(c), :] * keep).astype(BF16)


def block_output(count, own, received):
    return pl.pallas_call(
        block_out_body,
        in_specs=[SM] + [VM] * 4,
        out_specs=VM,
        out_shape=shape((C, T, D), BF16),
        scratch_shapes=[pltpu.VMEM((ROWS, D), F32), pltpu.VMEM((NG, ROWS, LANE), F32)],
        compiler_params=params_of(),
        cost_estimate=cost(0, 4e6),
        name="block_output",
    )(count, own, *received)


def mlp_back_body(b, dz, y, ln2g, gp_h, wdown_h, wup_h, da_o, dy_o, dyr_o, sv_o, dbup_o,
                  gp, wdown, wup, acc, dd, sem_g, sem_d, sem_u):
    def cp_g(n):
        return pltpu.make_async_copy(
            gp_h.at[:, lanes_at(n, FCH)], gp.at[:, lanes_at(n, FCH)], sem_g.at[n]
        )

    def cp_u(n):
        return pltpu.make_async_copy(
            wup_h.at[b, :, lanes_at(n, FCH)], wup.at[:, lanes_at(n, FCH)], sem_u.at[n]
        )

    def cp_d(n):
        return pltpu.make_async_copy(
            wdown_h.at[b, lanes_at(n, FCH), :], wdown.at[lanes_at(n, FCH), :], sem_d.at[n]
        )

    for n in range(N_F):
        cp_d(n).start()
        cp_g(n).start()
        cp_u(n).start()
    dd[...] = dz[...].astype(BF16)
    acc[...] = jnp.zeros_like(acc)

    def step(n, _):
        cp_d(n).wait()
        grad_act = nt(dd[...], wdown[lanes_at(n, FCH), :])
        cp_g(n).wait()
        da = (grad_act * gp[:, lanes_at(n, FCH)].astype(F32)).astype(BF16)
        da_o[:, lanes_at(n, FCH)] = da
        dbup_o[:, lanes_at(n, FCH)] = colsum(da.astype(F32))
        cp_u(n).wait()
        acc[...] += nt(da, wup[:, lanes_at(n, FCH)])
        return 0

    lax.fori_loop(0, N_F, step, 0)
    dh2 = acc[...]
    normed, inverse = norm_parts(y[...])
    sv_o[0:1, :] = colsum(dh2 * normed)
    sv_o[1:2, :] = colsum(dh2)
    dy = dz[...] + norm_back(dh2, normed, inverse, ln2g[b : b + 1, :])
    dy_o[...] = dy
    low = dy.astype(BF16)
    dyr_o[...] = low
    sv_o[2:3, :] = colsum(low.astype(F32))


def mlp_back(b, dz, y, gp, p):
    return pl.pallas_call(
        functools.partial(mlp_back_body, b),
        in_specs=[VM] * 3 + [ANY] * 3,
        out_specs=[VM] * 5,
        out_shape=[
            shape((ROWS, FF), BF16),
            shape((ROWS, D), F32),
            shape((ROWS, D), BF16),
            shape((3, D), F32),
            shape((1, FF), F32),
        ],
        scratch_shapes=[
            pltpu.VMEM((ROWS, FF), BF16),
            pltpu.VMEM((FF, D), BF16),
            pltpu.VMEM((D, FF), BF16),
            pltpu.VMEM((ROWS, D), F32),
            pltpu.VMEM((ROWS, D), BF16),
            pltpu.SemaphoreType.DMA((N_F,)),
            pltpu.SemaphoreType.DMA((N_F,)),
            pltpu.SemaphoreType.DMA((N_F,)),
        ],
        compiler_params=params_of(),
        cost_estimate=cost(2 * ROWS * 8 * D * D, 20e6),
        name=f"mlp_back_{b}",
    )(dz, y, p["ln2_gain"], gp, p["w_down"], p["w_up"])


def attn_back_body(b, dyr, qkvc, bias, dy, z, ln1g, wout_h, wqkv_h, *refs):
    if b == 0:
        (r3_o, sv_o, ds_o, out, wout, wqkv, do_s, dqkv_s, dq, acc, sem_o, sem_q) = refs
    else:
        (r3_o, sv_o, ds_o, own_o, sx_o, sc_o, sd_o,
         wout, wqkv, do_s, dqkv_s, dq, acc, sem_o, sem_q) = refs
    cp_o = pltpu.make_async_copy(wout_h.at[b], wout, sem_o)
    cp_o.start()

    def cp_q(n):
        return pltpu.make_async_copy(
            wqkv_h.at[b, :, lanes_at(n, QCH)], wqkv.at[:, lanes_at(n, QCH)], sem_q.at[n]
        )

    for n in range(N_Q):
        cp_q(n).start()
    do_s[:, ROWS:, :] = jnp.zeros((NG, PAD_ROWS - ROWS, LANE), F32)
    ds_o[...] = jnp.zeros_like(ds_o)
    cp_o.wait()
    do = nt(dyr[...], wout[...]).astype(BF16).astype(F32)
    for g in range(NG):
        do_s[g, 0:ROWS, :] = do[:, LANE * g : LANE * (g + 1)]
    masks = head_masks()

    def attend(c, _):
        for g in range(NG):
            q = qkvc[c, g]
            k = qkvc[c, NG + g]
            v = qkvc[c, 2 * NG + g]
            q_wide = spread(q.astype(F32), masks)
            do_wide = spread(do_s[g, pad_rows(c), :], masks)
            probs = soft(nt(k, q_wide) + bias[g])
            weighted = probs * nt(v, do_wide)
            ds = weighted - probs * jnp.sum(weighted, axis=0, keepdims=True)
            ds_o[g] += ds
            low = ds.astype(BF16)
            dqkv_s[g, pad_rows(c), :] = gather_heads(tn(low, k), masks) * SCALE
            dqkv_s[NG + g, pad_rows(c), :] = nn(low, q_wide)
            dqkv_s[2 * NG + g, pad_rows(c), :] = nn(probs.astype(BF16), do_wide)
        return 0

    lax.fori_loop(0, C, attend, 0)
    for g in range(3 * NG):
        dq[:, LANE * g : LANE * (g + 1)] = dqkv_s[g, 0:ROWS, :].astype(BF16)
    sv_o[2:3, :] = colsum(dq[:, 0:D].astype(F32))
    sv_o[3:4, :] = colsum(dq[:, 2 * D :].astype(F32))
    acc[...] = jnp.zeros_like(acc)

    def step(n, _):
        cp_q(n).wait()
        acc[...] += nt(dq[:, lanes_at(n, QCH)], wqkv[:, lanes_at(n, QCH)])
        return 0

    lax.fori_loop(0, N_Q, step, 0)
    wq, wo = 3 * D // 4, D // 4
    for c in range(2):
        for x in range(2):
            w = 2 * x + c
            r3_o[c, :, D * x : D * (x + 1)] = jnp.concatenate(
                [dq[:, wq * w : wq * (w + 1)], dyr[:, wo * w : wo * (w + 1)]], axis=1
            )
    dh = acc[...]
    normed, inverse = norm_parts(z[...])
    sv_o[0:1, :] = colsum(dh * normed)
    sv_o[1:2, :] = colsum(dh)
    acc[...] = dy[...] + norm_back(dh, normed, inverse, ln1g[b : b + 1, :])
    if b == 0:
        for g in range(NG):
            do_s[g, 0:ROWS, :] = acc[:, LANE * g : LANE * (g + 1)]
        for c in range(C):
            for g in range(NG):
                out[c, :, LANE * g : LANE * (g + 1)] = do_s[g, crop_rows(c), :]
    else:
        own_o[...] = acc[...].reshape(T, C, D)
        take_pieces(acc, (sx_o, sc_o, sd_o), BACK_SEND)


def attn_back(b, dyr, qkvc, bias, dy, z, p):
    outs = [
        shape((2, ROWS, 2 * D), BF16),
        shape((4, D), F32),
        shape((NG, TP, GT), F32),
    ] + ([shape((C, T, D), F32)] if b == 0 else PIECES)
    return pl.pallas_call(
        functools.partial(attn_back_body, b),
        in_specs=[VM] * 6 + [ANY] * 2,
        out_specs=[VM] * len(outs),
        out_shape=outs,
        scratch_shapes=[
            pltpu.VMEM((D, D), BF16),
            pltpu.VMEM((D, 3 * D), BF16),
            pltpu.VMEM((NG, PAD_ROWS, LANE), F32),
            pltpu.VMEM((3 * NG, PAD_ROWS, LANE), F32),
            pltpu.VMEM((ROWS, 3 * D), BF16),
            pltpu.VMEM((ROWS, D), F32),
            pltpu.SemaphoreType.DMA,
            pltpu.SemaphoreType.DMA((N_Q,)),
        ],
        compiler_params=params_of(),
        cost_estimate=cost(2 * ROWS * 6 * D * D, 20e6),
        name=f"attn_back_{b}",
    )(dyr, qkvc, bias, dy, z, p["ln1_gain"], p["w_out"], p["w_qkv"])


def weight_grad(kind, core, left, right, received=None):
    if kind == "up":
        grid = (2, 2)
        specs = [
            pl.BlockSpec((ROWS, D), lambda x, n, s: (0, 0)),
            pl.BlockSpec((ROWS, D // 2), lambda x, n, s: (0, (x * 2 + s[0]) * 2 + n)),
        ]
        out_spec = pl.BlockSpec((1, D, D // 2), lambda x, n, s: (x, 0, n))
        out = shape((2, D, D), F32)
    elif kind == "down":
        grid = (4,)
        specs = [
            pl.BlockSpec((1, ROWS, D // 2), lambda m, s: (s[0], 0, 0)),
            pl.BlockSpec((ROWS, FF // 4), lambda m, s: (0, m)),
        ]
        out_spec = pl.BlockSpec((2, D // 2, FF // 8), lambda m, s: (m, 0, 0))
        out = shape((8, D // 2, FF // 8), F32)
    else:
        grid = (2,)
        specs = [
            pl.BlockSpec((ROWS, D), lambda x, s: (0, 0)),
            pl.BlockSpec((ROWS, D), lambda x, s: (0, 0)),
            pl.BlockSpec((1, ROWS, D), lambda x, s: (s[0], 0, x)),
        ]
        out_spec = pl.BlockSpec((1, D, D), lambda x, s: (x, 0, 0))
        out = shape((2, D, D), F32)

    def body(s, *refs):
        got = None
        if received is not None:
            got = refs[-2]
        o = refs[-1]

        def put(where, value):
            o[where] = value if got is None else value + got[where]

        if kind == "up":
            put((0,), tn(refs[0][...], refs[1][...]))
        elif kind == "down":
            for k in range(2):
                put((k,), tn(refs[0][0], refs[1][:, k * (FF // 8) : (k + 1) * (FF // 8)]))
        else:
            hid, att, r = refs[0][...], refs[1][...], refs[2]
            edge = 3 * D // 4
            lo = edge // LANE * LANE
            put((0, slice(None), slice(0, lo)), tn(hid, r[0, :, 0:lo]))
            mid = r[0, :, lo : lo + LANE]
            lane = lax.broadcasted_iota(jnp.int32, (D, LANE), 1)
            put(
                (0, slice(None), slice(lo, lo + LANE)),
                jnp.where(lane < edge - lo, tn(hid, mid), tn(att, mid)),
            )
            put((0, slice(None), slice(lo + LANE, D)), tn(att, r[0, :, lo + LANE :]))

    args = [*left, right]
    if received is not None:
        args.append(received.reshape(out.shape))
        specs.append(out_spec)
    return pl.pallas_call(
        body,
        grid_spec=pltpu.PrefetchScalarGridSpec(
            num_scalar_prefetch=1, grid=grid, in_specs=specs, out_specs=out_spec
        ),
        out_shape=out,
        compiler_params=params_of(),
        cost_estimate=cost(2 * ROWS * 2 * D * D, 6e6 if received is None else 11e6),
        name=f"weight_grad_{kind}",
    )(core, *args)


def insert_bit(i, place, bit):
    return ((i >> place) << (place + 1)) | (bit << place) | (i & ((1 << place) - 1))


def split_sum(kept, fixed, recv, place, bits):
    n, r, w = recv.shape

    def at_recv(flip):
        return lambda i, s: (insert_bit(i, place, s[0] ^ flip), 0, 0)

    def at_kept(flip):
        if fixed is None:
            return at_recv(flip)
        return lambda i, s: (insert_bit(insert_bit(i, place, s[0] ^ flip), fixed, s[1]), 0, 0)

    def body(s, ka, ra, kb, rb, keep_o, send_o):
        keep_o[...] = ka[...] + ra[...]
        send_o[...] = kb[...] + rb[...]

    block = (1, r, w)
    return pl.pallas_call(
        body,
        grid_spec=pltpu.PrefetchScalarGridSpec(
            num_scalar_prefetch=1,
            grid=(n // 2,),
            in_specs=[
                pl.BlockSpec(block, at_kept(0)),
                pl.BlockSpec(block, at_recv(0)),
                pl.BlockSpec(block, at_kept(1)),
                pl.BlockSpec(block, at_recv(1)),
            ],
            out_specs=[pl.BlockSpec(block, lambda i, s: (i, 0, 0))] * 2,
        ),
        out_shape=[shape((n // 2, r, w), F32)] * 2,
        compiler_params=params_of(),
        cost_estimate=cost(n * r * w, 12 * n * r * w),
        name="split_sum",
    )(bits, kept, recv, kept, recv)


def scatter_sum(full, names, order, links):
    names = list(names)
    place = len(names) - 1 - names.index(order[0])
    axis, perm, bit = links[order[0]]
    n, r, w = full.shape
    view = full.reshape(n >> (place + 1), 2, 1 << place, r, w)
    send = lax.dynamic_index_in_dim(view, 1 - bit, 1, False).reshape(n // 2, r, w)
    recv = lax.ppermute(send, axis, perm)
    kept, fixed, fixed_bit = full, place, bit
    names.remove(order[0])
    for name in order[1:]:
        place = len(names) - 1 - names.index(name)
        axis, perm, bit = links[name]
        kept, send = split_sum(kept, fixed, recv, place, jnp.stack([bit, fixed_bit]))
        recv = lax.ppermute(send, axis, perm)
        fixed, fixed_bit = None, bit * 0
        names.remove(name)
    return (kept + recv)[0]


def scatter_rest(block, dim, img, sub):
    step = sub // 2
    while step:
        bit = (img // step) % 2
        half = block.shape[dim] // 2
        keep = lax.dynamic_slice_in_dim(block, bit * half, half, dim)
        send = lax.dynamic_slice_in_dim(block, (1 - bit) * half, half, dim)
        perm = [(i, i ^ step) for i in range(8 * sub)]
        block = keep + lax.ppermute(send, "img", perm)
        step //= 2
    return block


def relative_onehot():
    places = jnp.arange(TP, dtype=jnp.int32)
    rows_at, cols_at = places // SIDE, places % SIDE
    rel = (rows_at[None, :] - rows_at[:, None] + 6) * 13 + cols_at[None, :] - cols_at[:, None] + 6
    real = (places[:, None] < T) & (places[None, :] < T)
    rel = jnp.where(real, rel, -1)
    return (jnp.arange(169, dtype=jnp.int32)[:, None] == rel.reshape(1, -1)).astype(F32)


def region_of(coords):
    return jnp.where(coords < 7, 0, jnp.where(coords < 11, 1, 2))


def spread_bias(bias_table, onehot, quadrant):
    rows = jnp.dot(
        bias_table.transpose(0, 2, 1).reshape(2 * HEADS, 169),
        onehot,
        precision=lax.Precision.HIGHEST,
        preferred_element_type=F32,
    )
    rows = rows.reshape(2, NG, PER, TP, TP).transpose(0, 1, 3, 2, 4)
    places = jnp.arange(TP, dtype=jnp.int32)
    labels = 3 * region_of(quadrant // 2 * 7 + places // 7) + region_of(quadrant % 2 * 7 + places % 7)
    mask = jnp.where(labels[:, None] == labels[None, :], 0.0, -100.0).astype(F32)
    mask = jnp.stack([jnp.zeros_like(mask), mask])
    mask = jnp.where((places < T)[None, :, None], mask, NEG)
    return (rows + mask[:, None, :, None, :]).reshape(2, NG, TP, GT)


def per_device(
    tokens, crop_count, ln1_gain, ln1_bias, w_qkv, b_query, b_value, bias_table, w_out, b_out,
    ln2_gain, ln2_bias, w_up, b_up, w_down, b_down, cotangent, *, n_img,
):
    win, img = lax.axis_index("win"), lax.axis_index("img")
    sub = n_img // 8
    x_bit, core = win // 2, win % 2
    links = {"x": ("win", [(i, i ^ 2) for i in range(4)], x_bit)}
    for k in range(3):
        links[k] = ("img", [(i, i ^ (sub << k)) for i in range(n_img)], (img // (sub << k)) % 2)
    core_swap = [(i, i ^ 1) for i in range(4)]
    mine, other = jnp.reshape(core, (1,)), jnp.reshape(1 - core, (1,))
    p = dict(
        ln1_gain=ln1_gain, ln1_bias=ln1_bias, w_qkv=w_qkv, b_query=b_query, b_value=b_value,
        w_out=w_out, b_out=b_out, ln2_gain=ln2_gain, ln2_bias=ln2_bias, w_up=w_up, b_up=b_up,
        w_down=w_down, b_down=b_down,
    )

    def exchange(pieces):
        ways = ([(i, i ^ 2) for i in range(4)], core_swap, [(i, i ^ 3) for i in range(4)])
        return [lax.ppermute(a, "win", way) for a, way in zip(pieces, ways)]

    onehot = relative_onehot()
    biases = spread_bias(bias_table, onehot, win)
    fwd = [None, None]
    out = block_fwd(0, (tokens[:, 0],), biases[0], p)
    fwd[0] = out[:8]
    ct_own, *ct_send = cotangent_pieces(crop_count, cotangent[:, 0])
    dz, dd, db_down = join_grad(True, ct_own, exchange(ct_send))
    out = block_fwd(1, (out[8], *exchange(out[9:])), biases[1], p)
    fwd[1] = out[:8]
    block_out = block_output(crop_count, out[8], exchange(out[9:]))

    def core_sum(kind, left, right):
        theirs = weight_grad(kind, other, left, right)
        return weight_grad(kind, mine, left, right, lax.ppermute(theirs, "win", core_swap))

    rows, tables, mats = [None, None], [None, None], [None, None]
    side = ("x", 2, 1, 0)
    for b in (1, 0):
        z, h, qkvc, o, y, h2, g, gp = fwd[b]
        full = core_sum("down", [dd], g)
        g_down = scatter_sum(full.reshape(16, D // 4, FF // 8), (2, 1, 0, "x"), (0, "x", 1, 2), links)
        da, dy, dyr, sv_m, db_up = mlp_back(b, dz, y, gp, p)
        full = core_sum("up", [h2], da)
        g_up = scatter_sum(full.reshape(16, D // 8, D), side, ("x", 0, 1, 2), links)
        outs = attn_back(b, dyr, qkvc, biases[b], dy, z, p)
        r3, sv_a, ds = outs[:3]
        rows[b] = jnp.concatenate([sv_a, sv_m, db_down, db_up.reshape(4, D)], axis=0)
        tables[b] = ds
        if b == 1:
            dz, dd, db_down = join_grad(False, outs[3], exchange(outs[4:]))
        else:
            grad_tokens = outs[3][:, None]
        full = core_sum("attn", [h, o], r3)
        order = (1, "x", 0, 2) if b else (1, 0, "x", 2)
        g_att = scatter_sum(full.reshape(16, D // 8, D), side, order, links)
        g_up, g_att = (scatter_rest(v, 0, img, sub) for v in (g_up, g_att))
        g_down = scatter_rest(g_down, 1, img, sub)
        mats[b] = (g_att[:, : 3 * D // 4], g_att[:, 3 * D // 4 :], g_up, g_down.T)

    g_qkv, g_out, g_up, g_down = (jnp.stack(pair) for pair in zip(*mats))
    ds = jnp.stack(tables).reshape(2, NG, TP, PER, TP).transpose(0, 1, 3, 2, 4)
    table = lax.dot_general(
        ds.reshape(2 * HEADS, TP * TP),
        onehot,
        (((1,), (1,)), ((), ())),
        precision=lax.Precision.HIGHEST,
        preferred_element_type=F32,
    )
    table = jnp.pad(table, ((0, 0), (0, 256 - 169))).reshape(2 * HEADS // 3, D)
    small = jnp.concatenate(rows + [table], axis=0)
    for axis, size in (("win", 4), ("img", n_img)):
        step = 1
        while step < size:
            small = small + lax.ppermute(small, axis, [(i, i ^ step) for i in range(size)])
            step *= 2
    table = small[24:].reshape(2, HEADS, 256)[:, :, :169].transpose(0, 2, 1)
    width = D // n_img

    def share(first, n=1):
        full = small[:24].reshape(2, 12, D)[:, first : first + n].reshape(2, n * D)
        return lax.dynamic_slice_in_dim(full, img * (n * width), n * width, 1)

    return (
        block_out[:, None], grad_tokens, share(0), share(1), g_qkv, share(2), share(3), table,
        g_out, share(6), share(4), share(5), g_up, share(8, 4), g_down, share(7),
    )


def solution(mesh):
    shard = P("img", "win", None, None)
    vec, mat = P(None, "img"), P(None, "img", "win")
    return jax.shard_map(
        functools.partial(per_device, n_img=mesh.shape["img"]),
        mesh=mesh,
        in_specs=(shard, P("img")) + (P(),) * 14 + (shard,),
        out_specs=(shard, shard, vec, vec, mat, vec, vec, P(), mat, vec, vec, vec, mat, vec, mat, vec),
        check_vma=False,
    )
```

```python
import functools

import jax
import jax.numpy as jnp
from jax import lax
from jax.experimental import pallas as pl
from jax.experimental.pallas import tpu as pltpu
from jax.sharding import PartitionSpec as P

HEADS = 24
HD = 32
SIDE = 7
T = SIDE * SIDE
TP = 56
TQ = 64
D = 768
FF = 3072
C = 8
ROWS = T * C
PAD_ROWS = TQ * C
HALF = C // 2
PIECE = T * HALF
LANE = 128
NG = D // LANE
PER = LANE // HD
GT = PER * TQ
EPSILON = 1e-05
SCALE = HD ** (-0.5)
NEG = -1e30
QCH = 384
FCH = 768
N_Q = 3 * D // QCH
N_F = FF // FCH
W_UP = D // 2
MINE = D // 4
VMEM_LIMIT = 58 << 20
COST = 0.4
F32 = jnp.float32
BF16 = jnp.bfloat16

TAIL_K = 0.3
TAIL = (
    0.11963200491345692,
    0.12071217642148169,
    0.10017566554041868,
    0.12769280877164998,
    -0.052036176065482394,
    0.20455934198696718,
    -0.15616004916725648,
    0.035424145900813254,
)
INV_SQRT_2PI = 0.3989422804014327

def nt(left, right):
    return lax.dot_general(left, right, (((1,), (1,)), ((), ())), preferred_element_type=F32)


def tn(left, right):
    return lax.dot_general(left, right, (((0,), (0,)), ((), ())), preferred_element_type=F32)


def nn(left, right):
    return jnp.dot(left, right, preferred_element_type=F32)


def norm_parts(values):
    average = jnp.mean(values, axis=-1, keepdims=True)
    centered = values - average
    inverse = lax.rsqrt(jnp.mean(centered * centered, axis=-1, keepdims=True) + EPSILON)
    return centered * inverse, inverse


def norm_back(grad_out, normed, inverse, gain):
    scaled = grad_out * gain
    return inverse * (
        scaled
        - jnp.mean(scaled, axis=-1, keepdims=True)
        - normed * jnp.mean(scaled * normed, axis=-1, keepdims=True)
    )


def gelu_parts(a):
    bell = jnp.exp(-0.5 * a * a)
    size = jnp.abs(a)
    t = 1.0 / (1.0 + TAIL_K * size)
    poly = jnp.full_like(t, TAIL[-1])
    for coef in TAIL[-2::-1]:
        poly = poly * t + coef
    tail = bell * (t * poly)
    phi = jnp.where(a < 0, tail, 1.0 - tail)
    return a * phi, phi + a * (INV_SQRT_2PI * bell)


def head_masks(rows):
    lanes = lax.broadcasted_iota(jnp.int32, (rows, LANE), 1)
    return [(lanes >= HD * h) & (lanes < HD * (h + 1)) for h in range(PER)]


def spread(values, ones):
    return jnp.concatenate([values * m for m in ones], axis=0)


def gather_heads(stacked, masks):
    out = stacked[(PER - 1) * TQ : (PER - 1) * TQ + TP]
    for h in range(PER - 2, -1, -1):
        out = jnp.where(masks[h], stacked[h * TQ : h * TQ + TP], out)
    return out


def soft(scores):
    e = jnp.exp(scores - jnp.max(scores, axis=0, keepdims=True))
    return e * (1.0 / jnp.sum(e, axis=0, keepdims=True))


def colsum(values):
    return jnp.sum(values, axis=0, keepdims=True)


def rows_of(w, n=T, stride=C):
    return pl.ds(w, n, stride=stride)


def lanes_at(n, width):
    return pl.ds(pl.multiple_of(n * width, width), width)


def put_rolled(dest, source, a, back):
    shift, kept = (-3, range(3, 7)) if back else (3, range(0, 4))
    for i in range(SIDE):
        for j in range(SIDE):
            half = a if i in kept else 1 - a
            tile = source[half, SIDE * ((i + shift) % SIDE) + (j + shift) % SIDE]
            if j not in kept:
                tile = pltpu.roll(tile, HALF, 0)
            t = SIDE * i + j
            dest[C * t : C * (t + 1), :] = tile


ANY = pl.BlockSpec(memory_space=pl.ANY)
VM = pl.BlockSpec(memory_space=pltpu.VMEM)
SM = pl.BlockSpec(memory_space=pltpu.SMEM)


def cost(micros):
    return pl.CostEstimate(flops=int(micros * COST * 1.15e9), bytes_accessed=0, transcendentals=0)


def shape(dims, dtype):
    return jax.ShapeDtypeStruct(dims, dtype)


def fixed(dims, single=False):
    mode = dict(pipeline_mode=pl.Buffered(1)) if single else {}
    return pl.BlockSpec(dims, lambda *_: (0,) * len(dims), **mode)


def per_half(dims):
    return pl.BlockSpec((1, *dims), lambda a, *_: (a, *(0,) * len(dims)))


def call(body, args, in_specs, outs, out_specs, estimate, name, after=(), grid=(), scalars=0, scratch=(), reuse=False):
    n_in, n_after = len(args), len(after)

    def wrapped(*refs):
        return body(*refs[:n_in], *refs[n_in + n_after :])

    return pl.pallas_call(
        wrapped,
        grid_spec=pltpu.PrefetchScalarGridSpec(
            num_scalar_prefetch=scalars,
            grid=grid,
            in_specs=list(in_specs) + [ANY] * n_after,
            out_specs=out_specs,
            scratch_shapes=list(scratch),
        ),
        out_shape=outs,
        input_output_aliases={n_in + k: k for k in range(n_after)} if reuse else {},
        compiler_params=pltpu.CompilerParams(vmem_limit_bytes=VMEM_LIMIT),
        cost_estimate=estimate,
        name=name,
    )(*args, *after)


def crop_rows(core, count, crops, after=()):
    def body(at, n, src, mine, other, s):
        wide = src[...].astype(F32).reshape(ROWS, D)
        for g in range(NG):
            s[g] = wide[:, LANE * g : LANE * (g + 1)]
        for k in range(HALF):
            for out, c in ((mine, at[0]), (other, 1 - at[0])):
                crop = HALF * c + k
                keep = jnp.where(crop < n[0], 1.0, 0.0).astype(F32)
                for g in range(NG):
                    out[g, rows_of(k, stride=HALF), :] = s[g, rows_of(crop), :] * keep

    return call(
        body, (core, count, crops), [SM, SM, VM], [shape((NG, PIECE, LANE), F32)] * 2, [VM] * 2, cost(2.5), "crop_rows", after, scratch=[pltpu.VMEM((NG, ROWS, LANE), F32)],
    )


def weave(dest, pieces):
    for b, piece in enumerate(pieces):
        for k in range(HALF):
            for g in range(NG):
                dest[g, rows_of(HALF * b + k), :] = piece[g, rows_of(k, stride=HALF), :]


def join_pieces(x_at, pieces, after=()):
    def body(x, *refs):
        *src, out, s = refs
        for k in range(2):
            weave(s, src[2 * k : 2 * k + 2])
            for g in range(NG):
                out[x[0] ^ k, :, :, LANE * g : LANE * (g + 1)] = s[g].reshape(T, C, LANE)

    return call(
        body, (x_at, *pieces), [SM] + [VM] * 4, shape((2, T, C, D), F32), VM, cost(4), "join_pieces", after,
        scratch=[pltpu.VMEM((NG, ROWS, LANE), F32)],
    )


def own_quadrants(x_at, both_halves, rolled, after=()):
    def body(x, src, mine, other, full, s):
        if rolled:
            put_rolled(full, src, x[0], True)
        else:
            full[...] = src[x[0]].reshape(ROWS, D)
        for g in range(NG):
            s[g] = full[:, LANE * g : LANE * (g + 1)]
        for b, out in enumerate((mine, other)):
            for k in range(HALF):
                for g in range(NG):
                    out[g, rows_of(k, stride=HALF), :] = s[g, rows_of(HALF * b + k), :]

    return call(
        body, (x_at, both_halves), [SM, VM], [shape((NG, PIECE, LANE), F32)] * 2, [VM] * 2, cost(3), "own_quadrants", after, scratch=[pltpu.VMEM((ROWS, D), F32), pltpu.VMEM((NG, ROWS, LANE), F32)],
    )


def token_major(core, count, mine, theirs, after=()):
    def body(at, n, a, b, out, s):
        for k in range(HALF):
            for src, c in ((a, at[0]), (b, 1 - at[0])):
                crop = HALF * c + k
                keep = jnp.where(crop < n[0], 1.0, 0.0).astype(F32)
                for g in range(NG):
                    s[g, rows_of(crop), :] = src[g, rows_of(k, stride=HALF), :] * keep
        for g in range(NG):
            out[:, :, LANE * g : LANE * (g + 1)] = s[g].reshape(T, C, LANE).astype(BF16)

    return call(
        body, (core, count, mine, theirs), [SM, SM, VM, VM], shape((T, C, D), BF16), VM, cost(2.5), "token_major", after, scratch=[pltpu.VMEM((NG, ROWS, LANE), F32)],
    )


def crop_major(core, mine, theirs, after=()):
    def body(at, a, b, out):
        for k in range(HALF):
            for src, c in ((a, at[0]), (b, 1 - at[0])):
                for g in range(NG):
                    out[pl.ds((HALF * c + k) * (T * NG) + g, T, stride=NG), :] = src[g, rows_of(k, stride=HALF), :]

    return call(
        body, (core, mine, theirs), [SM, VM, VM], shape((C * T * NG, LANE), F32), VM, cost(2.5), "crop_major", after,
    )


def fwd_body(b, *refs):
    a = pl.program_id(0)
    if b == 0:
        _, p0, p1, *rest = refs
    else:
        src, mask, *rest = refs
    (
        bias, ln1g, ln1b, bq, bv, bout, ln2g, ln2b, bup, bdown,
        wqkv_h, wout_h, wup_h, wdown_h,
        z_o, h_o, qkvc_o, o_o, y_o, h2_o, g_o, gp_o, zn_o,
        wqkv, wout, wup, wdown, qkv_s, o_s, bqkv, acc, bias_s, sem_q, sem_o, sem_u, sem_d,
    ) = rest

    def cp_q(n):
        return pltpu.make_async_copy(
            wqkv_h.at[b, :, lanes_at(n, QCH)], wqkv.at[:, lanes_at(n, QCH)], sem_q.at[n]
        )

    def cp_u(n):
        return pltpu.make_async_copy(
            wup_h.at[b, :, lanes_at(n, FCH)], wup.at[:, lanes_at(n, FCH)], sem_u.at[n]
        )

    def cp_d(n):
        return pltpu.make_async_copy(
            wdown_h.at[b, lanes_at(n, FCH), :], wdown.at[lanes_at(n, FCH), :], sem_d.at[n]
        )

    cp_o = pltpu.make_async_copy(wout_h.at[b], wout, sem_o)

    def wait(copy):
        @pl.when(a == 0)
        def _():
            copy.wait()

    @pl.when(a == 0)
    def _():
        for n in range(N_Q):
            cp_q(n).start()
        cp_o.start()
        for n in range(N_F):
            cp_u(n).start()
            cp_d(n).start()
        bqkv[:, 0:D] = bq[b : b + 1, :]
        bqkv[:, D : 2 * D] = jnp.zeros((1, D), F32)
        bqkv[:, 2 * D :] = bv[b : b + 1, :]
        qkv_s[:, ROWS:, :] = jnp.zeros((3 * NG, PAD_ROWS - ROWS, LANE), F32)

    if b == 0:
        weave(o_s, (p0, p1))
        for g in range(NG):
            z_o[0, :, LANE * g : LANE * (g + 1)] = o_s[g, 0:ROWS, :]
    else:
        put_rolled(z_o.at[0], src, a, False)
        for w in range(2):
            for g in range(NG):
                bias_s[w * NG + g] = bias[NG + g] + mask[0, w]
    normed, _ = norm_parts(z_o[0])
    h_o[0] = (normed * ln1g[b : b + 1, :] + ln1b[b : b + 1, :]).astype(BF16)

    def qkv_step(n, _):
        wait(cp_q(n))
        joint = nn(h_o[0], wqkv[:, lanes_at(n, QCH)]) + bqkv[:, lanes_at(n, QCH)]
        joint = joint * jnp.where(n < D // QCH, SCALE, 1.0)
        joint = joint.astype(BF16).astype(F32)
        for k in range(QCH // LANE):
            qkv_s[n * (QCH // LANE) + k, 0:ROWS, :] = joint[:, LANE * k : LANE * (k + 1)]
        return 0

    lax.fori_loop(0, N_Q, qkv_step, 0)
    masks = head_masks(TP)
    ones = [m.astype(F32).astype(BF16) for m in head_masks(TQ)]

    def attend(w, _):
        for g in range(NG):
            q = qkv_s[g, rows_of(w, TQ), :].astype(BF16)
            k = qkv_s[NG + g, rows_of(w, TP), :].astype(BF16)
            v = qkv_s[2 * NG + g, rows_of(w, TP), :].astype(BF16)
            qkvc_o[0, w, g] = q
            qkvc_o[0, w, NG + g, 0:TP] = k
            qkvc_o[0, w, 2 * NG + g, 0:TP] = v
            added = bias[g] if b == 0 else bias_s[w // HALF * NG + g]
            probs = soft(nt(k, spread(q, ones)) + added)
            o_s[g, rows_of(w, TP), :] = gather_heads(tn(probs.astype(BF16), v), masks)
        return 0

    lax.fori_loop(0, C, attend, 0, unroll=2)
    for g in range(NG):
        o_o[0, :, LANE * g : LANE * (g + 1)] = o_s[g, 0:ROWS, :].astype(BF16)
    wait(cp_o)
    y_o[0] = z_o[0] + (nn(o_o[0], wout[...]) + bout[b : b + 1, :])
    normed, _ = norm_parts(y_o[0])
    h2_o[0] = (normed * ln2g[b : b + 1, :] + ln2b[b : b + 1, :]).astype(BF16)
    acc[...] = jnp.zeros_like(acc)

    def mlp_step(n, _):
        wait(cp_u(n))
        up = nn(h2_o[0], wup[:, lanes_at(n, FCH)]) + bup[b : b + 1, lanes_at(n, FCH)]
        act, slope = gelu_parts(up)
        act = act.astype(BF16)
        g_o[0, :, lanes_at(n, FCH)] = act
        gp_o[0, :, lanes_at(n, FCH)] = slope.astype(BF16)
        wait(cp_d(n))
        acc[...] += nn(act, wdown[lanes_at(n, FCH), :])
        return 0

    lax.fori_loop(0, N_F, mlp_step, 0)
    zn_o[0] = (y_o[0] + (acc[...] + bdown[b : b + 1, :])).reshape(T, C, D)


def block_fwd(b, sources, bias, p, which=None, after=()):
    outs = [
        shape((2, ROWS, D), F32),
        shape((2, ROWS, D), BF16),
        shape((2, C, 3 * NG, TQ, LANE), BF16),
        shape((2, ROWS, D), BF16),
        shape((2, ROWS, D), F32),
        shape((2, ROWS, D), BF16),
        shape((2, ROWS, FF), BF16),
        shape((2, ROWS, FF), BF16),
        shape((2, T, C, D), F32),
    ]
    if b == 0:
        specs = [fixed((NG, PIECE, LANE), True)] * 2
        out_specs = [
            pl.BlockSpec((1, *o.shape[1:]), lambda a, s, n=len(o.shape) - 1: (s[0] ^ which, *(0,) * n)) for o in outs
        ]
    else:
        specs = [fixed((2, T, C, D), True), per_half((2, TP, GT))]
        out_specs = [per_half(o.shape[1:]) for o in outs]
    small = (bias, p["ln1_gain"], p["ln1_bias"], p["b_query"], p["b_value"], p["b_out"],
             p["ln2_gain"], p["ln2_bias"], p["b_up"], p["b_down"])
    big = (p["w_qkv"], p["w_out"], p["w_up"], p["w_down"])
    return call(
        functools.partial(fwd_body, b),
        (*sources, *small, *big),
        specs + [fixed(v.shape, True) for v in small] + [ANY] * 4,
        outs,
        out_specs,
        cost(25 if which is not None else 46),
        f"forward_{b}",
        after,
        grid=(2 if which is None else 1,),
        scalars=int(which is not None),
        reuse=which == 1,
        scratch=[
            pltpu.VMEM((D, 3 * D), BF16),
            pltpu.VMEM((D, D), BF16),
            pltpu.VMEM((D, FF), BF16),
            pltpu.VMEM((FF, D), BF16),
            pltpu.VMEM((3 * NG, PAD_ROWS, LANE), F32),
            pltpu.VMEM((NG, PAD_ROWS, LANE), F32),
            pltpu.VMEM((1, 3 * D), F32),
            pltpu.VMEM((ROWS, D), F32),
            pltpu.VMEM((2 * NG, TP, GT), F32),
            pltpu.SemaphoreType.DMA((N_Q,)),
            pltpu.SemaphoreType.DMA,
            pltpu.SemaphoreType.DMA((N_F,)),
            pltpu.SemaphoreType.DMA((N_F,)),
        ],
    )


def mlp_back_body(b, x_at, src, y, gp, ln2g, wdown_h, wup_h, dd_o, da_o, dy_o, dyr_o, sv_o,
                  wdown, wup, acc, dz, dd, sem_d, sem_u):
    a = pl.program_id(0)

    def cp_u(n):
        return pltpu.make_async_copy(
            wup_h.at[b, :, lanes_at(n, D)], wup.at[:, lanes_at(n, D)], sem_u.at[n]
        )

    def cp_d(n):
        return pltpu.make_async_copy(
            wdown_h.at[b, lanes_at(n, D), :], wdown.at[lanes_at(n, D), :], sem_d.at[n]
        )

    def wait(copy):
        @pl.when(a == 0)
        def _():
            copy.wait()

    @pl.when(a == 0)
    def _():
        for n in range(4):
            cp_d(n).start()
            cp_u(n).start()
        sv_o[...] = jnp.zeros_like(sv_o)

    put_rolled(dz, src, a, b == 0)
    low = dz[...].astype(BF16)
    dd[...] = low
    sv_o[3:4, :] += colsum(low.astype(F32))
    for x in range(2):

        @pl.when(x_at[0] == x)
        def _():
            for c in range(2):
                w = 2 * x + c
                dd_o[c, 0] = dd[:, MINE * w : MINE * (w + 1)]

    acc[...] = jnp.zeros_like(acc)

    def step(n, _):
        wait(cp_d(n))
        grad_act = nt(dd[...], wdown[lanes_at(n, D), :])
        da = (grad_act * gp[0, :, lanes_at(n, D)].astype(F32)).astype(BF16)

        @pl.when(n // 2 == x_at[0])
        def _():
            da_o[0, :, lanes_at(n % 2, D)] = da

        sv_o[pl.ds(4 + n, 1), :] += colsum(da.astype(F32))
        wait(cp_u(n))
        acc[...] += nt(da, wup[:, lanes_at(n, D)])
        return 0

    lax.fori_loop(0, 4, step, 0)
    dh2 = acc[...]
    normed, inverse = norm_parts(y[0])
    sv_o[0:1, :] += colsum(dh2 * normed)
    sv_o[1:2, :] += colsum(dh2)
    dy = dz[...] + norm_back(dh2, normed, inverse, ln2g[b : b + 1, :])
    dy_o[0] = dy
    low = dy.astype(BF16)
    dyr_o[0] = low
    sv_o[2:3, :] += colsum(low.astype(F32))


def mlp_back(b, x_at, src, y, gp, p, after=()):
    return call(
        functools.partial(mlp_back_body, b),
        (x_at, src, y, gp, p["ln2_gain"], p["w_down"], p["w_up"]),
        [SM, fixed((2, T, C, D), True), per_half((ROWS, D)), per_half((ROWS, FF)), fixed((2, D)), ANY, ANY],
        [
            shape((2, 2, ROWS, MINE), BF16),
            shape((2, ROWS, FF // 2), BF16),
            shape((2, ROWS, D), F32),
            shape((2, ROWS, D), BF16),
            shape((8, D), F32),
        ],
        [
            pl.BlockSpec((2, 1, ROWS, MINE), lambda a: (0, a, 0, 0)),
            per_half((ROWS, FF // 2)),
            per_half((ROWS, D)),
            per_half((ROWS, D)),
            fixed((8, D)),
        ],
        cost(23),
        f"mlp_back_{b}",
        after,
        grid=(2,),
        scratch=[
            pltpu.VMEM((FF, D), BF16),
            pltpu.VMEM((D, FF), BF16),
            pltpu.VMEM((ROWS, D), F32),
            pltpu.VMEM((ROWS, D), F32),
            pltpu.VMEM((ROWS, D), BF16),
            pltpu.SemaphoreType.DMA((4,)),
            pltpu.SemaphoreType.DMA((4,)),
        ],
    )


TABLE = 256
BLOCK = (D // 8, D)


def table_sums(ds, moved):
    row = lax.broadcasted_iota(jnp.int32, (GT, PER * LANE), 0)
    col = lax.broadcasted_iota(jnp.int32, (GT, PER * LANE), 1)
    t = row & (TQ - 1)
    i = sum((t >= SIDE * k).astype(jnp.int32) for k in range(1, SIDE))
    there = (row >> 6 == col >> 7) & (t < T) & ((col & (LANE - 1)) == t + 6 * i)
    onehot = there.astype(F32).astype(BF16)
    moved[:, NG * TP :, :] = jnp.zeros((PER, (8 - NG) * TP, LANE), F32)
    for g in range(NG):
        rest = ds[g]
        total = jnp.zeros((TP, PER * LANE), F32)
        for _ in range(3):
            part = rest.astype(BF16)
            total += nn(part, onehot)
            rest = rest - part.astype(F32)
        for h in range(PER):
            moved[h, TP * g : TP * (g + 1), :] = total[:, LANE * h : LANE * (h + 1)]


def sum_table(moved, put):
    for h in range(PER):
        total = jnp.zeros((8, TABLE), F32)
        for u in range(T):
            v = moved[h, pl.ds(u, 8, stride=TP), :]
            shift = 13 * (6 - u // SIDE) + 6 - u % SIDE
            total += pltpu.roll(jnp.concatenate([v, jnp.zeros_like(v)], axis=1), shift, 1)
        put(h, total)


def attn_back_body(b, x_at, dyr, qkvc, dy, z, *refs):
    if b == 1:
        mask, *refs = refs
    bias, ln1g, *refs = refs
    if b == 0:
        sv_m0, sv_a1, sv_m1, table1, *refs = refs
    (wout_h, wqkv_h, r3_o, sv_o, sum_o, grad_o,
     wout, wqkv, do_s, dqkv_s, dq, acc, bias_s, ds_o, moved, sem_o, sem_q) = refs
    a = pl.program_id(0)
    cp_o = pltpu.make_async_copy(wout_h.at[b], wout, sem_o)

    def cp_q(n):
        return pltpu.make_async_copy(
            wqkv_h.at[b, :, lanes_at(n, QCH)], wqkv.at[:, lanes_at(n, QCH)], sem_q.at[n]
        )

    def wait(copy):
        @pl.when(a == 0)
        def _():
            copy.wait()

    @pl.when(a == 0)
    def _():
        cp_o.start()
        for n in range(N_Q):
            cp_q(n).start()
        do_s[:, ROWS:, :] = jnp.zeros((NG, PAD_ROWS - ROWS, LANE), F32)
        ds_o[...] = jnp.zeros_like(ds_o)
        sv_o[...] = jnp.zeros_like(sv_o)

    if b == 1:
        for w in range(2):
            for g in range(NG):
                bias_s[w * NG + g] = bias[NG + g] + mask[0, w]
    wait(cp_o)
    do = nt(dyr[0], wout[...]).astype(BF16).astype(F32)
    for g in range(NG):
        do_s[g, 0:ROWS, :] = do[:, LANE * g : LANE * (g + 1)]
    masks = head_masks(TP)
    ones = [m.astype(F32).astype(BF16) for m in head_masks(TQ)]

    def attend(w, _):
        for g in range(NG):
            q = qkvc[0, w, g]
            k = qkvc[0, w, NG + g, 0:TP]
            v = qkvc[0, w, 2 * NG + g, 0:TP]
            q_wide = spread(q, ones)
            do_wide = spread(do_s[g, rows_of(w, TQ), :].astype(BF16), ones)
            added = bias[g] if b == 0 else bias_s[w // HALF * NG + g]
            probs = soft(nt(k, q_wide) + added)
            weighted = probs * nt(v, do_wide)
            ds = weighted - probs * jnp.sum(weighted, axis=0, keepdims=True)
            ds_o[g] += ds
            low = ds.astype(BF16)
            dqkv_s[g, rows_of(w, TP), :] = gather_heads(tn(low, k), masks) * SCALE
            dqkv_s[NG + g, rows_of(w, TP), :] = nn(low, q_wide)
            dqkv_s[2 * NG + g, rows_of(w, TP), :] = nn(probs.astype(BF16), do_wide)
        return 0

    lax.fori_loop(0, C, attend, 0, unroll=2)
    for g in range(3 * NG):
        dq[:, LANE * g : LANE * (g + 1)] = dqkv_s[g, 0:ROWS, :].astype(BF16)
    sv_o[2:3, :] += colsum(dq[:, 0:D].astype(F32))
    sv_o[3:4, :] += colsum(dq[:, 2 * D :].astype(F32))
    acc[...] = jnp.zeros_like(acc)

    def step(n, _):
        wait(cp_q(n))
        acc[...] += nt(dq[:, lanes_at(n, QCH)], wqkv[:, lanes_at(n, QCH)])
        return 0

    lax.fori_loop(0, N_Q, step, 0)
    for x in range(2):

        @pl.when(x_at[0] == x)
        def _():
            for c in range(2):
                w = 2 * x + c
                r3_o[c, 0] = jnp.concatenate(
                    [dq[:, 3 * MINE * w : 3 * MINE * (w + 1)], dyr[0, :, MINE * w : MINE * (w + 1)]], axis=1
                )

    dh = acc[...]
    normed, inverse = norm_parts(z[0])
    sv_o[0:1, :] += colsum(dh * normed)
    sv_o[1:2, :] += colsum(dh)
    grad_o[0] = (dy[0] + norm_back(dh, normed, inverse, ln1g[b : b + 1, :])).reshape(T, C, D)

    @pl.when(a == 1)
    def _():
        table_sums(ds_o, moved)
        if b == 1:
            sum_table(moved, lambda h, v: sum_o.__setitem__(h, v))
            return
        sum_o[...] = jnp.zeros_like(sum_o)
        for at, ref in ((0, sv_o), (4, sv_m0), (12, sv_a1), (16, sv_m1)):
            sum_o[at : at + ref.shape[0], :] = ref[...]
        for h in range(PER):
            sum_o[24 + 8 * h : 32 + 8 * h, TABLE : 2 * TABLE] = table1[h]
        sum_table(moved, lambda h, v: sum_o.__setitem__((slice(24 + 8 * h, 32 + 8 * h), slice(0, TABLE)), v))


def attn_back(b, x_at, dyr, qkvc, dy, z, mask, bias, p, sums=(), after=()):
    masks = [mask] if b else []
    sum_shape = (PER, 8, TABLE) if b else BLOCK
    return call(
        functools.partial(attn_back_body, b),
        (x_at, dyr, qkvc, dy, z, *masks, bias, p["ln1_gain"], *sums, p["w_out"], p["w_qkv"]),
        [SM, per_half((ROWS, D)), per_half((C, 3 * NG, TQ, LANE)), per_half((ROWS, D)), per_half((ROWS, D))]
        + [per_half((2, TP, GT))] * b
        + [fixed(bias.shape, True), fixed((2, D)), *(fixed(v.shape) for v in sums), ANY, ANY],
        [shape((2, 2, ROWS, D), BF16), shape((4, D), F32), shape(sum_shape, F32), shape((2, T, C, D), F32)],
        [
            pl.BlockSpec((2, 1, ROWS, D), lambda a: (0, a, 0, 0)),
            fixed((4, D)),
            fixed(sum_shape),
            per_half((T, C, D)),
        ],
        cost(48),
        f"attn_back_{b}",
        after,
        grid=(2,),
        scratch=[
            pltpu.VMEM((D, D), BF16),
            pltpu.VMEM((D, 3 * D), BF16),
            pltpu.VMEM((NG, PAD_ROWS, LANE), F32),
            pltpu.VMEM((3 * NG, PAD_ROWS, LANE), F32),
            pltpu.VMEM((ROWS, 3 * D), BF16),
            pltpu.VMEM((ROWS, D), F32),
            pltpu.VMEM((2 * NG, TP, GT), F32),
            pltpu.VMEM((NG, TP, GT), F32),
            pltpu.VMEM((PER, 8 * TP, LANE), F32),
            pltpu.SemaphoreType.DMA,
            pltpu.SemaphoreType.DMA((N_Q,)),
        ],
    )


def halves(left, right):
    return tn(left(0), right(0)) + tn(left(1), right(1))


def insert_bit(i, place, bit):
    return ((i >> place) << (place + 1)) | (bit << place) | (i & ((1 << place) - 1))


def row_pairs(values, k):
    height = values.shape[0] // 8
    for i in range(4):
        low = insert_bit(i, k, 0)
        high = low | (1 << k)
        yield i, low, high, values[height * low : height * (low + 1)], values[height * high : height * (high + 1)]


def put_down(out, i, total):
    half = MINE // 2
    out[i, :, 0:W_UP] = total[0:half]
    out[i, :, W_UP:] = total[half:]


def get_down(block):
    return jnp.concatenate([block[:, 0:W_UP], block[:, W_UP:]], axis=0)


def mlp_other(bits, dd, act, hid, da, after=()):
    def down(s, l, r, out):
        for k in range(2):
            lanes = slice(k * W_UP, (k + 1) * W_UP)
            put_down(out, k, halves(lambda a: l[0, a], lambda a: r[a, :, lanes]))

    out = shape((16, *BLOCK), F32)
    first = call(
        down, (bits, dd, act),
        [pl.BlockSpec((1, 2, ROWS, MINE), lambda i, s: (1 - s[0], 0, 0, 0)),
         pl.BlockSpec((2, ROWS, D), lambda i, s: (0, 0, i))],
        out, pl.BlockSpec((2, *BLOCK), lambda i, s: (i, 0, 0)),
        cost(6.5), "down_other", after, (4,), 1,
    )

    def up(s, l, r, out):
        out[...] = halves(lambda a: l[a], lambda a: r[a]).reshape(8, D // 8, W_UP)

    return call(
        up, (bits, hid, da),
        [fixed((2, ROWS, D)), pl.BlockSpec((2, ROWS, W_UP), lambda n, s: (0, 0, 2 * (1 - s[0]) + n))],
        [out], [pl.BlockSpec((8, D // 8, W_UP), lambda n, s: (1, 0, n))],
        cost(5.4), "up_other", (first,), (2,), 1, reuse=True,
    )[0]


def mlp_mine(bits, dd, act, hid, da, recv, first, after=()):
    def down(s, l, rk, rs, gk, gs, keep, send):
        put_down(keep, 0, halves(lambda a: l[0, a], lambda a: rk[a]) + get_down(gk[0]))
        put_down(send, 0, halves(lambda a: l[0, a], lambda a: rs[a]) + get_down(gs[0]))

    def block(flip):
        return lambda i, s: insert_bit(i, first, s[1 + first] ^ flip)

    outs = [shape((8, *BLOCK), F32)] * 2
    half = call(
        down, (bits, dd, act, act, recv, recv),
        [pl.BlockSpec((1, 2, ROWS, MINE), lambda i, s: (s[0], 0, 0, 0))]
        + [pl.BlockSpec((2, ROWS, W_UP), lambda i, s, m=block(f): (0, 0, m(i, s))) for f in (0, 1)]
        + [pl.BlockSpec((1, *BLOCK), lambda i, s, m=block(f): (m(i, s), 0, 0)) for f in (0, 1)],
        outs, [pl.BlockSpec((1, *BLOCK), lambda i, s: (i, 0, 0))] * 2,
        cost(6.9), "down_mine", after, (4,), 1,
    )

    def up(s, l, r, got, keep, send):
        total = halves(lambda a: l[a], lambda a: r[a])
        mine = s[1 + first] == 0
        for i, j, k, p, q in row_pairs(total, first):
            p, q = p + got[j], q + got[k]
            keep[i] = jnp.where(mine, p, q)
            send[i] = jnp.where(mine, q, p)

    return call(
        up, (bits, hid, da, recv),
        [fixed((2, ROWS, D)), pl.BlockSpec((2, ROWS, W_UP), lambda n, s: (0, 0, 2 * s[0] + n)),
         pl.BlockSpec((8, D // 8, W_UP), lambda n, s: (1, 0, n))],
        outs, [pl.BlockSpec((4, D // 8, W_UP), lambda n, s: (1, 0, n))] * 2,
        cost(5.7), "up_mine", half, (2,), 1, reuse=True,
    )


def attn_total(hid, att, r, lo, width):
    edge = 3 * MINE
    cut = edge // LANE * LANE

    def product(left, a, b):
        return halves(lambda k: left[k], lambda k: r[k, :, a - lo : b - lo])

    parts = []
    if lo < cut:
        parts.append(product(hid, lo, min(cut, lo + width)))
    if lo + width > cut:
        lane = lax.broadcasted_iota(jnp.int32, (D, LANE), 1)
        span = (cut, cut + LANE)
        parts.append(jnp.where(lane < edge - cut, product(hid, *span), product(att, *span)))
    if lo + width > cut + LANE:
        parts.append(product(att, cut + LANE, lo + width))
    return parts[0] if len(parts) == 1 else jnp.concatenate(parts, axis=1)


def attn_other(bits, hid, att, r3, after=()):
    def body(s, h, o, r, *outs):
        for n in range(2):

            @pl.when(pl.program_id(0) == n)
            def _():
                total = attn_total(h, o, r.at[0], n * W_UP, W_UP).reshape(8, D // 8, W_UP)
                outs[2 * n][...] = total[0:4]
                outs[2 * n + 1][...] = total[4:8]

    right = pl.BlockSpec((1, 2, ROWS, W_UP), lambda n, s: (1 - s[0], 0, 0, n))
    return call(
        body, (bits, hid, att, r3), [fixed((2, ROWS, D)), fixed((2, ROWS, D)), right],
        [shape((4, D // 8, W_UP), F32)] * 4, [fixed((4, D // 8, W_UP))] * 4,
        cost(7), "attn_other", after, (2,), 1,
    )


def attn_mine(bits, hid, att, r3, recv, first, cols, small=None, after=()):
    extra = small is not None
    width = W_UP * len(cols)

    def body(s, h, o, r, *refs):
        gots, more, (keep, send) = refs[: 2 * len(cols)], refs[2 * len(cols) : -2], refs[-2:]
        for k, n in enumerate(cols):

            @pl.when(pl.program_id(0) == k)
            def _():
                total = attn_total(h, o, r.at[0], n * W_UP, W_UP)
                mine = s[1 + first] == 0
                for i, j, jj, p, q in row_pairs(total, first):
                    p, q = p + gots[2 * k + j // 4][j % 4], q + gots[2 * k + jj // 4][jj % 4]
                    keep[i] = jnp.where(mine, p, q)
                    send[i] = jnp.where(mine, q, p)
                if extra:
                    added = more[0][...] + more[1][...]
                    keep[4] = added
                    send[4] = added

    at = lambda n: n + cols[0]
    specs = [
        fixed((2, ROWS, D)),
        fixed((2, ROWS, D)),
        pl.BlockSpec((1, 2, ROWS, W_UP), lambda n, s: (s[0], 0, 0, at(n))),
    ]
    args = [bits, hid, att, r3]
    for n in cols:
        args += recv[2 * n : 2 * n + 2]
        specs += [fixed((4, D // 8, W_UP))] * 2
    if extra:
        args += small
        specs += [pl.BlockSpec((D // 8, W_UP), lambda n, s: (0, at(n)))] * 2
    out = pl.BlockSpec((4 + extra, D // 8, W_UP), lambda n, s: (0, 0, n))
    return call(
        body, args, specs, [shape((4 + extra, D // 8, width), F32)] * 2, [out] * 2,
        cost(1.5 + 2.8 * len(cols)), "attn_mine", after, (len(cols),), 1,
    )


def split_sum(kept, recv, place, bit, extra, after=()):
    n, r, w = recv.shape
    half = (n - extra) // 2

    def body(s, ka, ra, kb, rb, keep_o, send_o):
        keep_o[...] = ka[...] + ra[...]
        send_o[...] = kb[...] + rb[...]

    def at(flip):
        def index(i, s):
            j = insert_bit(i, place, s[0] ^ flip)
            return (jnp.where(i == half, 2 * half, j) if extra else j, 0, 0)

        return pl.BlockSpec((1, r, w), index)

    return call(
        body, (jnp.reshape(bit, (1,)), kept, recv, kept, recv), [at(0), at(0), at(1), at(1)],
        [shape((half + extra, r, w), F32)] * 2, [pl.BlockSpec((1, r, w), lambda i, s: (i, 0, 0))] * 2,
        cost(1.5 + n * r * w * 5e-6), "split_sum", after, (half + extra,), 1,
    )


class Halving:
    def __init__(self, names, links, extra=0):
        self.names, self.links, self.extra = list(names), links, extra

    def send(self, name, kept, out):
        axis, perm, _ = self.links[name]
        if name in self.names:
            self.names.remove(name)
        self.kept, self.recv = kept, lax.ppermute(out, axis, perm)
        return kept

    def step(self, name, after=()):
        place = len(self.names) - 1 - self.names.index(name)
        kept, out = split_sum(self.kept, self.recv, place, self.links[name][2], self.extra, after)
        return self.send(name, kept, out)

    def result(self):
        return self.kept + self.recv


def scatter_rest(block, dim, img, sub):
    step = sub // 2
    while step:
        bit = (img // step) % 2
        half = block.shape[dim] // 2
        keep = lax.dynamic_slice_in_dim(block, bit * half, half, dim)
        send = lax.dynamic_slice_in_dim(block, (1 - bit) * half, half, dim)
        perm = [(i, i ^ step) for i in range(8 * sub)]
        block = keep + lax.ppermute(send, "img", perm)
        step //= 2
    return block


def relative_onehot():
    at = jnp.arange(TP * TQ, dtype=jnp.int32)
    u, t = at // TQ, at % TQ
    rel = (t // SIDE - u // SIDE + 6) * 13 + t % SIDE - u % SIDE + 6
    rel = jnp.where((u < T) & (t < T), rel, -1)
    return (jnp.arange(169, dtype=jnp.int32)[:, None] == rel[None, :]).astype(F32)


def region_of(coords):
    return jnp.where(coords < 7, 0, jnp.where(coords < 11, 1, 2))


def spread_bias(bias_table, onehot):
    rows = jnp.dot(
        bias_table.transpose(0, 2, 1).reshape(2 * HEADS, 169),
        onehot,
        precision=lax.Precision.HIGHEST,
        preferred_element_type=F32,
    )
    rows = rows.reshape(2, NG, PER, TP, TQ).transpose(0, 1, 3, 2, 4).reshape(2 * NG, TP, GT)
    return jnp.where((jnp.arange(TP) < T)[None, :, None], rows, NEG)


def shift_masks(core):
    places = jnp.arange(TQ, dtype=jnp.int32)
    step = jnp.arange(2, dtype=jnp.int32)
    rows = region_of(step[:, None] * SIDE + places // SIDE)
    cols = region_of((core ^ step)[:, None] * SIDE + places % SIDE)
    labels = 3 * rows[:, None] + cols[None, :]
    mask = jnp.where(labels[:, :, :TP, None] == labels[:, :, None, :], 0.0, -100.0).astype(F32)
    return jnp.tile(mask, (1, 1, 1, PER))


def per_device(
    tokens, crop_count, ln1_gain, ln1_bias, w_qkv, b_query, b_value, bias_table, w_out, b_out,
    ln2_gain, ln2_bias, w_up, b_up, w_down, b_down, cotangent, *, n_img,
):
    win, img = lax.axis_index("win"), lax.axis_index("img")
    sub = n_img // 8
    x_bit, core = win // 2, win % 2
    links = {}
    for k in range(3):
        links[k] = ("img", [(i, i ^ (sub << k)) for i in range(n_img)], (img // (sub << k)) % 2)
    bits = jnp.stack([core, links[0][2], links[1][2], links[2][2]])
    at_core, at_x = jnp.reshape(core, (1,)), jnp.reshape(x_bit, (1,))
    all_valid = jnp.full((1,), C, jnp.int32)
    p = dict(
        ln1_gain=ln1_gain, ln1_bias=ln1_bias, w_qkv=w_qkv, b_query=b_query, b_value=b_value,
        w_out=w_out, b_out=b_out, ln2_gain=ln2_gain, ln2_bias=ln2_bias, w_up=w_up, b_up=b_up,
        w_down=w_down, b_down=b_down,
    )

    def over(way, a):
        return lax.ppermute(a, "win", [(i, i ^ way) for i in range(4)])

    def swap(a):
        return over(1, a)

    onehot = relative_onehot()
    bias = spread_bias(bias_table, onehot)
    mask = shift_masks(core)

    mine, other = crop_rows(at_core, all_valid, tokens[:, 0].transpose(1, 0, 2))
    near, far = swap(other), (over(2, mine), over(3, other))
    ct_mine, ct_other = crop_rows(at_core, crop_count, cotangent[:, 0].transpose(1, 0, 2), (mine,))
    ct_near, ct_far = swap(ct_other), (over(2, ct_mine), over(3, ct_other))
    fwd0 = block_fwd(0, (at_x, mine, near), bias, p, 0, (ct_mine,))
    fwd0 = block_fwd(0, (at_x, *far), bias, p, 1, fwd0)
    fwd1 = block_fwd(1, (fwd0[8], mask), bias, p)
    z0, h0, qkvc0, o0, y0, h20, g0, gp0, _ = fwd0
    z1, h1, qkvc1, o1, y1, h21, g1, gp1, zn = fwd1
    ct = join_pieces(at_x, (ct_mine, ct_near, *ct_far), (zn,))

    def stream(first, extra=0, more=()):
        return Halving([*more, *(k for k in (2, 1, 0) if k != first)], links, extra)

    mlp1, mlp0 = (stream(0, 0, ("which",)) for _ in range(2))
    att1, att0 = stream(0), [stream(0, 1), stream(1, 1)]

    dd1, da1, dy, dyr, sv_m1 = mlp_back(1, at_x, ct, y1, gp1, p)
    part = mlp_other(bits, dd1, g1, h21, da1)
    mlp_x = swap(part)
    r31, sv_a1, table1, grad1 = attn_back(1, at_x, dyr, qkvc1, dy, z1, mask, bias, p, (), (part,))
    last = mlp1.send(0, *mlp_mine(bits, dd1, g1, h21, da1, mlp_x, 0, (sv_a1,)))
    part = attn_other(bits, h1, o1, r31, (last,))
    att_x = [swap(a) for a in part]

    dd0, da0, dy, dyr, sv_m0 = mlp_back(0, at_x, grad1, y0, gp0, p, (part[3],))
    last = att1.send(0, *attn_mine(bits, h1, o1, r31, att_x, 0, (0, 1), None, (sv_m0,)))
    out_mine, out_other = own_quadrants(at_x, zn, True, (last,))
    last = mlp1.step(1, (out_mine,))
    part = mlp_other(bits, dd0, g0, h20, da0, (last,))
    mlp_x = swap(part)
    out_x = swap(out_other)
    block_out = token_major(at_core, crop_count, out_mine, out_x, (part,))
    last = mlp0.send(0, *mlp_mine(bits, dd0, g0, h20, da0, mlp_x, 0, (block_out,)))
    last = att1.step(1, (last,))
    last = mlp1.step(2, (last,))
    r30, sv_a0, small, grad0 = attn_back(
        0, at_x, dyr, qkvc0, dy, z0, mask, bias, p, (sv_m0, sv_a1, sv_m1, table1), (last,)
    )
    part = attn_other(bits, h0, o0, r30)
    att_x = [swap(a) for a in part]
    small = [small, swap(small)]
    last = mlp0.step(1, (part[3],))
    for k in range(2):
        kept, out = attn_mine(bits, h0, o0, r30, att_x, k, (k,), small, (last,))
        last = att0[k].send(k, kept, out)
    last = att1.step(2, (last,))
    in_mine, in_other = own_quadrants(at_x, grad0, False, (last,))
    in_x = swap(in_other)
    last = in_mine
    for s, name in ((mlp0, 2), (att0[0], 1), (att0[1], 0), (att0[0], 2), (att0[1], 2)):
        last = s.step(name, (last,))
    grad_tokens = crop_major(at_core, in_mine, in_x, (last,)).reshape(C, 1, T, D)

    parts = [a.result() for a in att0]
    g_att = (jnp.concatenate([a[0] for a in parts], axis=1), att1.result()[0])
    small = jnp.concatenate([a[1] for a in parts], axis=1)[:56]
    for k in range(sub.bit_length() - 1):
        small = small + lax.ppermute(small, "img", [(i, i ^ (1 << k)) for i in range(n_img)])
    mats = []
    for b, mlp in enumerate((mlp0, mlp1)):
        att = scatter_rest(g_att[b], 0, img, sub)
        down, up = mlp.result()
        g_down = scatter_rest(get_down(down), 1, img, sub)
        g_up = scatter_rest(up, 0, img, sub)
        mats.append((att[:, : 3 * D // 4], att[:, 3 * D // 4 :], g_up, g_down.T))

    g_qkv, g_out, g_up, g_down = (jnp.stack(pair) for pair in zip(*mats))
    table = small[24:].reshape(PER, 8, 3, TABLE)[:, :NG, :2, :169].transpose(2, 3, 1, 0).reshape(2, 169, HEADS)
    width = D // n_img

    vectors = small[:24].reshape(2, 12, D)
    mine = lax.dynamic_slice_in_dim(vectors[:, :8], img * width, width, 2)
    up_bias = lax.dynamic_slice_in_dim(vectors[:, 8:].reshape(2, FF), img * (4 * width), 4 * width, 1)

    return (
        block_out.transpose(1, 0, 2)[:, None], grad_tokens, mine[:, 0], mine[:, 1], g_qkv, mine[:, 2], mine[:, 3], table,
        g_out, mine[:, 6], mine[:, 4], mine[:, 5], g_up, up_bias, g_down, mine[:, 7],
    )


def solution(mesh):
    shard = P("img", "win", None, None)
    vec, mat = P(None, "img"), P(None, "img", "win")
    return jax.shard_map(
        functools.partial(per_device, n_img=mesh.shape["img"]),
        mesh=mesh,
        in_specs=(shard, P("img")) + (P(),) * 14 + (shard,),
        out_specs=(shard, shard, vec, vec, mat, vec, vec, P(), mat, vec, vec, vec, mat, vec, mat, vec),
        check_vma=False,
    )
```

```python
import functools

import jax
import jax.numpy as jnp
from jax import lax
from jax.experimental import pallas as pl
from jax.experimental.pallas import tpu as pltpu
from jax.sharding import PartitionSpec as P

HEADS = 24
HD = 32
SIDE = 7
T = SIDE * SIDE
TP = 56
TQ = 64
D = 768
FF = 3072
C = 8
ROWS = T * C
PAD_ROWS = TQ * C
HALF = C // 2
PIECE = T * HALF
LANE = 128
NG = D // LANE
PER = LANE // HD
GT = PER * TQ
EPSILON = 1e-05
SCALE = HD ** (-0.5)
NEG = -1e30
QCH = 768
FCH = 1536
WIN = 2
N_Q = 3 * D // QCH
N_F = FF // FCH
W_UP = D // 2
MINE = D // 4
VMEM_LIMIT = 58 << 20
COST = 0.4
F32 = jnp.float32
BF16 = jnp.bfloat16

TAIL_K = 0.3
TAIL = (
    0.11963200491345692,
    0.12071217642148169,
    0.10017566554041868,
    0.12769280877164998,
    -0.052036176065482394,
    0.20455934198696718,
    -0.15616004916725648,
    0.035424145900813254,
)
INV_SQRT_2PI = 0.3989422804014327

def nt(left, right):
    return lax.dot_general(left, right, (((1,), (1,)), ((), ())), preferred_element_type=F32)


def tn(left, right):
    return lax.dot_general(left, right, (((0,), (0,)), ((), ())), preferred_element_type=F32)


def nn(left, right):
    return jnp.dot(left, right, preferred_element_type=F32)


def norm_parts(values):
    average = jnp.mean(values, axis=-1, keepdims=True)
    centered = values - average
    inverse = lax.rsqrt(jnp.mean(centered * centered, axis=-1, keepdims=True) + EPSILON)
    return centered * inverse, inverse


def norm_back(grad_out, normed, inverse, gain):
    scaled = grad_out * gain
    return inverse * (
        scaled
        - jnp.mean(scaled, axis=-1, keepdims=True)
        - normed * jnp.mean(scaled * normed, axis=-1, keepdims=True)
    )


def gelu_parts(a):
    bell = jnp.exp(-0.5 * a * a)
    size = jnp.abs(a)
    t = 1.0 / (1.0 + TAIL_K * size)
    poly = jnp.full_like(t, TAIL[-1])
    for coef in TAIL[-2::-1]:
        poly = poly * t + coef
    tail = bell * (t * poly)
    phi = jnp.where(a < 0, tail, 1.0 - tail)
    return a * phi, phi + a * (INV_SQRT_2PI * bell)


def head_masks(rows):
    lanes = lax.broadcasted_iota(jnp.int32, (rows, LANE), 1)
    return [(lanes >= HD * h) & (lanes < HD * (h + 1)) for h in range(PER)]


def spread(values, ones):
    return jnp.concatenate([values * m for m in ones], axis=0)


def gather_heads(stacked, masks):
    out = stacked[(PER - 1) * TQ : (PER - 1) * TQ + TP]
    for h in range(PER - 2, -1, -1):
        out = jnp.where(masks[h], stacked[h * TQ : h * TQ + TP], out)
    return out


def soft(scores):
    e = jnp.exp(scores - jnp.max(scores, axis=0, keepdims=True))
    return e * (1.0 / jnp.sum(e, axis=0, keepdims=True))


def colsum(values):
    return jnp.sum(values, axis=0, keepdims=True)


def rows_of(w, n=T, stride=C):
    return pl.ds(w, n, stride=stride)


def lanes_at(n, width):
    return pl.ds(pl.multiple_of(n * width, width), width)


def put_rolled(dest, source, a, back):
    shift, kept = (-3, range(3, 7)) if back else (3, range(0, 4))
    for i in range(SIDE):
        for j in range(SIDE):
            half = a if i in kept else 1 - a
            tile = source[half, SIDE * ((i + shift) % SIDE) + (j + shift) % SIDE]
            if j not in kept:
                tile = pltpu.roll(tile, HALF, 0)
            t = SIDE * i + j
            dest[C * t : C * (t + 1), :] = tile


ANY = pl.BlockSpec(memory_space=pl.ANY)
VM = pl.BlockSpec(memory_space=pltpu.VMEM)
SM = pl.BlockSpec(memory_space=pltpu.SMEM)


def cost(micros):
    return pl.CostEstimate(flops=int(micros * COST * 1.15e9), bytes_accessed=0, transcendentals=0)


def shape(dims, dtype):
    return jax.ShapeDtypeStruct(dims, dtype)


def fixed(dims, single=False):
    mode = dict(pipeline_mode=pl.Buffered(1)) if single else {}
    return pl.BlockSpec(dims, lambda *_: (0,) * len(dims), **mode)


def per_half(dims):
    return pl.BlockSpec((1, *dims), lambda a, *_: (a, *(0,) * len(dims)))


def call(body, args, in_specs, outs, out_specs, estimate, name, after=(), grid=(), scalars=0, scratch=(), reuse=0):
    n_in, n_after = len(args), len(after)

    def wrapped(*refs):
        return body(*refs[:n_in], *refs[n_in + n_after :])

    return pl.pallas_call(
        wrapped,
        grid_spec=pltpu.PrefetchScalarGridSpec(
            num_scalar_prefetch=scalars,
            grid=grid,
            in_specs=list(in_specs) + [ANY] * n_after,
            out_specs=out_specs,
            scratch_shapes=list(scratch),
        ),
        out_shape=outs,
        input_output_aliases={n_in + k: k for k in range(reuse)},
        compiler_params=pltpu.CompilerParams(vmem_limit_bytes=VMEM_LIMIT),
        cost_estimate=estimate,
        name=name,
    )(*args, *after)


def crop_rows(core, count, crops, after=()):
    def body(at, n, src, mine, other, s):
        wide = src[...].astype(F32).reshape(ROWS, D)
        for g in range(NG):
            s[g] = wide[:, LANE * g : LANE * (g + 1)]
        for k in range(HALF):
            for out, c in ((mine, at[0]), (other, 1 - at[0])):
                crop = HALF * c + k
                keep = jnp.where(crop < n[0], 1.0, 0.0).astype(F32)
                for g in range(NG):
                    out[g, rows_of(k, stride=HALF), :] = s[g, rows_of(crop), :] * keep

    return call(
        body, (core, count, crops), [SM, SM, VM], [shape((NG, PIECE, LANE), F32)] * 2, [VM] * 2, cost(2.5), "crop_rows", after, scratch=[pltpu.VMEM((NG, ROWS, LANE), F32)],
    )


def weave(dest, pieces):
    for b, piece in enumerate(pieces):
        for k in range(HALF):
            for g in range(NG):
                dest[g, rows_of(HALF * b + k), :] = piece[g, rows_of(k, stride=HALF), :]


def join_pieces(x_at, pieces, after=()):
    def body(x, *refs):
        *src, out, s = refs
        for k in range(2):
            weave(s, src[2 * k : 2 * k + 2])
            for g in range(NG):
                out[x[0] ^ k, :, :, LANE * g : LANE * (g + 1)] = s[g].reshape(T, C, LANE)

    return call(
        body, (x_at, *pieces), [SM] + [VM] * 4, shape((2, T, C, D), F32), VM, cost(4), "join_pieces", after,
        scratch=[pltpu.VMEM((NG, ROWS, LANE), F32)],
    )


def own_quadrants(x_at, both_halves, rolled, after=()):
    def body(x, src, mine, other, full, s):
        if rolled:
            put_rolled(full, src, x[0], True)
        else:
            full[...] = src[x[0]].reshape(ROWS, D)
        for g in range(NG):
            s[g] = full[:, LANE * g : LANE * (g + 1)]
        for b, out in enumerate((mine, other)):
            for k in range(HALF):
                for g in range(NG):
                    out[g, rows_of(k, stride=HALF), :] = s[g, rows_of(HALF * b + k), :]

    return call(
        body, (x_at, both_halves), [SM, VM], [shape((NG, PIECE, LANE), F32)] * 2, [VM] * 2, cost(3), "own_quadrants", after, scratch=[pltpu.VMEM((ROWS, D), F32), pltpu.VMEM((NG, ROWS, LANE), F32)],
    )


def token_major(core, count, mine, theirs, after=()):
    def body(at, n, a, b, out, s):
        for k in range(HALF):
            for src, c in ((a, at[0]), (b, 1 - at[0])):
                crop = HALF * c + k
                keep = jnp.where(crop < n[0], 1.0, 0.0).astype(F32)
                for g in range(NG):
                    s[g, rows_of(crop), :] = src[g, rows_of(k, stride=HALF), :] * keep
        for g in range(NG):
            out[:, :, LANE * g : LANE * (g + 1)] = s[g].reshape(T, C, LANE).astype(BF16)

    return call(
        body, (core, count, mine, theirs), [SM, SM, VM, VM], shape((T, C, D), BF16), VM, cost(2.5), "token_major", after, scratch=[pltpu.VMEM((NG, ROWS, LANE), F32)],
    )


def crop_major(core, mine, theirs, after=()):
    def body(at, a, b, out):
        for k in range(HALF):
            for src, c in ((a, at[0]), (b, 1 - at[0])):
                for g in range(NG):
                    out[pl.ds((HALF * c + k) * (T * NG) + g, T, stride=NG), :] = src[g, rows_of(k, stride=HALF), :]

    return call(
        body, (core, mine, theirs), [SM, VM, VM], shape((C * T * NG, LANE), F32), VM, cost(2.5), "crop_major", after,
    )


def fwd_body(b, which, *refs):
    a = pl.program_id(0)
    if b == 0:
        at_x, p0, p1, *rest = refs
    else:
        src, mask, *rest = refs
    (
        bias, ln1g, ln1b, bq, bv, bout, ln2g, ln2b, bup, bdown,
        wqkv_h, wout_h, wup_h, wdown_h,
        z_h, h_h, qkvc_h, o_h, y_h, h2_h, g_h, gp_h, zn_o,
        wqkv, wout, wup, wdown, qkv_s, o_s, bqkv, bias_s,
        z_o, h_o, qkvc_o, o_o, y_o, h2_o, g_o, gp_o, sem_q, sem_o, sem_u, sem_d, sem_out,
    ) = rest
    at = at_x[0] ^ which if b == 0 else a
    results = (
        (z_o, z_h), (h_o, h_h), (qkvc_o, qkvc_h), (o_o, o_h), (y_o, y_h), (h2_o, h2_h), (g_o, g_h), (gp_o, gp_h),
    )

    def out(k):
        return pltpu.make_async_copy(results[k][0].at[0], results[k][1].at[at], sem_out.at[k])

    def free(k):
        @pl.when(a > 0)
        def _():
            out(k).wait()

    def cp_q(n):
        return pltpu.make_async_copy(
            wqkv_h.at[b, :, lanes_at(n, QCH)], wqkv.at[:, lanes_at(n, QCH)], sem_q.at[n]
        )

    def cp_u(n):
        return pltpu.make_async_copy(
            wup_h.at[b, :, lanes_at(n, FCH)], wup.at[:, lanes_at(n, FCH)], sem_u.at[n]
        )

    def cp_d(n):
        return pltpu.make_async_copy(
            wdown_h.at[b, lanes_at(n, FCH), :], wdown.at[lanes_at(n, FCH), :], sem_d.at[n]
        )

    cp_o = pltpu.make_async_copy(wout_h.at[b], wout, sem_o)

    def wait(copy):
        @pl.when(a == 0)
        def _():
            copy.wait()

    @pl.when(a == 0)
    def _():
        for n in range(N_Q):
            cp_q(n).start()
        cp_o.start()
        for n in range(N_F):
            cp_u(n).start()
            cp_d(n).start()
        bqkv[:, 0:D] = bq[b : b + 1, :]
        bqkv[:, D : 2 * D] = jnp.zeros((1, D), F32)
        bqkv[:, 2 * D :] = bv[b : b + 1, :]
        qkv_s[:, ROWS:, :] = jnp.zeros((3 * NG, PAD_ROWS - ROWS, LANE), F32)

    free(0)
    if b == 0:
        weave(o_s, (p0, p1))
        for g in range(NG):
            z_o[0, :, LANE * g : LANE * (g + 1)] = o_s[g, 0:ROWS, :]
    else:
        put_rolled(z_o.at[0], src, a, False)
        for w in range(2):
            for g in range(NG):
                bias_s[w * NG + g] = bias[NG + g] + mask[0, w]
    out(0).start()
    normed, _ = norm_parts(z_o[0])
    free(1)
    h_o[0] = (normed * ln1g[b : b + 1, :] + ln1b[b : b + 1, :]).astype(BF16)
    out(1).start()

    def qkv_step(n, _):
        wait(cp_q(n))
        joint = nn(h_o[0], wqkv[:, lanes_at(n, QCH)]) + bqkv[:, lanes_at(n, QCH)]
        joint = joint * jnp.where(n < D // QCH, SCALE, 1.0)
        joint = joint.astype(BF16).astype(F32)
        for k in range(QCH // LANE):
            qkv_s[n * (QCH // LANE) + k, 0:ROWS, :] = joint[:, LANE * k : LANE * (k + 1)]
        return 0

    lax.fori_loop(0, N_Q, qkv_step, 0)
    masks = head_masks(TP)
    ones = [m.astype(F32).astype(BF16) for m in head_masks(TQ)]

    def attend(step, _):
        items = [(step * WIN + i, g) for i in range(WIN) for g in range(NG)]
        qs = [qkv_s[g, rows_of(w, TQ), :].astype(BF16) for w, g in items]
        ks = [qkv_s[NG + g, rows_of(w, TP), :].astype(BF16) for w, g in items]
        vs = [qkv_s[2 * NG + g, rows_of(w, TP), :].astype(BF16) for w, g in items]
        for (w, g), q, k, v in zip(items, qs, ks, vs):
            qkvc_o[0, w, g] = q
            qkvc_o[0, w, NG + g, 0:TP] = k
            qkvc_o[0, w, 2 * NG + g, 0:TP] = v
        added = [bias[g] if b == 0 else bias_s[w // HALF * NG + g] for w, g in items]
        scores = [nt(k, spread(q, ones)) + extra for k, q, extra in zip(ks, qs, added)]
        probs = [soft(score).astype(BF16) for score in scores]
        for (w, g), prob, v in zip(items, probs, vs):
            o_s[g, rows_of(w, TP), :] = gather_heads(tn(prob, v), masks)
        return 0

    free(2)
    lax.fori_loop(0, C // WIN, attend, 0, unroll=2)
    out(2).start()
    free(3)
    for g in range(NG):
        o_o[0, :, LANE * g : LANE * (g + 1)] = o_s[g, 0:ROWS, :].astype(BF16)
    out(3).start()
    wait(cp_o)
    free(4)
    y_o[0] = z_o[0] + (nn(o_o[0], wout[...]) + bout[b : b + 1, :])
    out(4).start()
    normed, _ = norm_parts(y_o[0])
    free(5)
    h2_o[0] = (normed * ln2g[b : b + 1, :] + ln2b[b : b + 1, :]).astype(BF16)
    out(5).start()
    free(6)
    free(7)
    def mlp_step(n, _):
        wait(cp_u(n))
        up = nn(h2_o[0], wup[:, lanes_at(n, FCH)]) + bup[b : b + 1, lanes_at(n, FCH)]
        act, slope = gelu_parts(up)
        g_o[0, :, lanes_at(n, FCH)] = act.astype(BF16)
        gp_o[0, :, lanes_at(n, FCH)] = slope.astype(BF16)
        return 0

    lax.fori_loop(0, N_F, mlp_step, 0)
    out(6).start()
    out(7).start()
    for n in range(N_F):
        wait(cp_d(n))
    zn_o[0] = (y_o[0] + (nn(g_o[0], wdown[...]) + bdown[b : b + 1, :])).reshape(T, C, D)

    @pl.when(a == pl.num_programs(0) - 1)
    def _():
        for k in range(len(results)):
            out(k).wait()


def block_fwd(b, sources, bias, p, which=None, after=()):
    outs = [
        shape((2, ROWS, D), F32),
        shape((2, ROWS, D), BF16),
        shape((2, C, 3 * NG, TQ, LANE), BF16),
        shape((2, ROWS, D), BF16),
        shape((2, ROWS, D), F32),
        shape((2, ROWS, D), BF16),
        shape((2, ROWS, FF), BF16),
        shape((2, ROWS, FF), BF16),
        shape((2, T, C, D), F32),
    ]
    if b == 0:
        specs = [fixed((NG, PIECE, LANE), True)] * 2
        out_specs = [pl.BlockSpec((1, T, C, D), lambda a, s: (s[0] ^ which, 0, 0, 0))]
    else:
        specs = [fixed((2, T, C, D), True), per_half((2, TP, GT))]
        out_specs = [per_half((T, C, D))]
    small = (bias, p["ln1_gain"], p["ln1_bias"], p["b_query"], p["b_value"], p["b_out"],
             p["ln2_gain"], p["ln2_bias"], p["b_up"], p["b_down"])
    big = (p["w_qkv"], p["w_out"], p["w_up"], p["w_down"])
    return call(
        functools.partial(fwd_body, b, which),
        (*sources, *small, *big),
        specs + [fixed(v.shape, True) for v in small] + [ANY] * 4,
        outs,
        [ANY] * 8 + out_specs,
        cost(21 if which is not None else 36),
        f"forward_{b}",
        after,
        grid=(2 if which is None else 1,),
        scalars=int(which is not None),
        reuse=len(outs) if which == 1 else 0,
        scratch=[
            pltpu.VMEM((D, 3 * D), BF16),
            pltpu.VMEM((D, D), BF16),
            pltpu.VMEM((D, FF), BF16),
            pltpu.VMEM((FF, D), BF16),
            pltpu.VMEM((3 * NG, PAD_ROWS, LANE), F32),
            pltpu.VMEM((NG, PAD_ROWS, LANE), F32),
            pltpu.VMEM((1, 3 * D), F32),
            pltpu.VMEM((2 * NG, TP, GT), F32),
            *(pltpu.VMEM((1, *o.shape[1:]), o.dtype) for o in outs[:8]),
            pltpu.SemaphoreType.DMA((N_Q,)),
            pltpu.SemaphoreType.DMA,
            pltpu.SemaphoreType.DMA((N_F,)),
            pltpu.SemaphoreType.DMA((N_F,)),
            pltpu.SemaphoreType.DMA((8,)),
        ],
    )


def mlp_back_body(b, x_at, core, src, y, gp, act, hid, ln2g, wdown_h, wup_h, dd_o, da_o, dy_o, dyr_o, sv_o, down_o, up_o,
                  wdown, wup, dz, dd, da_s, sem_d, sem_u):
    a = pl.program_id(0)

    def cp_u(n):
        return pltpu.make_async_copy(
            wup_h.at[b, :, lanes_at(n, D)], wup.at[:, lanes_at(n, D)], sem_u.at[n]
        )

    def cp_d(n):
        return pltpu.make_async_copy(
            wdown_h.at[b, lanes_at(n, D), :], wdown.at[lanes_at(n, D), :], sem_d.at[n]
        )

    def wait(copy):
        @pl.when(a == 0)
        def _():
            copy.wait()

    @pl.when(a == 0)
    def _():
        for n in range(4):
            cp_d(n).start()
            cp_u(n).start()
        sv_o[...] = jnp.zeros_like(sv_o)

    put_rolled(dz, src, a, b == 0)
    low = dz[...].astype(BF16)
    dd[...] = low
    sv_o[3:4, :] += colsum(low.astype(F32))
    for x in range(2):

        @pl.when(x_at[0] == x)
        def _():
            for c in range(2):
                w = 2 * x + c
                dd_o[c, 0] = dd[:, MINE * w : MINE * (w + 1)]

    def step(n, _):
        wait(cp_d(n))
        grad_act = nt(dd[...], wdown[lanes_at(n, D), :])
        da = (grad_act * gp[0, :, lanes_at(n, D)].astype(F32)).astype(BF16)

        da_s[:, lanes_at(n, D)] = da

        @pl.when(n // 2 == x_at[0])
        def _():
            da_o[0, :, lanes_at(n % 2, D)] = da

        sv_o[pl.ds(4 + n, 1), :] += colsum(da.astype(F32))
        return 0

    lax.fori_loop(0, 4, step, 0)
    for n in range(4):
        wait(cp_u(n))
    dh2 = nt(da_s[...], wup[...])
    normed, inverse = norm_parts(y[0])
    sv_o[0:1, :] += colsum(dh2 * normed)
    sv_o[1:2, :] += colsum(dh2)
    dy = dz[...] + norm_back(dh2, normed, inverse, ln2g[b : b + 1, :])
    dy_o[0] = dy
    low = dy.astype(BF16)
    dyr_o[0] = low
    sv_o[2:3, :] += colsum(low.astype(F32))
    down = tn(dd_o[1 - core[0], 0], act[0])
    up = tn(hid[0], da_o[0, :, lanes_at(1 - core[0], D)])

    def put(add):
        for k in range(8):
            add_down(down_o, k, down[:, W_UP * k : W_UP * (k + 1)], add)
            rows = up[D // 8 * k : D // 8 * (k + 1)]
            up_o[k] = up_o[k] + rows if add else rows

    for half in range(2):
        pl.when(a == half)(functools.partial(put, half == 1))


def mlp_back(b, x_at, core, src, y, gp, act, hid, p, after=()):
    return call(
        functools.partial(mlp_back_body, b),
        (x_at, core, src, y, gp, act, hid, p["ln2_gain"], p["w_down"], p["w_up"]),
        [SM, SM, fixed((2, T, C, D), True), per_half((ROWS, D)), per_half((ROWS, FF)), per_half((ROWS, FF)),
         per_half((ROWS, D)), fixed((2, D)), ANY, ANY],
        [
            shape((2, 2, ROWS, MINE), BF16),
            shape((2, ROWS, FF // 2), BF16),
            shape((2, ROWS, D), F32),
            shape((2, ROWS, D), BF16),
            shape((8, D), F32),
            shape((8, *BLOCK), F32),
            shape((8, *BLOCK), F32),
        ],
        [
            pl.BlockSpec((2, 1, ROWS, MINE), lambda a: (0, a, 0, 0)),
            per_half((ROWS, FF // 2)),
            per_half((ROWS, D)),
            per_half((ROWS, D)),
            fixed((8, D)),
            fixed((8, *BLOCK), True),
            fixed((8, *BLOCK), True),
        ],
        cost(22),
        f"mlp_back_{b}",
        after,
        grid=(2,),
        scratch=[
            pltpu.VMEM((FF, D), BF16),
            pltpu.VMEM((D, FF), BF16),
            pltpu.VMEM((ROWS, D), F32),
            pltpu.VMEM((ROWS, D), BF16),
            pltpu.VMEM((ROWS, FF), BF16),
            pltpu.SemaphoreType.DMA((4,)),
            pltpu.SemaphoreType.DMA((4,)),
        ],
    )


TABLE = 256
BLOCK = (D // 8, D)


def table_sums(ds, moved):
    row = lax.broadcasted_iota(jnp.int32, (GT, PER * LANE), 0)
    col = lax.broadcasted_iota(jnp.int32, (GT, PER * LANE), 1)
    t = row & (TQ - 1)
    i = sum((t >= SIDE * k).astype(jnp.int32) for k in range(1, SIDE))
    there = (row >> 6 == col >> 7) & (t < T) & ((col & (LANE - 1)) == t + 6 * i)
    onehot = there.astype(F32).astype(BF16)
    moved[:, NG * TP :, :] = jnp.zeros((PER, (8 - NG) * TP, LANE), F32)
    for g in range(NG):
        rest = ds[g]
        total = jnp.zeros((TP, PER * LANE), F32)
        for _ in range(3):
            part = rest.astype(BF16)
            total += nn(part, onehot)
            rest = rest - part.astype(F32)
        for h in range(PER):
            moved[h, TP * g : TP * (g + 1), :] = total[:, LANE * h : LANE * (h + 1)]


def sum_table(moved, put):
    for h in range(PER):
        total = jnp.zeros((8, TABLE), F32)
        for u in range(T):
            v = moved[h, pl.ds(u, 8, stride=TP), :]
            shift = 13 * (6 - u // SIDE) + 6 - u % SIDE
            total += pltpu.roll(jnp.concatenate([v, jnp.zeros_like(v)], axis=1), shift, 1)
        put(h, total)


def attn_back_body(b, x_at, core, dyr, qkvc, dy, z, hid, att, *refs):
    if b == 1:
        mask, *refs = refs
    bias, ln1g, *refs = refs
    if b == 0:
        sv_m0, sv_a1, sv_m1, table1, *refs = refs
    (wout_h, wqkv_h, r3_o, sv_o, sum_o, grad_o, *part_o,
     wout, wqkv, do_s, dqkv_s, dq, bias_s, ds_o, moved, sem_o, sem_q) = refs
    a = pl.program_id(0)
    cp_o = pltpu.make_async_copy(wout_h.at[b], wout, sem_o)

    def cp_q(n):
        return pltpu.make_async_copy(
            wqkv_h.at[b, :, lanes_at(n, QCH)], wqkv.at[:, lanes_at(n, QCH)], sem_q.at[n]
        )

    def wait(copy):
        @pl.when(a == 0)
        def _():
            copy.wait()

    @pl.when(a == 0)
    def _():
        cp_o.start()
        for n in range(N_Q):
            cp_q(n).start()
        do_s[:, ROWS:, :] = jnp.zeros((NG, PAD_ROWS - ROWS, LANE), F32)
        ds_o[...] = jnp.zeros_like(ds_o)
        sv_o[...] = jnp.zeros_like(sv_o)

    if b == 1:
        for w in range(2):
            for g in range(NG):
                bias_s[w * NG + g] = bias[NG + g] + mask[0, w]
    wait(cp_o)
    do = nt(dyr[0], wout[...]).astype(BF16).astype(F32)
    for g in range(NG):
        do_s[g, 0:ROWS, :] = do[:, LANE * g : LANE * (g + 1)]
    masks = head_masks(TP)
    ones = [m.astype(F32).astype(BF16) for m in head_masks(TQ)]

    def attend(step, _):
        items = [(step * WIN + i, g) for i in range(WIN) for g in range(NG)]
        ks = [qkvc[0, w, NG + g, 0:TP] for w, g in items]
        q_wide = [spread(qkvc[0, w, g], ones) for w, g in items]
        do_wide = [spread(do_s[g, rows_of(w, TQ), :].astype(BF16), ones) for w, g in items]
        added = [bias[g] if b == 0 else bias_s[w // HALF * NG + g] for w, g in items]
        scores = [nt(k, q) + extra for k, q, extra in zip(ks, q_wide, added)]
        dprobs = [nt(qkvc[0, w, 2 * NG + g, 0:TP], d) for (w, g), d in zip(items, do_wide)]
        probs = [soft(score) for score in scores]
        weighted = [p * d for p, d in zip(probs, dprobs)]
        ds = [x - p * jnp.sum(x, axis=0, keepdims=True) for x, p in zip(weighted, probs)]
        for (w, g), d in zip(items, ds):
            ds_o[g] += d
        low = [d.astype(BF16) for d in ds]
        dks = [nn(x, q) for x, q in zip(low, q_wide)]
        dvs = [nn(p.astype(BF16), d) for p, d in zip(probs, do_wide)]
        dqs = [tn(x, k) for x, k in zip(low, ks)]
        for (w, g), d_q, d_k, d_v in zip(items, dqs, dks, dvs):
            dqkv_s[g, rows_of(w, TP), :] = gather_heads(d_q, masks) * SCALE
            dqkv_s[NG + g, rows_of(w, TP), :] = d_k
            dqkv_s[2 * NG + g, rows_of(w, TP), :] = d_v
        return 0

    lax.fori_loop(0, C // WIN, attend, 0)
    for g in range(3 * NG):
        dq[:, LANE * g : LANE * (g + 1)] = dqkv_s[g, 0:ROWS, :].astype(BF16)
    sv_o[2:3, :] += colsum(dq[:, 0:D].astype(F32))
    sv_o[3:4, :] += colsum(dq[:, 2 * D :].astype(F32))
    for n in range(N_Q):
        wait(cp_q(n))
    dh = nt(dq[...], wqkv[...])
    for x in range(2):

        @pl.when(x_at[0] == x)
        def _():
            for c in range(2):
                w = 2 * x + c
                r3_o[c, 0] = jnp.concatenate(
                    [dq[:, 3 * MINE * w : 3 * MINE * (w + 1)], dyr[0, :, MINE * w : MINE * (w + 1)]], axis=1
                )

    normed, inverse = norm_parts(z[0])
    sv_o[0:1, :] += colsum(dh * normed)
    sv_o[1:2, :] += colsum(dh)
    grad_o[0] = (dy[0] + norm_back(dh, normed, inverse, ln1g[b : b + 1, :])).reshape(T, C, D)
    other = r3_o[1 - core[0], 0]
    parts = [attn_columns(tn, hid[0], att[0], other[:, W_UP * n : W_UP * (n + 1)], W_UP * n, W_UP) for n in range(2)]

    def put_parts(add):
        for out, part in zip(part_o, parts):
            blocks = part.reshape(8, D // 8, W_UP)
            out[...] = out[...] + blocks if add else blocks

    for half in range(2):
        pl.when(a == half)(functools.partial(put_parts, half == 1))

    @pl.when(a == 1)
    def _():
        table_sums(ds_o, moved)
        if b == 1:
            sum_table(moved, lambda h, v: sum_o.__setitem__(h, v))
            return
        sum_o[...] = jnp.zeros_like(sum_o)
        for at, ref in ((0, sv_o), (4, sv_m0), (12, sv_a1), (16, sv_m1)):
            for k in range(2):
                sum_o[24 * k + at : 24 * k + at + ref.shape[0], :] = ref[:, W_UP * k : W_UP * (k + 1)]

        def put(h, v, at=48):
            sum_o[at + NG * h : at + NG * (h + 1), 0:TABLE] = v[0:NG]

        sum_table(moved, put)
        for h in range(PER):
            put(h, table1[h], 72)


def attn_back(b, x_at, core, dyr, qkvc, dy, z, hid, att, mask, bias, p, sums=(), after=()):
    masks = [mask] if b else []
    sum_shape = (PER, 8, TABLE) if b else (D // 8, W_UP)
    return call(
        functools.partial(attn_back_body, b),
        (x_at, core, dyr, qkvc, dy, z, hid, att, *masks, bias, p["ln1_gain"], *sums, p["w_out"], p["w_qkv"]),
        [SM, SM, per_half((ROWS, D)), per_half((C, 3 * NG, TQ, LANE))] + [per_half((ROWS, D))] * 4
        + [per_half((2, TP, GT))] * b
        + [fixed(bias.shape, True), fixed((2, D)), *(fixed(v.shape) for v in sums), ANY, ANY],
        [shape((2, 2, ROWS, D), BF16), shape((4, D), F32), shape(sum_shape, F32), shape((2, T, C, D), F32)]
        + [shape((8, D // 8, W_UP), F32)] * 2,
        [
            pl.BlockSpec((2, 1, ROWS, D), lambda a: (0, a, 0, 0)),
            fixed((4, D)),
            fixed(sum_shape),
            per_half((T, C, D)),
        ]
        + [fixed((8, D // 8, W_UP), True)] * 2,
        cost(31),
        f"attn_back_{b}",
        after,
        grid=(2,),
        scratch=[
            pltpu.VMEM((D, D), BF16),
            pltpu.VMEM((D, 3 * D), BF16),
            pltpu.VMEM((NG, PAD_ROWS, LANE), F32),
            pltpu.VMEM((3 * NG, PAD_ROWS, LANE), F32),
            pltpu.VMEM((ROWS, 3 * D), BF16),
            pltpu.VMEM((2 * NG, TP, GT), F32),
            pltpu.VMEM((NG, TP, GT), F32),
            pltpu.VMEM((PER, 8 * TP, LANE), F32),
            pltpu.SemaphoreType.DMA,
            pltpu.SemaphoreType.DMA((N_Q,)),
        ],
    )


def halves(left, right):
    return tn(left(0), right(0)) + tn(left(1), right(1))


def insert_bit(i, place, bit):
    return ((i >> place) << (place + 1)) | (bit << place) | (i & ((1 << place) - 1))


def row_pairs(values, k):
    height = values.shape[0] // 8
    for i in range(4):
        low = insert_bit(i, k, 0)
        high = low | (1 << k)
        yield i, low, high, values[height * low : height * (low + 1)], values[height * high : height * (high + 1)]


def put_down(out, i, total):
    half = MINE // 2
    out[i, :, 0:W_UP] = total[0:half]
    out[i, :, W_UP:] = total[half:]


def add_down(out, i, total, add):
    put_down(out, i, total + get_down(out[i]) if add else total)


def get_down(block):
    return jnp.concatenate([block[:, 0:W_UP], block[:, W_UP:]], axis=0)


def down_mine(bits, dd, act, recv, first, after=()):
    def body(s, l, rk, rs, gk, gs, keep, send):
        put_down(keep, 0, halves(lambda a: l[0, a], lambda a: rk[a]) + get_down(gk[0]))
        put_down(send, 0, halves(lambda a: l[0, a], lambda a: rs[a]) + get_down(gs[0]))

    def block(flip):
        return lambda i, s: insert_bit(i, first, s[1 + first] ^ flip)

    return call(
        body, (bits, dd, act, act, recv, recv),
        [pl.BlockSpec((1, 2, ROWS, MINE), lambda i, s: (s[0], 0, 0, 0))]
        + [pl.BlockSpec((2, ROWS, W_UP), lambda i, s, m=block(f): (0, 0, m(i, s))) for f in (0, 1)]
        + [pl.BlockSpec((1, *BLOCK), lambda i, s, m=block(f): (m(i, s), 0, 0)) for f in (0, 1)],
        [shape((4, *BLOCK), F32)] * 2, [pl.BlockSpec((1, *BLOCK), lambda i, s: (i, 0, 0))] * 2,
        cost(6.9), "down_mine", after, (4,), 1,
    )


def up_mine(bits, hid, da, recv, first, after=()):
    def body(s, l, r, got, keep, send):
        total = halves(lambda a: l[a], lambda a: r[a])
        mine = s[1 + first] == 0
        for i, j, k, p, q in row_pairs(total, first):
            p, q = p + got[j], q + got[k]
            keep[i] = jnp.where(mine, p, q)
            send[i] = jnp.where(mine, q, p)

    return call(
        body, (bits, hid, da, recv),
        [fixed((2, ROWS, D)), pl.BlockSpec((2, ROWS, W_UP), lambda n, s: (0, 0, 2 * s[0] + n)),
         pl.BlockSpec((8, D // 8, W_UP), lambda n, s: (0, 0, n))],
        [shape((4, *BLOCK), F32)] * 2, [pl.BlockSpec((4, D // 8, W_UP), lambda n, s: (0, 0, n))] * 2,
        cost(5.7), "up_mine", after, (2,), 1,
    )


def attn_columns(product, hid, att, r, lo, width):
    edge = 3 * MINE
    cut = edge // LANE * LANE
    parts = []
    if lo < cut:
        parts.append(product(hid, r[..., 0 : min(cut - lo, width)]))
    if lo + width > cut:
        lane = lax.broadcasted_iota(jnp.int32, (D, LANE), 1)
        right = r[..., cut - lo : cut - lo + LANE]
        parts.append(jnp.where(lane < edge - cut, product(hid, right), product(att, right)))
    if lo + width > cut + LANE:
        parts.append(product(att, r[..., cut - lo + LANE : width]))
    return parts[0] if len(parts) == 1 else jnp.concatenate(parts, axis=1)


def two_halves(left, right):
    return tn(left[0], right[0]) + tn(left[1], right[1])


def attn_mine(bits, hid, att, r3, recv, first, cols, small=None, after=()):
    extra = small is not None
    width = W_UP * len(cols)

    def body(s, h, o, r, *refs):
        gots, more, (keep, send) = refs[: len(cols)], refs[len(cols) : -2], refs[-2:]
        for k, n in enumerate(cols):

            @pl.when(pl.program_id(0) == k)
            def _():
                total = attn_columns(two_halves, h, o, r[0], n * W_UP, W_UP)
                mine = s[1 + first] == 0
                for i, j, jj, p, q in row_pairs(total, first):
                    p, q = p + gots[k][j], q + gots[k][jj]
                    keep[i] = jnp.where(mine, p, q)
                    send[i] = jnp.where(mine, q, p)
                if extra:
                    added = more[0][...] + more[1][...]
                    keep[4] = added
                    send[4] = added

    at = lambda n: n + cols[0]
    specs = [
        fixed((2, ROWS, D)),
        fixed((2, ROWS, D)),
        pl.BlockSpec((1, 2, ROWS, W_UP), lambda n, s: (s[0], 0, 0, at(n))),
    ]
    args = [bits, hid, att, r3]
    for n in cols:
        args.append(recv[n])
        specs.append(fixed((8, D // 8, W_UP)))
    if extra:
        args += small
        specs += [fixed((D // 8, W_UP))] * 2
    out = pl.BlockSpec((4 + extra, D // 8, W_UP), lambda n, s: (0, 0, n))
    return call(
        body, args, specs, [shape((4 + extra, D // 8, width), F32)] * 2, [out] * 2,
        cost(1.5 + 2.8 * len(cols)), "attn_mine", after, (len(cols),), 1,
    )


def split_sum(streams, extra, after=(), through=()):
    n = streams[0][1].shape[0]
    half = (n - extra) // 2

    def body(s, *refs):
        ins, outs = refs[: 4 * len(streams)], refs[4 * len(streams) + len(through) :]
        for k in range(len(streams)):
            ka, ra, kb, rb = ins[4 * k : 4 * k + 4]
            outs[2 * k][...] = ka[...] + ra[...]
            outs[2 * k + 1][...] = kb[...] + rb[...]

    args, specs = [jnp.stack([bit for *_, bit in streams])], []
    outs, out_specs = [shape(a.shape, a.dtype) for a in through], [ANY] * len(through)
    for k, (kept, recv, place, _) in enumerate(streams):
        block = (1, *recv.shape[1:])

        def at(flip, k=k, place=place, block=block):
            def index(i, s):
                j = insert_bit(i, place, s[k] ^ flip)
                return (jnp.where(i == half, 2 * half, j) if extra else j, 0, 0)

            return pl.BlockSpec(block, index)

        args += [kept, recv, kept, recv]
        specs += [at(0), at(0), at(1), at(1)]
        outs += [shape((half + extra, *recv.shape[1:]), F32)] * 2
        out_specs += [pl.BlockSpec(block, lambda i, s: (i, 0, 0))] * 2
    size = sum(recv.size for _, recv, *_ in streams)
    return call(
        body, args, specs, outs, out_specs, cost(1.5 + size * 5e-6), "split_sum", (*through, *after), (half + extra,), 1,
        reuse=len(through),
    )


def steps(*pairs, after=(), through=()):
    args = []
    for s, name in pairs:
        args.append((s.kept, s.recv, len(s.names) - 1 - s.names.index(name), s.links[name][2]))
    outs = split_sum(args, pairs[0][0].extra, after, through)
    passed, outs = outs[: len(through)], outs[len(through) :]
    for k, (s, name) in enumerate(pairs):
        s.send(name, outs[2 * k], outs[2 * k + 1])
    return (outs[0], *passed) if through else outs[0]


class Halving:
    def __init__(self, names, links, extra=0):
        self.names, self.links, self.extra = list(names), links, extra

    def send(self, name, kept, out):
        axis, perm, _ = self.links[name]
        if name in self.names:
            self.names.remove(name)
        self.kept, self.recv = kept, lax.ppermute(out, axis, perm)
        return kept

    def step(self, name, after=()):
        return steps((self, name), after=after)

    def pair(self):
        return self.kept, self.recv


def last_sums(downs, ups, att0, att1, after=()):
    pairs = [*downs, *ups, *att0, att1]

    def body(*refs):
        ins, (qkv, out, up, down, small) = refs[: 2 * len(pairs)], refs[2 * len(pairs) :]
        total = [ins[2 * i][0] + ins[2 * i + 1][0] for i in range(len(pairs))]
        for b in range(2):
            down[b] = get_down(total[b])
            up[b] = total[2 + b]
        edge = 3 * MINE
        for b, att in enumerate((jnp.concatenate([total[4], total[5]], axis=1), total[6])):
            qkv[b] = att[:, 0:edge]
            out[b] = att[:, edge:]
        small[...] = ins[8][1] + ins[9][1]

    rows = D // 8
    return call(
        body, [a for pair in pairs for a in pair], [VM] * (2 * len(pairs)),
        [shape((2, rows, 3 * MINE), F32), shape((2, rows, MINE), F32), shape((2, rows, D), F32),
         shape((2, MINE, W_UP), F32), shape((rows, W_UP), F32)],
        [VM] * 5, cost(4), "last_sums", after,
    )


def scatter_rest(block, dim, img, sub):
    step = sub // 2
    while step:
        bit = (img // step) % 2
        half = block.shape[dim] // 2
        keep = lax.dynamic_slice_in_dim(block, bit * half, half, dim)
        send = lax.dynamic_slice_in_dim(block, (1 - bit) * half, half, dim)
        perm = [(i, i ^ step) for i in range(8 * sub)]
        block = keep + lax.ppermute(send, "img", perm)
        step //= 2
    return block


def relative_onehot():
    at = jnp.arange(TP * TQ, dtype=jnp.int32)
    u, t = at // TQ, at % TQ
    rel = (t // SIDE - u // SIDE + 6) * 13 + t % SIDE - u % SIDE + 6
    rel = jnp.where((u < T) & (t < T), rel, -1)
    return (jnp.arange(169, dtype=jnp.int32)[:, None] == rel[None, :]).astype(F32)


def region_of(coords):
    return jnp.where(coords < 7, 0, jnp.where(coords < 11, 1, 2))


def spread_bias(bias_table, onehot):
    rows = jnp.dot(
        bias_table.transpose(0, 2, 1).reshape(2 * HEADS, 169),
        onehot,
        precision=lax.Precision.HIGHEST,
        preferred_element_type=F32,
    )
    rows = rows.reshape(2, NG, PER, TP, TQ).transpose(0, 1, 3, 2, 4).reshape(2 * NG, TP, GT)
    return jnp.where((jnp.arange(TP) < T)[None, :, None], rows, NEG)


def shift_masks(core):
    places = jnp.arange(TQ, dtype=jnp.int32)
    step = jnp.arange(2, dtype=jnp.int32)
    rows = region_of(step[:, None] * SIDE + places // SIDE)
    cols = region_of((core ^ step)[:, None] * SIDE + places % SIDE)
    labels = 3 * rows[:, None] + cols[None, :]
    mask = jnp.where(labels[:, :, :TP, None] == labels[:, :, None, :], 0.0, -100.0).astype(F32)
    return jnp.tile(mask, (1, 1, 1, PER))


def per_device(
    tokens, crop_count, ln1_gain, ln1_bias, w_qkv, b_query, b_value, bias_table, w_out, b_out,
    ln2_gain, ln2_bias, w_up, b_up, w_down, b_down, cotangent, *, n_img,
):
    win, img = lax.axis_index("win"), lax.axis_index("img")
    sub = n_img // 8
    x_bit, core = win // 2, win % 2
    links = {}
    for k in range(3):
        links[k] = ("img", [(i, i ^ (sub << k)) for i in range(n_img)], (img // (sub << k)) % 2)
    bits = jnp.stack([core, links[0][2], links[1][2], links[2][2]])
    at_core, at_x = jnp.reshape(core, (1,)), jnp.reshape(x_bit, (1,))
    all_valid = jnp.full((1,), C, jnp.int32)
    p = dict(
        ln1_gain=ln1_gain, ln1_bias=ln1_bias, w_qkv=w_qkv, b_query=b_query, b_value=b_value,
        w_out=w_out, b_out=b_out, ln2_gain=ln2_gain, ln2_bias=ln2_bias, w_up=w_up, b_up=b_up,
        w_down=w_down, b_down=b_down,
    )

    def over(way, a):
        return lax.ppermute(a, "win", [(i, i ^ way) for i in range(4)])

    def swap(a):
        return over(1, a)

    onehot = relative_onehot()
    bias = spread_bias(bias_table, onehot)
    mask = shift_masks(core)

    mine, other = crop_rows(at_core, all_valid, tokens[:, 0].transpose(1, 0, 2))
    near, far = swap(other), (over(2, mine), over(3, other))
    ct_mine, ct_other = crop_rows(at_core, crop_count, cotangent[:, 0].transpose(1, 0, 2), (mine,))
    ct_near, ct_far = swap(ct_other), (over(2, ct_mine), over(3, ct_other))
    fwd0 = block_fwd(0, (at_x, mine, near), bias, p, 0, (ct_mine,))
    fwd0 = block_fwd(0, (at_x, *far), bias, p, 1, fwd0)
    fwd1 = block_fwd(1, (fwd0[8], mask), bias, p)
    z0, h0, qkvc0, o0, y0, h20, g0, gp0, _ = fwd0
    z1, h1, qkvc1, o1, y1, h21, g1, gp1, zn = fwd1
    ct = join_pieces(at_x, (ct_mine, ct_near, *ct_far), (zn,))

    def stream(first, extra=0):
        return Halving([k for k in (2, 1, 0) if k != first], links, extra)

    down1, up1, att1, down0, up0 = (stream(k) for k in (0, 1, 0, 0, 1))
    att0 = [stream(0, 1), stream(1)]

    dd1, da1, dy, dyr, sv_m1, *part = mlp_back(1, at_x, at_core, ct, y1, gp1, g1, h21, p)
    down_x, up_x = (swap(a) for a in part)
    r31, sv_a1, table1, grad1, *part = attn_back(
        1, at_x, at_core, dyr, qkvc1, dy, z1, h1, o1, mask, bias, p, (), (part[0],)
    )
    att_x = [swap(a) for a in part]
    last = down1.send(0, *down_mine(bits, dd1, g1, down_x, 0, (sv_a1,)))
    last = up1.send(1, *up_mine(bits, h21, da1, up_x, 1, (last,)))

    dd0, da0, dy, dyr, sv_m0, *part = mlp_back(0, at_x, at_core, grad1, y0, gp0, g0, h20, p, (last, *att_x))
    last, *part = steps((down1, 1), (up1, 0), after=(sv_m0,), through=part)
    down_x, up_x = (swap(a) for a in part)
    last = att1.send(0, *attn_mine(bits, h1, o1, r31, att_x, 0, (0, 1), None, (last,)))
    out_mine, out_other = own_quadrants(at_x, zn, True, (last,))
    out_x = swap(out_other)
    last = down0.send(0, *down_mine(bits, dd0, g0, down_x, 0, (out_mine,)))
    last = up0.send(1, *up_mine(bits, h20, da0, up_x, 1, (last,)))
    last = steps((down1, 2), (up1, 2), after=(last,))
    r30, sv_a0, small, grad0, *part = attn_back(
        0, at_x, at_core, dyr, qkvc0, dy, z0, h0, o0, mask, bias, p, (sv_m0, sv_a1, sv_m1, table1), (last,)
    )
    last, small, *part = steps(
        (up0, 0), (down0, 1), (att1, 1), after=(sv_a0, down1.recv, up1.recv), through=(small, *part)
    )
    att_x = [swap(a) for a in part]
    small = [small, swap(small)]
    block_out = token_major(at_core, crop_count, out_mine, out_x, (last,))
    in_mine, in_other = own_quadrants(at_x, grad0, False, (block_out,))
    in_x = swap(in_other)
    last = in_mine
    for k in range(2):
        kept, out = attn_mine(bits, h0, o0, r30, att_x, k, (k,), None if k else small, (last,))
        last = att0[k].send(k, kept, out)
    last = steps((up0, 2), (down0, 2), (att1, 2), after=(last,))
    last = att0[0].step(1, (last, up0.recv))
    last = att0[1].step(0, (last, down0.recv))
    last = att0[0].step(2, (last,))
    last = att0[1].step(2, (last,))
    grad_tokens = crop_major(at_core, in_mine, in_x, (last,))

    g_qkv, g_out, g_up, g_down, small = last_sums(
        (down0.pair(), down1.pair()), (up0.pair(), up1.pair()), [a.pair() for a in att0], att1.pair(), (grad_tokens,)
    )
    for k in range(sub.bit_length() - 1):
        small = small + lax.ppermute(small, "img", [(i, i ^ (1 << k)) for i in range(n_img)])
    g_qkv, g_out, g_up = (scatter_rest(g, 1, img, sub) for g in (g_qkv, g_out, g_up))
    g_down = scatter_rest(g_down, 2, img, sub).transpose(0, 2, 1)
    table = small[48:, :169].reshape(2, PER, NG, 169).transpose(0, 3, 2, 1).reshape(2, 169, HEADS)
    width = D // n_img

    vectors = jnp.concatenate([small[:24], small[24:48]], axis=1).reshape(2, 12, D)
    mine = lax.dynamic_slice_in_dim(vectors[:, :8], img * width, width, 2)
    up_bias = lax.dynamic_slice_in_dim(vectors[:, 8:].reshape(2, FF), img * (4 * width), 4 * width, 1)

    return (
        block_out.transpose(1, 0, 2)[:, None], grad_tokens.reshape(C, 1, T, D), mine[:, 0], mine[:, 1], g_qkv, mine[:, 2], mine[:, 3], table,
        g_out, mine[:, 6], mine[:, 4], mine[:, 5], g_up, up_bias, g_down, mine[:, 7],
    )


def solution(mesh):
    shard = P("img", "win", None, None)
    vec, mat = P(None, "img"), P(None, "img", "win")
    return jax.shard_map(
        functools.partial(per_device, n_img=mesh.shape["img"]),
        mesh=mesh,
        in_specs=(shard, P("img")) + (P(),) * 14 + (shard,),
        out_specs=(shard, shard, vec, vec, mat, vec, vec, P(), mat, vec, vec, vec, mat, vec, mat, vec),
        check_vma=False,
    )
```

```python
import functools

import jax
import jax.numpy as jnp
from jax import lax
from jax.experimental import pallas as pl
from jax.experimental.pallas import tpu as pltpu
from jax.sharding import PartitionSpec as P

HEADS = 24
HD = 32
SIDE = 7
T = SIDE * SIDE
TP = 56
TQ = 64
D = 768
FF = 3072
C = 8
ROWS = T * C
PAD_ROWS = TQ * C
HALF = C // 2
PIECE = T * HALF
LANE = 128
NG = D // LANE
PER = LANE // HD
GT = PER * TQ
EPSILON = 1e-05
SCALE = HD ** (-0.5)
NEG = -1e30
QCH = 768
FCH = 1536
WIN = 2
N_Q = 3 * D // QCH
N_F = FF // FCH
W_UP = D // 2
MINE = D // 4
VMEM_LIMIT = 44 << 20
VMEM_SMALL = 24 << 20
BIG = ("forw", "mlp_", "attn")
COST = 0.4
F32 = jnp.float32
BF16 = jnp.bfloat16

TAIL_K = 0.3
TAIL = (
    0.11963200491345692,
    0.12071217642148169,
    0.10017566554041868,
    0.12769280877164998,
    -0.052036176065482394,
    0.20455934198696718,
    -0.15616004916725648,
    0.035424145900813254,
)
INV_SQRT_2PI = 0.3989422804014327

def nt(left, right):
    return lax.dot_general(left, right, (((1,), (1,)), ((), ())), preferred_element_type=F32)


def tn(left, right):
    return lax.dot_general(left, right, (((0,), (0,)), ((), ())), preferred_element_type=F32)


def nn(left, right):
    return jnp.dot(left, right, preferred_element_type=F32)


def norm_parts(values):
    average = jnp.mean(values, axis=-1, keepdims=True)
    centered = values - average
    inverse = lax.rsqrt(jnp.mean(centered * centered, axis=-1, keepdims=True) + EPSILON)
    return centered * inverse, inverse


def norm_back(grad_out, normed, inverse, gain):
    scaled = grad_out * gain
    return inverse * (
        scaled
        - jnp.mean(scaled, axis=-1, keepdims=True)
        - normed * jnp.mean(scaled * normed, axis=-1, keepdims=True)
    )


def gelu_parts(a):
    bell = jnp.exp(-0.5 * a * a)
    size = jnp.abs(a)
    t = 1.0 / (1.0 + TAIL_K * size)
    poly = jnp.full_like(t, TAIL[-1])
    for coef in TAIL[-2::-1]:
        poly = poly * t + coef
    tail = bell * (t * poly)
    phi = jnp.where(a < 0, tail, 1.0 - tail)
    return a * phi, phi + a * (INV_SQRT_2PI * bell)


def head_masks(rows):
    lanes = lax.broadcasted_iota(jnp.int32, (rows, LANE), 1)
    return [(lanes >= HD * h) & (lanes < HD * (h + 1)) for h in range(PER)]


def spread(values, ones):
    return jnp.concatenate([values * m for m in ones], axis=0)


def gather_heads(stacked, masks):
    out = stacked[(PER - 1) * TQ : (PER - 1) * TQ + TP]
    for h in range(PER - 2, -1, -1):
        out = jnp.where(masks[h], stacked[h * TQ : h * TQ + TP], out)
    return out


def soft(scores):
    e = jnp.exp(scores - jnp.max(scores, axis=0, keepdims=True))
    return e * (1.0 / jnp.sum(e, axis=0, keepdims=True))


def colsum(values):
    return jnp.sum(values, axis=0, keepdims=True)


def rows_of(w, n=T, stride=C):
    return pl.ds(w, n, stride=stride)


def lanes_at(n, width):
    return pl.ds(pl.multiple_of(n * width, width), width)


def put_rolled(dest, source, a, back):
    shift, kept = (-3, range(3, 7)) if back else (3, range(0, 4))
    for i in range(SIDE):
        for j in range(SIDE):
            half = a if i in kept else 1 - a
            tile = source[half, SIDE * ((i + shift) % SIDE) + (j + shift) % SIDE]
            if j not in kept:
                tile = pltpu.roll(tile, HALF, 0)
            t = SIDE * i + j
            dest[C * t : C * (t + 1), :] = tile


ANY = pl.BlockSpec(memory_space=pl.ANY)
VM = pl.BlockSpec(memory_space=pltpu.VMEM)
SM = pl.BlockSpec(memory_space=pltpu.SMEM)


def cost(micros):
    return pl.CostEstimate(flops=int(micros * COST * 1.15e9), bytes_accessed=0, transcendentals=0)


def shape(dims, dtype):
    return jax.ShapeDtypeStruct(dims, dtype)


def fixed(dims, single=False):
    mode = dict(pipeline_mode=pl.Buffered(1)) if single else {}
    return pl.BlockSpec(dims, lambda *_: (0,) * len(dims), **mode)


def per_half(dims):
    return pl.BlockSpec((1, *dims), lambda a, *_: (a, *(0,) * len(dims)))


def call(body, args, in_specs, outs, out_specs, estimate, name, after=(), grid=(), scalars=0, scratch=(), reuse=0):
    n_in, n_after = len(args), len(after)

    def wrapped(*refs):
        return body(*refs[:n_in], *refs[n_in + n_after :])

    return pl.pallas_call(
        wrapped,
        grid_spec=pltpu.PrefetchScalarGridSpec(
            num_scalar_prefetch=scalars,
            grid=grid,
            in_specs=list(in_specs) + [ANY] * n_after,
            out_specs=out_specs,
            scratch_shapes=list(scratch),
        ),
        out_shape=outs,
        input_output_aliases={n_in + k: k for k in range(reuse)},
        compiler_params=pltpu.CompilerParams(vmem_limit_bytes=VMEM_LIMIT if name[:4] in BIG else VMEM_SMALL),
        cost_estimate=estimate,
        name=name,
    )(*args, *after)


def crop_rows(core, count, crops, after=()):
    def body(at, n, src, mine, other, s):
        wide = src[...].astype(F32).reshape(ROWS, D)
        for g in range(NG):
            s[g] = wide[:, LANE * g : LANE * (g + 1)]
        for k in range(HALF):
            for out, c in ((mine, at[0]), (other, 1 - at[0])):
                crop = HALF * c + k
                keep = jnp.where(crop < n[0], 1.0, 0.0).astype(F32)
                for g in range(NG):
                    out[g, rows_of(k, stride=HALF), :] = s[g, rows_of(crop), :] * keep

    return call(
        body, (core, count, crops), [SM, SM, VM], [shape((NG, PIECE, LANE), F32)] * 2, [VM] * 2, cost(2.5), "crop_rows", after, scratch=[pltpu.VMEM((NG, ROWS, LANE), F32)],
    )


def weave(dest, pieces):
    for b, piece in enumerate(pieces):
        for k in range(HALF):
            for g in range(NG):
                dest[g, rows_of(HALF * b + k), :] = piece[g, rows_of(k, stride=HALF), :]


def join_pieces(x_at, pieces, after=()):
    def body(x, *refs):
        *src, out, s = refs
        for k in range(2):
            weave(s, src[2 * k : 2 * k + 2])
            for g in range(NG):
                out[x[0] ^ k, :, :, LANE * g : LANE * (g + 1)] = s[g].reshape(T, C, LANE)

    return call(
        body, (x_at, *pieces), [SM] + [VM] * 4, shape((2, T, C, D), F32), VM, cost(4), "join_pieces", after,
        scratch=[pltpu.VMEM((NG, ROWS, LANE), F32)],
    )


def own_quadrants(x_at, both_halves, rolled, after=()):
    def body(x, src, mine, other, full, s):
        if rolled:
            put_rolled(full, src, x[0], True)
        else:
            full[...] = src[x[0]].reshape(ROWS, D)
        for g in range(NG):
            s[g] = full[:, LANE * g : LANE * (g + 1)]
        for b, out in enumerate((mine, other)):
            for k in range(HALF):
                for g in range(NG):
                    out[g, rows_of(k, stride=HALF), :] = s[g, rows_of(HALF * b + k), :]

    return call(
        body, (x_at, both_halves), [SM, VM], [shape((NG, PIECE, LANE), F32)] * 2, [VM] * 2, cost(3), "own_quadrants", after, scratch=[pltpu.VMEM((ROWS, D), F32), pltpu.VMEM((NG, ROWS, LANE), F32)],
    )


def token_major(core, count, mine, theirs, after=()):
    def body(at, n, a, b, out, s):
        for k in range(HALF):
            for src, c in ((a, at[0]), (b, 1 - at[0])):
                crop = HALF * c + k
                keep = jnp.where(crop < n[0], 1.0, 0.0).astype(F32)
                for g in range(NG):
                    s[g, rows_of(crop), :] = src[g, rows_of(k, stride=HALF), :] * keep
        for g in range(NG):
            out[:, :, LANE * g : LANE * (g + 1)] = s[g].reshape(T, C, LANE).astype(BF16)

    return call(
        body, (core, count, mine, theirs), [SM, SM, VM, VM], shape((T, C, D), BF16), VM, cost(2.5), "token_major", after, scratch=[pltpu.VMEM((NG, ROWS, LANE), F32)],
    )


def crop_major(core, mine, theirs, after=()):
    def body(at, a, b, out):
        for k in range(HALF):
            for src, c in ((a, at[0]), (b, 1 - at[0])):
                for g in range(NG):
                    out[pl.ds((HALF * c + k) * (T * NG) + g, T, stride=NG), :] = src[g, rows_of(k, stride=HALF), :]

    return call(
        body, (core, mine, theirs), [SM, VM, VM], shape((C * T * NG, LANE), F32), VM, cost(2.5), "crop_major", after,
    )


def fwd_body(b, which, *refs):
    a = pl.program_id(0)
    if b == 0:
        at_x, p0, p1, *rest = refs
    else:
        core, src, *rest = refs
    (
        bias, ln1g, ln1b, bq, bv, bout, ln2g, ln2b, bup, bdown,
        wqkv_h, wout_h, wup_h, wdown_h,
        z_h, h_h, qkvc_h, o_h, y_h, h2_h, g_h, gp_h, zn_o,
        wqkv, wout, wup, wdown, qkv_s, o_s, bqkv, bias_s,
        z_o, h_o, qkvc_o, o_o, y_o, h2_o, g_o, gp_o, sem_q, sem_o, sem_u, sem_d, sem_out,
    ) = rest
    at = at_x[0] ^ which if b == 0 else a
    results = (
        (z_o, z_h), (h_o, h_h), (qkvc_o, qkvc_h), (o_o, o_h), (y_o, y_h), (h2_o, h2_h), (g_o, g_h), (gp_o, gp_h),
    )

    def out(k):
        return pltpu.make_async_copy(results[k][0].at[0], results[k][1].at[at], sem_out.at[k])

    def free(k):
        @pl.when(a > 0)
        def _():
            out(k).wait()

    def cp_q(n):
        return pltpu.make_async_copy(
            wqkv_h.at[b, :, lanes_at(n, QCH)], wqkv.at[:, lanes_at(n, QCH)], sem_q.at[n]
        )

    def cp_u(n):
        return pltpu.make_async_copy(
            wup_h.at[b, :, lanes_at(n, FCH)], wup.at[:, lanes_at(n, FCH)], sem_u.at[n]
        )

    def cp_d(n):
        return pltpu.make_async_copy(
            wdown_h.at[b, lanes_at(n, FCH), :], wdown.at[lanes_at(n, FCH), :], sem_d.at[n]
        )

    cp_o = pltpu.make_async_copy(wout_h.at[b], wout, sem_o)

    def wait(copy):
        @pl.when(a == 0)
        def _():
            copy.wait()

    @pl.when(a == 0)
    def _():
        for n in range(N_Q):
            cp_q(n).start()
        cp_o.start()
        for n in range(N_F):
            cp_u(n).start()
            cp_d(n).start()
        bqkv[:, 0:D] = bq[b : b + 1, :]
        bqkv[:, D : 2 * D] = jnp.zeros((1, D), F32)
        bqkv[:, 2 * D :] = bv[b : b + 1, :]
        qkv_s[:, ROWS:, :] = jnp.zeros((3 * NG, PAD_ROWS - ROWS, LANE), F32)

    free(0)
    if b == 0:
        weave(o_s, (p0, p1))
        for g in range(NG):
            z_o[0, :, LANE * g : LANE * (g + 1)] = o_s[g, 0:ROWS, :]
    else:
        put_rolled(z_o.at[0], src, a, False)
        for w in range(2):
            mask = shift_mask(a, core[0] ^ w)
            for g in range(NG):
                bias_s[w * NG + g] = bias[NG + g] + mask
    out(0).start()
    normed, _ = norm_parts(z_o[0])
    free(1)
    h_o[0] = (normed * ln1g[b : b + 1, :] + ln1b[b : b + 1, :]).astype(BF16)
    out(1).start()

    def qkv_step(n, _):
        wait(cp_q(n))
        joint = nn(h_o[0], wqkv[:, lanes_at(n, QCH)]) + bqkv[:, lanes_at(n, QCH)]
        joint = joint * jnp.where(n < D // QCH, SCALE, 1.0)
        joint = joint.astype(BF16).astype(F32)
        for k in range(QCH // LANE):
            qkv_s[n * (QCH // LANE) + k, 0:ROWS, :] = joint[:, LANE * k : LANE * (k + 1)]
        return 0

    lax.fori_loop(0, N_Q, qkv_step, 0)
    masks = head_masks(TP)
    ones = [m.astype(F32).astype(BF16) for m in head_masks(TQ)]

    def attend(step, _):
        items = [(step * WIN + i, g) for i in range(WIN) for g in range(NG)]
        qs = [qkv_s[g, rows_of(w, TQ), :].astype(BF16) for w, g in items]
        ks = [qkv_s[NG + g, rows_of(w, TP), :].astype(BF16) for w, g in items]
        vs = [qkv_s[2 * NG + g, rows_of(w, TP), :].astype(BF16) for w, g in items]
        for (w, g), q, k, v in zip(items, qs, ks, vs):
            qkvc_o[0, w, g] = q
            qkvc_o[0, w, NG + g, 0:TP] = k
            qkvc_o[0, w, 2 * NG + g, 0:TP] = v
        added = [bias[g] if b == 0 else bias_s[w // HALF * NG + g] for w, g in items]
        scores = [nt(k, spread(q, ones)) + extra for k, q, extra in zip(ks, qs, added)]
        probs = [soft(score).astype(BF16) for score in scores]
        for (w, g), prob, v in zip(items, probs, vs):
            o_s[g, rows_of(w, TP), :] = gather_heads(tn(prob, v), masks)
        return 0

    free(2)
    lax.fori_loop(0, C // WIN, attend, 0, unroll=2)
    out(2).start()
    free(3)
    for g in range(NG):
        o_o[0, :, LANE * g : LANE * (g + 1)] = o_s[g, 0:ROWS, :].astype(BF16)
    out(3).start()
    wait(cp_o)
    free(4)
    y_o[0] = z_o[0] + (nn(o_o[0], wout[...]) + bout[b : b + 1, :])
    out(4).start()
    normed, _ = norm_parts(y_o[0])
    free(5)
    h2_o[0] = (normed * ln2g[b : b + 1, :] + ln2b[b : b + 1, :]).astype(BF16)
    out(5).start()
    free(6)
    free(7)
    def mlp_step(n, _):
        wait(cp_u(n))
        up = nn(h2_o[0], wup[:, lanes_at(n, FCH)]) + bup[b : b + 1, lanes_at(n, FCH)]
        act, slope = gelu_parts(up)
        g_o[0, :, lanes_at(n, FCH)] = act.astype(BF16)
        gp_o[0, :, lanes_at(n, FCH)] = slope.astype(BF16)
        return 0

    lax.fori_loop(0, N_F, mlp_step, 0)
    out(6).start()
    out(7).start()
    for n in range(N_F):
        wait(cp_d(n))
    zn_o[0] = (y_o[0] + (nn(g_o[0], wdown[...]) + bdown[b : b + 1, :])).reshape(T, C, D)

    @pl.when(a == pl.num_programs(0) - 1)
    def _():
        for k in range(len(results)):
            out(k).wait()


def block_fwd(b, sources, bias, p, which=None, after=()):
    outs = [
        shape((2, ROWS, D), F32),
        shape((2, ROWS, D), BF16),
        shape((2, C, 3 * NG, TQ, LANE), BF16),
        shape((2, ROWS, D), BF16),
        shape((2, ROWS, D), F32),
        shape((2, ROWS, D), BF16),
        shape((2, ROWS, FF), BF16),
        shape((2, ROWS, FF), BF16),
        shape((2, T, C, D), F32),
    ]
    if b == 0:
        specs = [fixed((NG, PIECE, LANE), True)] * 2
        out_specs = [pl.BlockSpec((1, T, C, D), lambda a, s: (s[0] ^ which, 0, 0, 0))]
    else:
        specs = [SM, fixed((2, T, C, D), True)]
        out_specs = [per_half((T, C, D))]
    small = (bias, p["ln1_gain"], p["ln1_bias"], p["b_query"], p["b_value"], p["b_out"],
             p["ln2_gain"], p["ln2_bias"], p["b_up"], p["b_down"])
    big = (p["w_qkv"], p["w_out"], p["w_up"], p["w_down"])
    return call(
        functools.partial(fwd_body, b, which),
        (*sources, *small, *big),
        specs + [fixed(v.shape, True) for v in small] + [ANY] * 4,
        outs,
        [ANY] * 8 + out_specs,
        cost(21 if which is not None else 36),
        f"forward_{b}",
        after,
        grid=(2 if which is None else 1,),
        scalars=int(which is not None),
        reuse=len(outs) if which == 1 else 0,
        scratch=[
            pltpu.VMEM((D, 3 * D), BF16),
            pltpu.VMEM((D, D), BF16),
            pltpu.VMEM((D, FF), BF16),
            pltpu.VMEM((FF, D), BF16),
            pltpu.VMEM((3 * NG, PAD_ROWS, LANE), F32),
            pltpu.VMEM((NG, PAD_ROWS, LANE), F32),
            pltpu.VMEM((1, 3 * D), F32),
            pltpu.VMEM((2 * NG, TP, GT), F32),
            *(pltpu.VMEM((1, *o.shape[1:]), o.dtype) for o in outs[:8]),
            pltpu.SemaphoreType.DMA((N_Q,)),
            pltpu.SemaphoreType.DMA,
            pltpu.SemaphoreType.DMA((N_F,)),
            pltpu.SemaphoreType.DMA((N_F,)),
            pltpu.SemaphoreType.DMA((8,)),
        ],
    )


def mlp_back_body(b, x_at, core, src, y, gp, act, hid, ln2g, wdown_h, wup_h, dd_o, da_o, dy_o, sv_o, down_o, up_o,
                  wdown, wup, dz, dd, da_s, sem_d, sem_u):
    a = pl.program_id(0)

    def cp_u(n):
        return pltpu.make_async_copy(
            wup_h.at[b, :, lanes_at(n, D)], wup.at[:, lanes_at(n, D)], sem_u.at[n]
        )

    def cp_d(n):
        return pltpu.make_async_copy(
            wdown_h.at[b, lanes_at(n, D), :], wdown.at[lanes_at(n, D), :], sem_d.at[n]
        )

    def wait(copy):
        @pl.when(a == 0)
        def _():
            copy.wait()

    @pl.when(a == 0)
    def _():
        for n in range(4):
            cp_d(n).start()
            cp_u(n).start()
        sv_o[...] = jnp.zeros_like(sv_o)

    put_rolled(dz, src, a, b == 0)
    low = dz[...].astype(BF16)
    dd[...] = low
    sv_o[3:4, :] += colsum(low.astype(F32))
    for x in range(2):

        @pl.when(x_at[0] == x)
        def _():
            for c in range(2):
                w = 2 * x + c
                dd_o[c, 0] = dd[:, MINE * w : MINE * (w + 1)]

    def step(n, _):
        wait(cp_d(n))
        grad_act = nt(dd[...], wdown[lanes_at(n, D), :])
        da = (grad_act * gp[0, :, lanes_at(n, D)].astype(F32)).astype(BF16)

        da_s[:, lanes_at(n, D)] = da

        @pl.when(n // 2 == x_at[0])
        def _():
            da_o[0, :, lanes_at(n % 2, D)] = da

        sv_o[pl.ds(4 + n, 1), :] += colsum(da.astype(F32))
        return 0

    lax.fori_loop(0, 4, step, 0)
    for n in range(4):
        wait(cp_u(n))
    dh2 = nt(da_s[...], wup[...])
    normed, inverse = norm_parts(y[0])
    sv_o[0:1, :] += colsum(dh2 * normed)
    sv_o[1:2, :] += colsum(dh2)
    dy = dz[...] + norm_back(dh2, normed, inverse, ln2g[b : b + 1, :])
    dy_o[0] = dy
    sv_o[2:3, :] += colsum(dy.astype(BF16).astype(F32))
    down = tn(dd_o[1 - core[0], 0], act[0])
    up = tn(hid[0], da_o[0, :, lanes_at(1 - core[0], D)])

    def put(add):
        for k in range(8):
            add_down(down_o, k, down[:, W_UP * k : W_UP * (k + 1)], add)
            rows = up[D // 8 * k : D // 8 * (k + 1)]
            up_o[k] = up_o[k] + rows if add else rows

    for half in range(2):
        pl.when(a == half)(functools.partial(put, half == 1))


def mlp_back(b, x_at, core, src, y, gp, act, hid, p, after=()):
    return call(
        functools.partial(mlp_back_body, b),
        (x_at, core, src, y, gp, act, hid, p["ln2_gain"], p["w_down"], p["w_up"]),
        [SM, SM, fixed((2, T, C, D), True), per_half((ROWS, D)), per_half((ROWS, FF)), per_half((ROWS, FF)),
         per_half((ROWS, D)), fixed((2, D)), ANY, ANY],
        [
            shape((2, 2, ROWS, MINE), BF16),
            shape((2, ROWS, FF // 2), BF16),
            shape((2, ROWS, D), F32),
            shape((8, D), F32),
            shape((8, *BLOCK), F32),
            shape((8, *BLOCK), F32),
        ],
        [
            pl.BlockSpec((2, 1, ROWS, MINE), lambda a: (0, a, 0, 0)),
            per_half((ROWS, FF // 2)),
            per_half((ROWS, D)),
            fixed((8, D)),
            fixed((8, *BLOCK), True),
            fixed((8, *BLOCK), True),
        ],
        cost(22),
        f"mlp_back_{b}",
        after,
        grid=(2,),
        scratch=[
            pltpu.VMEM((FF, D), BF16),
            pltpu.VMEM((D, FF), BF16),
            pltpu.VMEM((ROWS, D), F32),
            pltpu.VMEM((ROWS, D), BF16),
            pltpu.VMEM((ROWS, FF), BF16),
            pltpu.SemaphoreType.DMA((4,)),
            pltpu.SemaphoreType.DMA((4,)),
        ],
    )


TABLE = 256
BLOCK = (D // 8, D)


def row_of(t):
    return sum((t >= SIDE * k).astype(jnp.int32) for k in range(1, 10))


def shift_mask(a, column):
    u = lax.broadcasted_iota(jnp.int32, (TP, GT), 0)
    t = lax.broadcasted_iota(jnp.int32, (TP, GT), 1) & (TQ - 1)
    iu, it = row_of(u), row_of(t)
    rows = (iu >= 4) != (it >= 4)
    cols = (u - SIDE * iu >= 4) != (t - SIDE * it >= 4)
    return jnp.where((rows & (a == 1)) | (cols & (column == 1)), -100.0, 0.0)


def table_sums(ds, moved):
    row = lax.broadcasted_iota(jnp.int32, (GT, PER * LANE), 0)
    col = lax.broadcasted_iota(jnp.int32, (GT, PER * LANE), 1)
    t = row & (TQ - 1)
    there = (row >> 6 == col >> 7) & (t < T) & ((col & (LANE - 1)) == t + 6 * row_of(t))
    onehot = there.astype(F32).astype(BF16)
    moved[:, NG * TP :, :] = jnp.zeros((PER, (8 - NG) * TP, LANE), F32)
    for g in range(NG):
        rest = ds[g]
        total = jnp.zeros((TP, PER * LANE), F32)
        for _ in range(3):
            part = rest.astype(BF16)
            total += nn(part, onehot)
            rest = rest - part.astype(F32)
        for h in range(PER):
            moved[h, TP * g : TP * (g + 1), :] = total[:, LANE * h : LANE * (h + 1)]


def sum_table(moved, put):
    for h in range(PER):
        total = jnp.zeros((8, TABLE), F32)
        for u in range(T):
            v = moved[h, pl.ds(u, 8, stride=TP), :]
            shift = 13 * (6 - u // SIDE) + 6 - u % SIDE
            total += pltpu.roll(jnp.concatenate([v, jnp.zeros_like(v)], axis=1), shift, 1)
        put(h, total)


def attn_back_body(b, x_at, core, dy, qkvc, z, hid, att, *refs):
    bias, ln1g, *refs = refs
    if b == 0:
        sv_m0, sv_a1, sv_m1, table1, *refs = refs
    (wout_h, wqkv_h, r3_o, sv_o, sum_o, grad_o, *part_o,
     wout, wqkv, do_s, dqkv_s, dq, bias_s, ds_o, moved, dyr, sem_o, sem_q) = refs
    a = pl.program_id(0)
    cp_o = pltpu.make_async_copy(wout_h.at[b], wout, sem_o)

    def cp_q(n):
        return pltpu.make_async_copy(
            wqkv_h.at[b, :, lanes_at(n, QCH)], wqkv.at[:, lanes_at(n, QCH)], sem_q.at[n]
        )

    def wait(copy):
        @pl.when(a == 0)
        def _():
            copy.wait()

    @pl.when(a == 0)
    def _():
        cp_o.start()
        for n in range(N_Q):
            cp_q(n).start()
        do_s[:, ROWS:, :] = jnp.zeros((NG, PAD_ROWS - ROWS, LANE), F32)
        ds_o[...] = jnp.zeros_like(ds_o)
        sv_o[...] = jnp.zeros_like(sv_o)

    if b == 1:
        for w in range(2):
            mask = shift_mask(a, core[0] ^ w)
            for g in range(NG):
                bias_s[w * NG + g] = bias[NG + g] + mask
    dyr[...] = dy[0].astype(BF16)
    wait(cp_o)
    do = nt(dyr[...], wout[...]).astype(BF16).astype(F32)
    for g in range(NG):
        do_s[g, 0:ROWS, :] = do[:, LANE * g : LANE * (g + 1)]
    masks = head_masks(TP)
    ones = [m.astype(F32).astype(BF16) for m in head_masks(TQ)]

    def attend(step, _):
        items = [(step * WIN + i, g) for i in range(WIN) for g in range(NG)]
        ks = [qkvc[0, w, NG + g, 0:TP] for w, g in items]
        q_wide = [spread(qkvc[0, w, g], ones) for w, g in items]
        do_wide = [spread(do_s[g, rows_of(w, TQ), :].astype(BF16), ones) for w, g in items]
        added = [bias[g] if b == 0 else bias_s[w // HALF * NG + g] for w, g in items]
        scores = [nt(k, q) + extra for k, q, extra in zip(ks, q_wide, added)]
        dprobs = [nt(qkvc[0, w, 2 * NG + g, 0:TP], d) for (w, g), d in zip(items, do_wide)]
        probs = [soft(score) for score in scores]
        weighted = [p * d for p, d in zip(probs, dprobs)]
        ds = [x - p * jnp.sum(x, axis=0, keepdims=True) for x, p in zip(weighted, probs)]
        for (w, g), d in zip(items, ds):
            ds_o[g] += d
        low = [d.astype(BF16) for d in ds]
        dks = [nn(x, q) for x, q in zip(low, q_wide)]
        dvs = [nn(p.astype(BF16), d) for p, d in zip(probs, do_wide)]
        dqs = [tn(x, k) for x, k in zip(low, ks)]
        for (w, g), d_q, d_k, d_v in zip(items, dqs, dks, dvs):
            dqkv_s[g, rows_of(w, TP), :] = gather_heads(d_q, masks) * SCALE
            dqkv_s[NG + g, rows_of(w, TP), :] = d_k
            dqkv_s[2 * NG + g, rows_of(w, TP), :] = d_v
        return 0

    lax.fori_loop(0, C // WIN, attend, 0)
    for g in range(3 * NG):
        dq[:, LANE * g : LANE * (g + 1)] = dqkv_s[g, 0:ROWS, :].astype(BF16)
    sv_o[2:3, :] += colsum(dq[:, 0:D].astype(F32))
    sv_o[3:4, :] += colsum(dq[:, 2 * D :].astype(F32))
    for n in range(N_Q):
        wait(cp_q(n))
    dh = nt(dq[...], wqkv[...])
    for x in range(2):

        @pl.when(x_at[0] == x)
        def _():
            for c in range(2):
                w = 2 * x + c
                r3_o[c, 0] = jnp.concatenate(
                    [dq[:, 3 * MINE * w : 3 * MINE * (w + 1)], dyr[:, MINE * w : MINE * (w + 1)]], axis=1
                )

    normed, inverse = norm_parts(z[0])
    sv_o[0:1, :] += colsum(dh * normed)
    sv_o[1:2, :] += colsum(dh)
    grad_o[0] = (dy[0] + norm_back(dh, normed, inverse, ln1g[b : b + 1, :])).reshape(T, C, D)
    other = r3_o[1 - core[0], 0]
    parts = [attn_columns(tn, hid[0], att[0], other[:, W_UP * n : W_UP * (n + 1)], W_UP * n, W_UP) for n in range(2)]

    def put_parts(add):
        for out, part in zip(part_o, parts):
            blocks = part.reshape(8, D // 8, W_UP)
            out[...] = out[...] + blocks if add else blocks

    for half in range(2):
        pl.when(a == half)(functools.partial(put_parts, half == 1))

    @pl.when(a == 1)
    def _():
        table_sums(ds_o, moved)
        if b == 1:
            sum_table(moved, lambda h, v: sum_o.__setitem__(h, v))
            return
        sum_o[...] = jnp.zeros_like(sum_o)
        for at, ref in ((0, sv_o), (4, sv_m0), (12, sv_a1), (16, sv_m1)):
            for k in range(2):
                sum_o[24 * k + at : 24 * k + at + ref.shape[0], :] = ref[:, W_UP * k : W_UP * (k + 1)]

        def put(h, v, at=48):
            sum_o[at + NG * h : at + NG * (h + 1), 0:TABLE] = v[0:NG]

        sum_table(moved, put)
        for h in range(PER):
            put(h, table1[h], 72)


def attn_back(b, x_at, core, dy, qkvc, z, hid, att, bias, p, sums=(), after=()):
    sum_shape = (PER, 8, TABLE) if b else (D // 8, W_UP)
    return call(
        functools.partial(attn_back_body, b),
        (x_at, core, dy, qkvc, z, hid, att, bias, p["ln1_gain"], *sums, p["w_out"], p["w_qkv"]),
        [SM, SM, per_half((ROWS, D)), per_half((C, 3 * NG, TQ, LANE))] + [per_half((ROWS, D))] * 3
        + [fixed(bias.shape, True), fixed((2, D)), *(fixed(v.shape) for v in sums), ANY, ANY],
        [shape((2, 2, ROWS, D), BF16), shape((4, D), F32), shape(sum_shape, F32), shape((2, T, C, D), F32)]
        + [shape((8, D // 8, W_UP), F32)] * 2,
        [
            pl.BlockSpec((2, 1, ROWS, D), lambda a: (0, a, 0, 0)),
            fixed((4, D)),
            fixed(sum_shape),
            per_half((T, C, D)),
        ]
        + [fixed((8, D // 8, W_UP), True)] * 2,
        cost(31),
        f"attn_back_{b}",
        after,
        grid=(2,),
        scratch=[
            pltpu.VMEM((D, D), BF16),
            pltpu.VMEM((D, 3 * D), BF16),
            pltpu.VMEM((NG, PAD_ROWS, LANE), F32),
            pltpu.VMEM((3 * NG, PAD_ROWS, LANE), F32),
            pltpu.VMEM((ROWS, 3 * D), BF16),
            pltpu.VMEM((2 * NG, TP, GT), F32),
            pltpu.VMEM((NG, TP, GT), F32),
            pltpu.VMEM((PER, 8 * TP, LANE), F32),
            pltpu.VMEM((ROWS, D), BF16),
            pltpu.SemaphoreType.DMA,
            pltpu.SemaphoreType.DMA((N_Q,)),
        ],
    )


def halves(left, right):
    return tn(left(0), right(0)) + tn(left(1), right(1))


def insert_bit(i, place, bit):
    return ((i >> place) << (place + 1)) | (bit << place) | (i & ((1 << place) - 1))


def row_pairs(values, k):
    height = values.shape[0] // 8
    for i in range(4):
        low = insert_bit(i, k, 0)
        high = low | (1 << k)
        yield i, low, high, values[height * low : height * (low + 1)], values[height * high : height * (high + 1)]


def put_down(out, i, total):
    half = MINE // 2
    out[i, :, 0:W_UP] = total[0:half]
    out[i, :, W_UP:] = total[half:]


def add_down(out, i, total, add):
    put_down(out, i, total + get_down(out[i]) if add else total)


def get_down(block):
    return jnp.concatenate([block[:, 0:W_UP], block[:, W_UP:]], axis=0)


def down_mine(bits, dd, act, recv, first, after=()):
    def body(s, l, rk, rs, gk, gs, keep, send):
        put_down(keep, 0, halves(lambda a: l[0, a], lambda a: rk[a]) + get_down(gk[0]))
        put_down(send, 0, halves(lambda a: l[0, a], lambda a: rs[a]) + get_down(gs[0]))

    def block(flip):
        return lambda i, s: insert_bit(i, first, s[1 + first] ^ flip)

    return call(
        body, (bits, dd, act, act, recv, recv),
        [pl.BlockSpec((1, 2, ROWS, MINE), lambda i, s: (s[0], 0, 0, 0))]
        + [pl.BlockSpec((2, ROWS, W_UP), lambda i, s, m=block(f): (0, 0, m(i, s))) for f in (0, 1)]
        + [pl.BlockSpec((1, *BLOCK), lambda i, s, m=block(f): (m(i, s), 0, 0)) for f in (0, 1)],
        [shape((4, *BLOCK), F32)] * 2, [pl.BlockSpec((1, *BLOCK), lambda i, s: (i, 0, 0))] * 2,
        cost(6.9), "down_mine", after, (4,), 1,
    )


def up_mine(bits, hid, da, recv, first, after=()):
    def body(s, l, r, got, keep, send):
        total = halves(lambda a: l[a], lambda a: r[a])
        mine = s[1 + first] == 0
        for i, j, k, p, q in row_pairs(total, first):
            p, q = p + got[j], q + got[k]
            keep[i] = jnp.where(mine, p, q)
            send[i] = jnp.where(mine, q, p)

    return call(
        body, (bits, hid, da, recv),
        [fixed((2, ROWS, D)), pl.BlockSpec((2, ROWS, W_UP), lambda n, s: (0, 0, 2 * s[0] + n)),
         pl.BlockSpec((8, D // 8, W_UP), lambda n, s: (0, 0, n))],
        [shape((4, *BLOCK), F32)] * 2, [pl.BlockSpec((4, D // 8, W_UP), lambda n, s: (0, 0, n))] * 2,
        cost(5.7), "up_mine", after, (2,), 1,
    )


def attn_columns(product, hid, att, r, lo, width):
    edge = 3 * MINE
    cut = edge // LANE * LANE
    parts = []
    if lo < cut:
        parts.append(product(hid, r[..., 0 : min(cut - lo, width)]))
    if lo + width > cut:
        lane = lax.broadcasted_iota(jnp.int32, (D, LANE), 1)
        right = r[..., cut - lo : cut - lo + LANE]
        parts.append(jnp.where(lane < edge - cut, product(hid, right), product(att, right)))
    if lo + width > cut + LANE:
        parts.append(product(att, r[..., cut - lo + LANE : width]))
    return parts[0] if len(parts) == 1 else jnp.concatenate(parts, axis=1)


def two_halves(left, right):
    return tn(left[0], right[0]) + tn(left[1], right[1])


def attn_mine(bits, hid, att, r3, recv, first, cols, small=None, after=()):
    extra = small is not None
    width = W_UP * len(cols)

    def body(s, h, o, r, *refs):
        gots, more, (keep, send) = refs[: len(cols)], refs[len(cols) : -2], refs[-2:]
        for k, n in enumerate(cols):

            @pl.when(pl.program_id(0) == k)
            def _():
                total = attn_columns(two_halves, h, o, r[0], n * W_UP, W_UP)
                mine = s[1 + first] == 0
                for i, j, jj, p, q in row_pairs(total, first):
                    p, q = p + gots[k][j], q + gots[k][jj]
                    keep[i] = jnp.where(mine, p, q)
                    send[i] = jnp.where(mine, q, p)
                if extra:
                    added = more[0][...] + more[1][...]
                    keep[4] = added
                    send[4] = added

    at = lambda n: n + cols[0]
    specs = [
        fixed((2, ROWS, D)),
        fixed((2, ROWS, D)),
        pl.BlockSpec((1, 2, ROWS, W_UP), lambda n, s: (s[0], 0, 0, at(n))),
    ]
    args = [bits, hid, att, r3]
    for n in cols:
        args.append(recv[n])
        specs.append(fixed((8, D // 8, W_UP)))
    if extra:
        args += small
        specs += [fixed((D // 8, W_UP))] * 2
    out = pl.BlockSpec((4 + extra, D // 8, W_UP), lambda n, s: (0, 0, n))
    return call(
        body, args, specs, [shape((4 + extra, D // 8, width), F32)] * 2, [out] * 2,
        cost(1.5 + 2.8 * len(cols)), "attn_mine", after, (len(cols),), 1,
    )


def split_sum(streams, extra, after=(), through=()):
    n = streams[0][1].shape[0]
    half = (n - extra) // 2

    def body(s, *refs):
        ins, outs = refs[: 4 * len(streams)], refs[4 * len(streams) + len(through) :]
        for k in range(len(streams)):
            ka, ra, kb, rb = ins[4 * k : 4 * k + 4]
            outs[2 * k][...] = ka[...] + ra[...]
            outs[2 * k + 1][...] = kb[...] + rb[...]

    args, specs = [jnp.stack([bit for *_, bit in streams])], []
    outs, out_specs = [shape(a.shape, a.dtype) for a in through], [ANY] * len(through)
    for k, (kept, recv, place, _) in enumerate(streams):
        block = (1, *recv.shape[1:])

        def at(flip, k=k, place=place, block=block):
            def index(i, s):
                j = insert_bit(i, place, s[k] ^ flip)
                return (jnp.where(i == half, 2 * half, j) if extra else j, 0, 0)

            return pl.BlockSpec(block, index)

        args += [kept, recv, kept, recv]
        specs += [at(0), at(0), at(1), at(1)]
        outs += [shape((half + extra, *recv.shape[1:]), F32)] * 2
        out_specs += [pl.BlockSpec(block, lambda i, s: (i, 0, 0))] * 2
    size = sum(recv.size for _, recv, *_ in streams)
    return call(
        body, args, specs, outs, out_specs, cost(1.5 + size * 5e-6), "split_sum", (*through, *after), (half + extra,), 1,
        reuse=len(through),
    )


def join_steps(joint, *pairs, after=()):
    kept = [s.kept for s, _ in pairs]
    recv = [s.recv for s, _ in pairs]

    def body(s, *refs):
        ins, (keep, send) = refs[:-2], refs[-2:]
        for k in range(len(pairs)):
            mine = s[k] == 0
            low, high = (ins[k][i] + ins[len(pairs) + k][i] for i in range(2))
            keep[k] = jnp.where(mine, low, high)
            send[k] = jnp.where(mine, high, low)

    bits = jnp.stack([s.links[name][2] for s, name in pairs])
    block = kept[0].shape
    keep, send = call(
        body, (bits, *kept, *recv), [fixed(block)] * (2 * len(pairs)),
        [shape((len(pairs), *block[1:]), F32)] * 2, [fixed((len(pairs), *block[1:]))] * 2,
        cost(2), "join_steps", after, (1,), 1,
    )
    joint.send(pairs[0][1], keep, send)
    return keep


def steps(*pairs, after=(), through=()):
    args = []
    for s, name in pairs:
        args.append((s.kept, s.recv, len(s.names) - 1 - s.names.index(name), s.links[name][2]))
    outs = split_sum(args, pairs[0][0].extra, after, through)
    passed, outs = outs[: len(through)], outs[len(through) :]
    for k, (s, name) in enumerate(pairs):
        s.send(name, outs[2 * k], outs[2 * k + 1])
    return (outs[0], *passed) if through else outs[0]


class Halving:
    def __init__(self, names, links, extra=0):
        self.names, self.links, self.extra = list(names), links, extra

    def send(self, name, kept, out):
        axis, perm, _ = self.links[name]
        if name in self.names:
            self.names.remove(name)
        self.kept, self.recv = kept, lax.ppermute(out, axis, perm)
        return kept

    def step(self, name, after=()):
        return steps((self, name), after=after)

    def pair(self):
        return self.kept, self.recv


def last_sums(mlps, att0, att1, after=()):
    pairs = [*mlps, *att0, att1]

    def body(*refs):
        ins, (qkv, out, up, down, small) = refs[: 2 * len(pairs)], refs[2 * len(pairs) :]
        for b in range(2):
            up[b] = ins[2 * b][0] + ins[2 * b + 1][0]
            down[b] = get_down(ins[2 * b][1] + ins[2 * b + 1][1])
        total = [ins[2 * i][0] + ins[2 * i + 1][0] for i in range(2, 5)]
        edge = 3 * MINE
        for b, att in enumerate((jnp.concatenate(total[0:2], axis=1), total[2])):
            qkv[b] = att[:, 0:edge]
            out[b] = att[:, edge:]
        small[...] = ins[4][1] + ins[5][1]

    rows = D // 8
    return call(
        body, [a for pair in pairs for a in pair], [VM] * (2 * len(pairs)),
        [shape((2, rows, 3 * MINE), F32), shape((2, rows, MINE), F32), shape((2, rows, D), F32),
         shape((2, MINE, W_UP), F32), shape((rows, W_UP), F32)],
        [VM] * 5, cost(4), "last_sums", after,
    )


def scatter_rest(block, dim, img, sub):
    step = sub // 2
    while step:
        bit = (img // step) % 2
        half = block.shape[dim] // 2
        keep = lax.dynamic_slice_in_dim(block, bit * half, half, dim)
        send = lax.dynamic_slice_in_dim(block, (1 - bit) * half, half, dim)
        perm = [(i, i ^ step) for i in range(8 * sub)]
        block = keep + lax.ppermute(send, "img", perm)
        step //= 2
    return block


def window_bias(table, after=()):
    pairs = 16

    def body(src, out, rolled, wide):
        l = lax.broadcasted_iota(jnp.int32, (LANE, GT), 0)
        t = lax.broadcasted_iota(jnp.int32, (LANE, GT), 1) & (TQ - 1)
        at = lax.broadcasted_iota(jnp.int32, (LANE, GT), 1) >> 6
        there = (t < T) & (l == t + 6 * row_of(t))
        wide[...] = jnp.zeros_like(wide)
        for h in range(PER):
            rows = [src[k // NG, PER * (k % NG) + h : PER * (k % NG) + h + 1] for k in range(2 * NG)]
            rows = jnp.concatenate(rows + [jnp.zeros((pairs - 2 * NG, TABLE), F32)], axis=0)
            for u in range(T):
                shift = 13 * (6 - u // SIDE) + 6 - u % SIDE
                rolled[pairs * u : pairs * (u + 1), :] = pltpu.roll(rows, (TABLE - shift) % TABLE, 1)[:, 0:LANE]
            ones = (there & (at == h)).astype(F32).astype(BF16)
            rest = rolled[...]
            for _ in range(3):
                part = rest.astype(BF16)
                moved = nn(part, ones)
                for k in range(2):
                    wide[k, 0 : pairs * T, :] += moved[:, LANE * k : LANE * (k + 1)]
                rest = rest - part.astype(F32)
        real = lax.broadcasted_iota(jnp.int32, (TP, LANE), 0) < T
        for b in range(2 * NG):
            for k in range(2):
                v = wide[k, pl.ds(b, TP, stride=pairs), :]
                out[b, :, LANE * k : LANE * (k + 1)] = jnp.where(real, v, NEG)

    return call(
        body, (table,), [VM], shape((2 * NG, TP, GT), F32), VM, cost(4), "window_bias", after,
        scratch=[pltpu.VMEM((pairs * T, LANE), F32), pltpu.VMEM((2, pairs * TP, LANE), F32)],
    )


def per_device(
    tokens, crop_count, ln1_gain, ln1_bias, w_qkv, b_query, b_value, bias_table, w_out, b_out,
    ln2_gain, ln2_bias, w_up, b_up, w_down, b_down, cotangent, *, n_img,
):
    win, img = lax.axis_index("win"), lax.axis_index("img")
    sub = n_img // 8
    x_bit, core = win // 2, win % 2
    links = {}
    for k in range(3):
        links[k] = ("img", [(i, i ^ (sub << k)) for i in range(n_img)], (img // (sub << k)) % 2)
    bits = jnp.stack([core, links[0][2], links[1][2], links[2][2]])
    at_core, at_x = jnp.reshape(core, (1,)), jnp.reshape(x_bit, (1,))
    all_valid = jnp.full((1,), C, jnp.int32)
    p = dict(
        ln1_gain=ln1_gain, ln1_bias=ln1_bias, w_qkv=w_qkv, b_query=b_query, b_value=b_value,
        w_out=w_out, b_out=b_out, ln2_gain=ln2_gain, ln2_bias=ln2_bias, w_up=w_up, b_up=b_up,
        w_down=w_down, b_down=b_down,
    )

    def over(way, a):
        return lax.ppermute(a, "win", [(i, i ^ way) for i in range(4)])

    def swap(a):
        return over(1, a)

    table = jnp.pad(bias_table.transpose(0, 2, 1), ((0, 0), (0, 0), (0, TABLE - 169)))
    bias = window_bias(table)

    mine, other = crop_rows(at_core, all_valid, tokens[:, 0].transpose(1, 0, 2))
    near, far = swap(other), (over(2, mine), over(3, other))
    ct_mine, ct_other = crop_rows(at_core, crop_count, cotangent[:, 0].transpose(1, 0, 2), (mine,))
    ct_near, ct_far = swap(ct_other), (over(2, ct_mine), over(3, ct_other))
    fwd0 = block_fwd(0, (at_x, mine, near), bias, p, 0, (ct_mine,))
    fwd0 = block_fwd(0, (at_x, *far), bias, p, 1, fwd0)
    fwd1 = block_fwd(1, (at_core, fwd0[8]), bias, p)
    z0, h0, qkvc0, o0, y0, h20, g0, gp0, _ = fwd0
    z1, h1, qkvc1, o1, y1, h21, g1, gp1, zn = fwd1
    ct = join_pieces(at_x, (ct_mine, ct_near, *ct_far), (zn,))

    def stream(first, extra=0):
        return Halving([k for k in (2, 1, 0) if k != first], links, extra)

    down1, up1, att1, down0, up0 = (stream(k) for k in (0, 1, 0, 0, 1))
    mlp1, mlp0 = (Halving([], links) for _ in range(2))
    att0 = [stream(0, 1), stream(0)]

    dd1, da1, dy, sv_m1, *part = mlp_back(1, at_x, at_core, ct, y1, gp1, g1, h21, p)
    down_x, up_x = (swap(a) for a in part)
    r31, sv_a1, table1, grad1, *part = attn_back(
        1, at_x, at_core, dy, qkvc1, z1, h1, o1, bias, p, (), (part[0],)
    )
    att_x = [swap(a) for a in part]
    last = down1.send(0, *down_mine(bits, dd1, g1, down_x, 0, (sv_a1,)))
    last = up1.send(1, *up_mine(bits, h21, da1, up_x, 1, (last,)))

    dd0, da0, dy, sv_m0, *part = mlp_back(0, at_x, at_core, grad1, y0, gp0, g0, h20, p, (last, *att_x))
    last, *part = steps((down1, 1), (up1, 0), after=(sv_m0,), through=part)
    down_x, up_x = (swap(a) for a in part)
    last = att1.send(0, *attn_mine(bits, h1, o1, r31, att_x, 0, (0, 1), None, (last,)))
    out_mine, out_other = own_quadrants(at_x, zn, True, (last,))
    out_x = swap(out_other)
    last = join_steps(mlp1, (up1, 2), (down1, 2), after=(out_mine,))
    last = down0.send(0, *down_mine(bits, dd0, g0, down_x, 0, (last,)))
    last = up0.send(1, *up_mine(bits, h20, da0, up_x, 1, (last,)))
    r30, sv_a0, small, grad0, *part = attn_back(
        0, at_x, at_core, dy, qkvc0, z0, h0, o0, bias, p, (sv_m0, sv_a1, sv_m1, table1), (last,)
    )
    last, small, *part = steps(
        (up0, 0), (down0, 1), (att1, 1), after=(sv_a0, mlp1.recv), through=(small, *part)
    )
    att_x = [swap(a) for a in part]
    small = [small, swap(small)]
    block_out = token_major(at_core, crop_count, out_mine, out_x, (last,))
    in_mine, in_other = own_quadrants(at_x, grad0, False, (block_out,))
    in_x = swap(in_other)
    last = in_mine
    kept, out = attn_mine(bits, h0, o0, r30, att_x, 0, (0,), small, (last,))
    last = att0[0].send(0, kept, out)
    last = join_steps(mlp0, (up0, 2), (down0, 2), after=(last,))
    kept, out = attn_mine(bits, h0, o0, r30, att_x, 0, (1,), None, (last,))
    last = att0[1].send(0, kept, out)
    last = att0[0].step(1, (last,))
    last = att1.step(2, (last,))
    last = att0[1].step(1, (last,))
    last = att0[0].step(2, (last, mlp0.recv))
    last = att0[1].step(2, (last,))
    grad_tokens = crop_major(at_core, in_mine, in_x, (last,))

    g_qkv, g_out, g_up, g_down, small = last_sums(
        (mlp0.pair(), mlp1.pair()), [a.pair() for a in att0], att1.pair(), (grad_tokens,)
    )
    for k in range(sub.bit_length() - 1):
        small = small + lax.ppermute(small, "img", [(i, i ^ (1 << k)) for i in range(n_img)])
    g_qkv, g_out, g_up = (scatter_rest(g, 1, img, sub) for g in (g_qkv, g_out, g_up))
    g_down = scatter_rest(g_down, 2, img, sub).transpose(0, 2, 1)
    table = small[48:, :169].reshape(2, PER, NG, 169).transpose(0, 3, 2, 1).reshape(2, 169, HEADS)
    width = D // n_img

    vectors = jnp.concatenate([small[:24], small[24:48]], axis=1).reshape(2, 12, D)
    mine = lax.dynamic_slice_in_dim(vectors[:, :8], img * width, width, 2)
    up_bias = lax.dynamic_slice_in_dim(vectors[:, 8:].reshape(2, FF), img * (4 * width), 4 * width, 1)

    return (
        block_out.transpose(1, 0, 2)[:, None], grad_tokens.reshape(C, 1, T, D), mine[:, 0], mine[:, 1], g_qkv, mine[:, 2], mine[:, 3], table,
        g_out, mine[:, 6], mine[:, 4], mine[:, 5], g_up, up_bias, g_down, mine[:, 7],
    )


def solution(mesh):
    shard = P("img", "win", None, None)
    vec, mat = P(None, "img"), P(None, "img", "win")
    return jax.shard_map(
        functools.partial(per_device, n_img=mesh.shape["img"]),
        mesh=mesh,
        in_specs=(shard, P("img")) + (P(),) * 14 + (shard,),
        out_specs=(shard, shard, vec, vec, mat, vec, vec, P(), mat, vec, vec, vec, mat, vec, mat, vec),
        check_vma=False,
    )
```

```python
import functools

import jax
import jax.numpy as jnp
from jax import lax
from jax.experimental import pallas as pl
from jax.experimental.pallas import tpu as pltpu
from jax.sharding import PartitionSpec as P

HEADS = 24
HD = 32
SIDE = 7
T = SIDE * SIDE
TP = 56
TQ = 64
D = 768
FF = 3072
C = 8
ROWS = T * C
PAD_ROWS = TQ * C
HALF = C // 2
PIECE = T * HALF
LANE = 128
NG = D // LANE
PER = LANE // HD
GT = PER * TQ
EPSILON = 1e-05
SCALE = HD ** (-0.5)
NEG = -1e30
QCH = 768
FCH = 1536
WIN = 4
N_Q = 3 * D // QCH
N_F = FF // FCH
W_UP = D // 2
MINE = D // 4
VMEM_OF = {"forwar": 48 << 20, "mlp_ba": 48 << 20, "attn_b": 44 << 20, "attn_m": 24 << 20}
VMEM_SMALL = 24 << 20
COST = 0.4
F32 = jnp.float32
BF16 = jnp.bfloat16

TAIL_K = 0.3
TAIL = (
    0.11963200491345692,
    0.12071217642148169,
    0.10017566554041868,
    0.12769280877164998,
    -0.052036176065482394,
    0.20455934198696718,
    -0.15616004916725648,
    0.035424145900813254,
)
INV_SQRT_2PI = 0.3989422804014327

def nt(left, right):
    return lax.dot_general(left, right, (((1,), (1,)), ((), ())), preferred_element_type=F32)


def tn(left, right):
    return lax.dot_general(left, right, (((0,), (0,)), ((), ())), preferred_element_type=F32)


def nn(left, right):
    return jnp.dot(left, right, preferred_element_type=F32)


def norm_parts(values):
    average = jnp.mean(values, axis=-1, keepdims=True)
    centered = values - average
    inverse = lax.rsqrt(jnp.mean(centered * centered, axis=-1, keepdims=True) + EPSILON)
    return centered * inverse, inverse


def norm_back(grad_out, normed, inverse, gain):
    scaled = grad_out * gain
    return inverse * (
        scaled
        - jnp.mean(scaled, axis=-1, keepdims=True)
        - normed * jnp.mean(scaled * normed, axis=-1, keepdims=True)
    )


def gelu_parts(a):
    bell = jnp.exp(-0.5 * a * a)
    size = jnp.abs(a)
    t = 1.0 / (1.0 + TAIL_K * size)
    poly = jnp.full_like(t, TAIL[-1])
    for coef in TAIL[-2::-1]:
        poly = poly * t + coef
    tail = bell * (t * poly)
    phi = jnp.where(a < 0, tail, 1.0 - tail)
    return a * phi, phi + a * (INV_SQRT_2PI * bell)


def head_masks(rows):
    lanes = lax.broadcasted_iota(jnp.int32, (rows, LANE), 1)
    return [(lanes >= HD * h) & (lanes < HD * (h + 1)) for h in range(PER)]


def spread(values, ones):
    return jnp.concatenate([values * m for m in ones], axis=0)


def gather_heads(stacked, masks):
    out = stacked[(PER - 1) * TQ : (PER - 1) * TQ + TP]
    for h in range(PER - 2, -1, -1):
        out = jnp.where(masks[h], stacked[h * TQ : h * TQ + TP], out)
    return out


def soft(scores):
    e = jnp.exp(scores - jnp.max(scores, axis=0, keepdims=True))
    return e * (1.0 / jnp.sum(e, axis=0, keepdims=True))


def colsum(values):
    return jnp.sum(values, axis=0, keepdims=True)


def rows_of(w, n=T, stride=C):
    return pl.ds(w, n, stride=stride)


def lanes_at(n, width):
    return pl.ds(pl.multiple_of(n * width, width), width)


def put_rolled(dest, source, a, back):
    shift, kept = (-3, range(3, 7)) if back else (3, range(0, 4))
    for i in range(SIDE):
        for j in range(SIDE):
            half = a if i in kept else 1 - a
            tile = source[half, SIDE * ((i + shift) % SIDE) + (j + shift) % SIDE]
            if j not in kept:
                tile = pltpu.roll(tile, HALF, 0)
            t = SIDE * i + j
            dest[C * t : C * (t + 1), :] = tile


ANY = pl.BlockSpec(memory_space=pl.ANY)
VM = pl.BlockSpec(memory_space=pltpu.VMEM)
SM = pl.BlockSpec(memory_space=pltpu.SMEM)


def cost(micros):
    return pl.CostEstimate(flops=int(micros * COST * 1.15e9), bytes_accessed=0, transcendentals=0)


def shape(dims, dtype):
    return jax.ShapeDtypeStruct(dims, dtype)


def fixed(dims, single=False):
    mode = dict(pipeline_mode=pl.Buffered(1)) if single else {}
    return pl.BlockSpec(dims, lambda *_: (0,) * len(dims), **mode)


def per_half(dims):
    return pl.BlockSpec((1, *dims), lambda a, *_: (a, *(0,) * len(dims)))


def call(body, args, in_specs, outs, out_specs, estimate, name, after=(), grid=(), scalars=0, scratch=(), reuse=0):
    n_in, n_after = len(args), len(after)

    def wrapped(*refs):
        return body(*refs[:n_in], *refs[n_in + n_after :])

    return pl.pallas_call(
        wrapped,
        grid_spec=pltpu.PrefetchScalarGridSpec(
            num_scalar_prefetch=scalars,
            grid=grid,
            in_specs=list(in_specs) + [ANY] * n_after,
            out_specs=out_specs,
            scratch_shapes=list(scratch),
        ),
        out_shape=outs,
        input_output_aliases={n_in + k: k for k in range(reuse)},
        compiler_params=pltpu.CompilerParams(vmem_limit_bytes=VMEM_OF.get(name[:6], VMEM_SMALL)),
        cost_estimate=estimate,
        name=name,
    )(*args, *after)


def crop_rows(core, count, crops, after=()):
    def body(at, n, src, mine, other, s):
        wide = src[...].astype(F32).reshape(ROWS, D)
        for g in range(NG):
            s[g] = wide[:, LANE * g : LANE * (g + 1)]
        for k in range(HALF):
            for out, c in ((mine, at[0]), (other, 1 - at[0])):
                crop = HALF * c + k
                keep = jnp.where(crop < n[0], 1.0, 0.0).astype(F32)
                for g in range(NG):
                    out[g, rows_of(k, stride=HALF), :] = s[g, rows_of(crop), :] * keep

    return call(
        body, (core, count, crops), [SM, SM, VM], [shape((NG, PIECE, LANE), F32)] * 2, [VM] * 2, cost(2.5), "crop_rows", after, scratch=[pltpu.VMEM((NG, ROWS, LANE), F32)],
    )


def weave(dest, pieces):
    for b, piece in enumerate(pieces):
        for k in range(HALF):
            for g in range(NG):
                dest[g, rows_of(HALF * b + k), :] = piece[g, rows_of(k, stride=HALF), :]


def own_quadrants(x_at, both_halves, rolled, after=()):
    def body(x, src, mine, other, full, s):
        if rolled:
            put_rolled(full, src, x[0], True)
        else:
            full[...] = src[x[0]].reshape(ROWS, D)
        for g in range(NG):
            s[g] = full[:, LANE * g : LANE * (g + 1)]
        for b, out in enumerate((mine, other)):
            for k in range(HALF):
                for g in range(NG):
                    out[g, rows_of(k, stride=HALF), :] = s[g, rows_of(HALF * b + k), :]

    return call(
        body, (x_at, both_halves), [SM, VM], [shape((NG, PIECE, LANE), F32)] * 2, [VM] * 2, cost(3), "own_quadrants", after, scratch=[pltpu.VMEM((ROWS, D), F32), pltpu.VMEM((NG, ROWS, LANE), F32)],
    )


def token_major(core, count, mine, theirs, after=()):
    def body(at, n, a, b, out, s):
        for k in range(HALF):
            for src, c in ((a, at[0]), (b, 1 - at[0])):
                crop = HALF * c + k
                keep = jnp.where(crop < n[0], 1.0, 0.0).astype(F32)
                for g in range(NG):
                    s[g, rows_of(crop), :] = src[g, rows_of(k, stride=HALF), :] * keep
        for g in range(NG):
            out[:, :, LANE * g : LANE * (g + 1)] = s[g].reshape(T, C, LANE).astype(BF16)

    return call(
        body, (core, count, mine, theirs), [SM, SM, VM, VM], shape((T, C, D), BF16), VM, cost(2.5), "token_major", after, scratch=[pltpu.VMEM((NG, ROWS, LANE), F32)],
    )


def crop_major(core, mine, theirs, after=()):
    def body(at, a, b, out):
        for k in range(HALF):
            for src, c in ((a, at[0]), (b, 1 - at[0])):
                for g in range(NG):
                    out[pl.ds((HALF * c + k) * (T * NG) + g, T, stride=NG), :] = src[g, rows_of(k, stride=HALF), :]

    return call(
        body, (core, mine, theirs), [SM, VM, VM], shape((C * T * NG, LANE), F32), VM, cost(2.5), "crop_major", after,
    )


def fwd_body(b, which, *refs):
    a = pl.program_id(0)
    if b == 0:
        at_x, p0, p1, *rest = refs
    else:
        core, src, *rest = refs
    (
        bias, ln1g, ln1b, bq, bv, bout, ln2g, ln2b, bup, bdown,
        wqkv_h, wout_h, wup_h, wdown_h,
        z_h, h_h, qkvc_h, o_h, y_h, h2_h, g_h, gp_h, zn_o,
        wqkv, wout, wup, wdown, qkv_s, o_s, bqkv, bias_s,
        z_o, h_o, qkvc_o, o_o, y_o, h2_o, g_o, gp_o, sem_q, sem_o, sem_u, sem_d, sem_out,
    ) = rest
    at = at_x[0] ^ which if b == 0 else a
    results = (
        (z_o, z_h), (h_o, h_h), (qkvc_o, qkvc_h), (o_o, o_h), (y_o, y_h), (h2_o, h2_h), (g_o, g_h), (gp_o, gp_h),
    )

    def out(k):
        return pltpu.make_async_copy(results[k][0].at[0], results[k][1].at[at], sem_out.at[k])

    def free(k):
        @pl.when(a > 0)
        def _():
            out(k).wait()

    def cp_q(n):
        return pltpu.make_async_copy(
            wqkv_h.at[b, :, lanes_at(n, QCH)], wqkv.at[:, lanes_at(n, QCH)], sem_q.at[n]
        )

    def cp_u(n):
        return pltpu.make_async_copy(
            wup_h.at[b, :, lanes_at(n, FCH)], wup.at[:, lanes_at(n, FCH)], sem_u.at[n]
        )

    def cp_d(n):
        return pltpu.make_async_copy(
            wdown_h.at[b, lanes_at(n, FCH), :], wdown.at[lanes_at(n, FCH), :], sem_d.at[n]
        )

    cp_o = pltpu.make_async_copy(wout_h.at[b], wout, sem_o)

    def wait(copy):
        @pl.when(a == 0)
        def _():
            copy.wait()

    @pl.when(a == 0)
    def _():
        for n in range(N_Q):
            cp_q(n).start()
        cp_o.start()
        for n in range(N_F):
            cp_u(n).start()
            cp_d(n).start()
        bqkv[:, 0:D] = bq[b : b + 1, :]
        bqkv[:, D : 2 * D] = jnp.zeros((1, D), F32)
        bqkv[:, 2 * D :] = bv[b : b + 1, :]
        qkv_s[:, ROWS:, :] = jnp.zeros((3 * NG, PAD_ROWS - ROWS, LANE), F32)

    free(0)
    if b == 0:
        weave(o_s, (p0, p1))
        for g in range(NG):
            z_o[0, :, LANE * g : LANE * (g + 1)] = o_s[g, 0:ROWS, :]
    else:
        put_rolled(z_o.at[0], src, a, False)
        for w in range(2):
            mask = shift_mask(a, core[0] ^ w)
            for g in range(NG):
                bias_s[w * NG + g] = bias[NG + g] + mask
    out(0).start()
    normed, _ = norm_parts(z_o[0])
    free(1)
    h_o[0] = (normed * ln1g[b : b + 1, :] + ln1b[b : b + 1, :]).astype(BF16)
    out(1).start()

    def qkv_step(n, _):
        wait(cp_q(n))
        joint = nn(h_o[0], wqkv[:, lanes_at(n, QCH)]) + bqkv[:, lanes_at(n, QCH)]
        joint = joint * jnp.where(n < D // QCH, SCALE, 1.0)
        joint = joint.astype(BF16).astype(F32)
        for k in range(QCH // LANE):
            qkv_s[n * (QCH // LANE) + k, 0:ROWS, :] = joint[:, LANE * k : LANE * (k + 1)]
        return 0

    lax.fori_loop(0, N_Q, qkv_step, 0)
    masks = head_masks(TP)
    ones = [m.astype(F32).astype(BF16) for m in head_masks(TQ)]

    def attend(step, _):
        items = [(step * WIN + i, g) for i in range(WIN) for g in range(NG)]
        qs = [qkv_s[g, rows_of(w, TQ), :].astype(BF16) for w, g in items]
        ks = [qkv_s[NG + g, rows_of(w, TP), :].astype(BF16) for w, g in items]
        vs = [qkv_s[2 * NG + g, rows_of(w, TP), :].astype(BF16) for w, g in items]
        for (w, g), q, k, v in zip(items, qs, ks, vs):
            qkvc_o[0, w, g] = q
            qkvc_o[0, w, NG + g, 0:TP] = k
            qkvc_o[0, w, 2 * NG + g, 0:TP] = v
        added = [bias[g] if b == 0 else bias_s[w // HALF * NG + g] for w, g in items]
        scores = [nt(k, spread(q, ones)) + extra for k, q, extra in zip(ks, qs, added)]
        probs = [soft(score).astype(BF16) for score in scores]
        for (w, g), prob, v in zip(items, probs, vs):
            o_s[g, rows_of(w, TP), :] = gather_heads(tn(prob, v), masks)
        return 0

    free(2)
    lax.fori_loop(0, C // WIN, attend, 0, unroll=2)
    out(2).start()
    free(3)
    for g in range(NG):
        o_o[0, :, LANE * g : LANE * (g + 1)] = o_s[g, 0:ROWS, :].astype(BF16)
    out(3).start()
    wait(cp_o)
    free(4)
    y_o[0] = z_o[0] + (nn(o_o[0], wout[...]) + bout[b : b + 1, :])
    out(4).start()
    normed, _ = norm_parts(y_o[0])
    free(5)
    h2_o[0] = (normed * ln2g[b : b + 1, :] + ln2b[b : b + 1, :]).astype(BF16)
    out(5).start()
    free(6)
    free(7)
    def mlp_step(n, _):
        wait(cp_u(n))
        up = nn(h2_o[0], wup[:, lanes_at(n, FCH)]) + bup[b : b + 1, lanes_at(n, FCH)]
        act, slope = gelu_parts(up)
        g_o[0, :, lanes_at(n, FCH)] = act.astype(BF16)
        gp_o[0, :, lanes_at(n, FCH)] = slope.astype(BF16)
        return 0

    lax.fori_loop(0, N_F, mlp_step, 0)
    out(6).start()
    out(7).start()
    for n in range(N_F):
        wait(cp_d(n))
    zn_o[0] = (y_o[0] + (nn(g_o[0], wdown[...]) + bdown[b : b + 1, :])).reshape(T, C, D)

    @pl.when(a == pl.num_programs(0) - 1)
    def _():
        for k in range(len(results)):
            out(k).wait()


def block_fwd(b, sources, bias, p, which=None, after=()):
    outs = [
        shape((2, ROWS, D), F32),
        shape((2, ROWS, D), BF16),
        shape((2, C, 3 * NG, TQ, LANE), BF16),
        shape((2, ROWS, D), BF16),
        shape((2, ROWS, D), F32),
        shape((2, ROWS, D), BF16),
        shape((2, ROWS, FF), BF16),
        shape((2, ROWS, FF), BF16),
        shape((2, T, C, D), F32),
    ]
    if b == 0:
        specs = [fixed((NG, PIECE, LANE), True)] * 2
        out_specs = [pl.BlockSpec((1, T, C, D), lambda a, s: (s[0] ^ which, 0, 0, 0))]
    else:
        specs = [SM, fixed((2, T, C, D), True)]
        out_specs = [per_half((T, C, D))]
    small = (bias, p["ln1_gain"], p["ln1_bias"], p["b_query"], p["b_value"], p["b_out"],
             p["ln2_gain"], p["ln2_bias"], p["b_up"], p["b_down"])
    big = (p["w_qkv"], p["w_out"], p["w_up"], p["w_down"])
    return call(
        functools.partial(fwd_body, b, which),
        (*sources, *small, *big),
        specs + [fixed(v.shape, True) for v in small] + [ANY] * 4,
        outs,
        [ANY] * 8 + out_specs,
        cost(21 if which is not None else 36),
        f"forward_{b}",
        after,
        grid=(2 if which is None else 1,),
        scalars=int(which is not None),
        reuse=len(outs) if which == 1 else 0,
        scratch=[
            pltpu.VMEM((D, 3 * D), BF16),
            pltpu.VMEM((D, D), BF16),
            pltpu.VMEM((D, FF), BF16),
            pltpu.VMEM((FF, D), BF16),
            pltpu.VMEM((3 * NG, PAD_ROWS, LANE), F32),
            pltpu.VMEM((NG, PAD_ROWS, LANE), F32),
            pltpu.VMEM((1, 3 * D), F32),
            pltpu.VMEM((2 * NG, TP, GT), F32),
            *(pltpu.VMEM((1, *o.shape[1:]), o.dtype) for o in outs[:8]),
            pltpu.SemaphoreType.DMA((N_Q,)),
            pltpu.SemaphoreType.DMA,
            pltpu.SemaphoreType.DMA((N_F,)),
            pltpu.SemaphoreType.DMA((N_F,)),
            pltpu.SemaphoreType.DMA((8,)),
        ],
    )


def mlp_back_body(b, x_at, core, *refs):
    if b == 1:
        (*pieces, y, gp, act, hid, ln2g,
         wdown_h, wup_h, dd_o, da_o, dy_o, sv_o, down_o, up_o,
         wdown, wup, dz, dd, da_s, src, woven, sem_d, sem_u) = refs
    else:
        (src, y, gp, act, hid, ln2g,
         wdown_h, wup_h, dd_o, da_o, dy_o, sv_o, down_o, up_o,
         wdown, wup, dz, dd, da_s, sem_d, sem_u) = refs
    a = pl.program_id(0)

    def cp_u(n):
        return pltpu.make_async_copy(
            wup_h.at[b, :, lanes_at(n, D)], wup.at[:, lanes_at(n, D)], sem_u.at[n]
        )

    def cp_d(n):
        return pltpu.make_async_copy(
            wdown_h.at[b, lanes_at(n, D), :], wdown.at[lanes_at(n, D), :], sem_d.at[n]
        )

    def wait(copy):
        @pl.when(a == 0)
        def _():
            copy.wait()

    @pl.when(a == 0)
    def _():
        for n in range(4):
            cp_d(n).start()
            cp_u(n).start()
        sv_o[...] = jnp.zeros_like(sv_o)
        if b == 1:
            for k in range(2):
                weave(woven, pieces[2 * k : 2 * k + 2])
                for g in range(NG):
                    src[x_at[0] ^ k, :, :, LANE * g : LANE * (g + 1)] = woven[g].reshape(T, C, LANE)

    put_rolled(dz, src, a, b == 0)
    low = dz[...].astype(BF16)
    dd[...] = low
    sv_o[3:4, :] += colsum(low.astype(F32))
    for x in range(2):

        @pl.when(x_at[0] == x)
        def _():
            for c in range(2):
                w = 2 * x + c
                dd_o[c, 0] = dd[:, MINE * w : MINE * (w + 1)]

    def step(n, _):
        wait(cp_d(n))
        grad_act = nt(dd[...], wdown[lanes_at(n, D), :])
        da = (grad_act * gp[0, :, lanes_at(n, D)].astype(F32)).astype(BF16)

        da_s[:, lanes_at(n, D)] = da

        @pl.when(n // 2 == x_at[0])
        def _():
            da_o[0, :, lanes_at(n % 2, D)] = da

        sv_o[pl.ds(4 + n, 1), :] += colsum(da.astype(F32))
        return 0

    lax.fori_loop(0, 4, step, 0)
    for n in range(4):
        wait(cp_u(n))
    dh2 = nt(da_s[...], wup[...])
    normed, inverse = norm_parts(y[0])
    sv_o[0:1, :] += colsum(dh2 * normed)
    sv_o[1:2, :] += colsum(dh2)
    dy = dz[...] + norm_back(dh2, normed, inverse, ln2g[b : b + 1, :])
    dy_o[0] = dy
    sv_o[2:3, :] += colsum(dy.astype(BF16).astype(F32))
    down = tn(dd_o[1 - core[0], 0], act[0])
    up = tn(hid[0], da_o[0, :, lanes_at(1 - core[0], D)])

    def put(add):
        for k in range(8):
            add_down(down_o, k, down[:, W_UP * k : W_UP * (k + 1)], add)
            rows = up[D // 8 * k : D // 8 * (k + 1)]
            up_o[k] = up_o[k] + rows if add else rows

    for half in range(2):
        pl.when(a == half)(functools.partial(put, half == 1))


def mlp_back(b, x_at, core, src, y, gp, act, hid, p, after=()):
    return call(
        functools.partial(mlp_back_body, b),
        (x_at, core, *src, y, gp, act, hid, p["ln2_gain"], p["w_down"], p["w_up"]),
        [SM, SM, *(fixed(v.shape, True) for v in src), per_half((ROWS, D)), per_half((ROWS, FF)), per_half((ROWS, FF)),
         per_half((ROWS, D)), fixed((2, D)), ANY, ANY],
        [
            shape((2, 2, ROWS, MINE), BF16),
            shape((2, ROWS, FF // 2), BF16),
            shape((2, ROWS, D), F32),
            shape((8, D), F32),
            shape((8, *BLOCK), F32),
            shape((8, *BLOCK), F32),
        ],
        [
            pl.BlockSpec((2, 1, ROWS, MINE), lambda a: (0, a, 0, 0)),
            per_half((ROWS, FF // 2)),
            per_half((ROWS, D)),
            fixed((8, D)),
            fixed((8, *BLOCK), True),
            fixed((8, *BLOCK), True),
        ],
        cost(22),
        f"mlp_back_{b}",
        after,
        grid=(2,),
        scratch=[
            pltpu.VMEM((FF, D), BF16),
            pltpu.VMEM((D, FF), BF16),
            pltpu.VMEM((ROWS, D), F32),
            pltpu.VMEM((ROWS, D), BF16),
            pltpu.VMEM((ROWS, FF), BF16),
            *([pltpu.VMEM((2, T, C, D), F32), pltpu.VMEM((NG, ROWS, LANE), F32)] if b else []),
            pltpu.SemaphoreType.DMA((4,)),
            pltpu.SemaphoreType.DMA((4,)),
        ],
    )


TABLE = 256
BLOCK = (D // 8, D)


def row_of(t):
    return sum((t >= SIDE * k).astype(jnp.int32) for k in range(1, 10))


def shift_mask(a, column):
    u = lax.broadcasted_iota(jnp.int32, (TP, GT), 0)
    t = lax.broadcasted_iota(jnp.int32, (TP, GT), 1) & (TQ - 1)
    iu, it = row_of(u), row_of(t)
    rows = (iu >= 4) != (it >= 4)
    cols = (u - SIDE * iu >= 4) != (t - SIDE * it >= 4)
    return jnp.where((rows & (a == 1)) | (cols & (column == 1)), -100.0, 0.0)


def table_sums(ds, moved):
    row = lax.broadcasted_iota(jnp.int32, (GT, PER * LANE), 0)
    col = lax.broadcasted_iota(jnp.int32, (GT, PER * LANE), 1)
    t = row & (TQ - 1)
    there = (row >> 6 == col >> 7) & (t < T) & ((col & (LANE - 1)) == t + 6 * row_of(t))
    onehot = there.astype(F32).astype(BF16)
    moved[:, NG * TP :, :] = jnp.zeros((PER, (8 - NG) * TP, LANE), F32)
    for g in range(NG):
        rest = ds[g]
        total = jnp.zeros((TP, PER * LANE), F32)
        for _ in range(3):
            part = rest.astype(BF16)
            total += nn(part, onehot)
            rest = rest - part.astype(F32)
        for h in range(PER):
            moved[h, TP * g : TP * (g + 1), :] = total[:, LANE * h : LANE * (h + 1)]


def sum_table(moved, put):
    for h in range(PER):
        total = jnp.zeros((8, TABLE), F32)
        for u in range(T):
            v = moved[h, pl.ds(u, 8, stride=TP), :]
            shift = 13 * (6 - u // SIDE) + 6 - u % SIDE
            total += pltpu.roll(jnp.concatenate([v, jnp.zeros_like(v)], axis=1), shift, 1)
        put(h, total)


def attn_back_body(b, x_at, core, dy, qkvc, z, hid, att, *refs):
    bias, ln1g, *refs = refs
    if b == 0:
        sv_m0, sv_a1, sv_m1, table1, *refs = refs
    (wout_h, wqkv_h, r3_o, sv_o, sum_o, grad_o, *part_o,
     wout, wqkv, do_s, dqkv_s, dq, bias_s, ds_o, moved, dyr, sem_o, sem_q) = refs
    a = pl.program_id(0)
    cp_o = pltpu.make_async_copy(wout_h.at[b], wout, sem_o)

    def cp_q(n):
        return pltpu.make_async_copy(
            wqkv_h.at[b, :, lanes_at(n, QCH)], wqkv.at[:, lanes_at(n, QCH)], sem_q.at[n]
        )

    def wait(copy):
        @pl.when(a == 0)
        def _():
            copy.wait()

    @pl.when(a == 0)
    def _():
        cp_o.start()
        for n in range(N_Q):
            cp_q(n).start()
        do_s[:, ROWS:, :] = jnp.zeros((NG, PAD_ROWS - ROWS, LANE), F32)
        ds_o[...] = jnp.zeros_like(ds_o)
        sv_o[...] = jnp.zeros_like(sv_o)

    if b == 1:
        for w in range(2):
            mask = shift_mask(a, core[0] ^ w)
            for g in range(NG):
                bias_s[w * NG + g] = bias[NG + g] + mask
    dyr[...] = dy[0].astype(BF16)
    wait(cp_o)
    do = nt(dyr[...], wout[...]).astype(BF16).astype(F32)
    for g in range(NG):
        do_s[g, 0:ROWS, :] = do[:, LANE * g : LANE * (g + 1)]
    masks = head_masks(TP)
    ones = [m.astype(F32).astype(BF16) for m in head_masks(TQ)]

    def attend(step, _):
        items = [(step * WIN + i, g) for i in range(WIN) for g in range(NG)]
        ks = [qkvc[0, w, NG + g, 0:TP] for w, g in items]
        q_wide = [spread(qkvc[0, w, g], ones) for w, g in items]
        do_wide = [spread(do_s[g, rows_of(w, TQ), :].astype(BF16), ones) for w, g in items]
        added = [bias[g] if b == 0 else bias_s[w // HALF * NG + g] for w, g in items]
        scores = [nt(k, q) + extra for k, q, extra in zip(ks, q_wide, added)]
        dprobs = [nt(qkvc[0, w, 2 * NG + g, 0:TP], d) for (w, g), d in zip(items, do_wide)]
        probs = [soft(score) for score in scores]
        weighted = [p * d for p, d in zip(probs, dprobs)]
        ds = [x - p * jnp.sum(x, axis=0, keepdims=True) for x, p in zip(weighted, probs)]
        for (w, g), d in zip(items, ds):
            ds_o[g] += d
        low = [d.astype(BF16) for d in ds]
        dks = [nn(x, q) for x, q in zip(low, q_wide)]
        dvs = [nn(p.astype(BF16), d) for p, d in zip(probs, do_wide)]
        dqs = [tn(x, k) for x, k in zip(low, ks)]
        for (w, g), d_q, d_k, d_v in zip(items, dqs, dks, dvs):
            dqkv_s[g, rows_of(w, TP), :] = gather_heads(d_q, masks) * SCALE
            dqkv_s[NG + g, rows_of(w, TP), :] = d_k
            dqkv_s[2 * NG + g, rows_of(w, TP), :] = d_v
        return 0

    lax.fori_loop(0, C // WIN, attend, 0)
    for g in range(3 * NG):
        dq[:, LANE * g : LANE * (g + 1)] = dqkv_s[g, 0:ROWS, :].astype(BF16)
    sv_o[2:3, :] += colsum(dq[:, 0:D].astype(F32))
    sv_o[3:4, :] += colsum(dq[:, 2 * D :].astype(F32))
    for n in range(N_Q):
        wait(cp_q(n))
    dh = nt(dq[...], wqkv[...])
    for x in range(2):

        @pl.when(x_at[0] == x)
        def _():
            for c in range(2):
                w = 2 * x + c
                r3_o[c, 0] = jnp.concatenate(
                    [dq[:, 3 * MINE * w : 3 * MINE * (w + 1)], dyr[:, MINE * w : MINE * (w + 1)]], axis=1
                )

    normed, inverse = norm_parts(z[0])
    sv_o[0:1, :] += colsum(dh * normed)
    sv_o[1:2, :] += colsum(dh)
    grad_o[0] = (dy[0] + norm_back(dh, normed, inverse, ln1g[b : b + 1, :])).reshape(T, C, D)
    other = r3_o[1 - core[0], 0]
    parts = [attn_columns(tn, hid[0], att[0], other[:, W_UP * n : W_UP * (n + 1)], W_UP * n, W_UP) for n in range(2)]

    def put_parts(add):
        for out, part in zip(part_o, parts):
            blocks = part.reshape(8, D // 8, W_UP)
            out[...] = out[...] + blocks if add else blocks

    for half in range(2):
        pl.when(a == half)(functools.partial(put_parts, half == 1))

    @pl.when(a == 1)
    def _():
        table_sums(ds_o, moved)
        if b == 1:
            sum_table(moved, lambda h, v: sum_o.__setitem__(h, v))
            return
        sum_o[...] = jnp.zeros_like(sum_o)
        for at, ref in ((0, sv_o), (4, sv_m0), (12, sv_a1), (16, sv_m1)):
            for k in range(2):
                sum_o[24 * k + at : 24 * k + at + ref.shape[0], :] = ref[:, W_UP * k : W_UP * (k + 1)]

        def put(h, v, at=48):
            sum_o[at + NG * h : at + NG * (h + 1), 0:TABLE] = v[0:NG]

        sum_table(moved, put)
        for h in range(PER):
            put(h, table1[h], 72)


def attn_back(b, x_at, core, dy, qkvc, z, hid, att, bias, p, sums=(), after=()):
    sum_shape = (PER, 8, TABLE) if b else (D // 8, W_UP)
    return call(
        functools.partial(attn_back_body, b),
        (x_at, core, dy, qkvc, z, hid, att, bias, p["ln1_gain"], *sums, p["w_out"], p["w_qkv"]),
        [SM, SM, per_half((ROWS, D)), per_half((C, 3 * NG, TQ, LANE))] + [per_half((ROWS, D))] * 3
        + [fixed(bias.shape, True), fixed((2, D)), *(fixed(v.shape) for v in sums), ANY, ANY],
        [shape((2, 2, ROWS, D), BF16), shape((4, D), F32), shape(sum_shape, F32), shape((2, T, C, D), F32)]
        + [shape((8, D // 8, W_UP), F32)] * 2,
        [
            pl.BlockSpec((2, 1, ROWS, D), lambda a: (0, a, 0, 0)),
            fixed((4, D)),
            fixed(sum_shape),
            per_half((T, C, D)),
        ]
        + [fixed((8, D // 8, W_UP), True)] * 2,
        cost(31),
        f"attn_back_{b}",
        after,
        grid=(2,),
        scratch=[
            pltpu.VMEM((D, D), BF16),
            pltpu.VMEM((D, 3 * D), BF16),
            pltpu.VMEM((NG, PAD_ROWS, LANE), F32),
            pltpu.VMEM((3 * NG, PAD_ROWS, LANE), F32),
            pltpu.VMEM((ROWS, 3 * D), BF16),
            pltpu.VMEM((2 * NG, TP, GT), F32),
            pltpu.VMEM((NG, TP, GT), F32),
            pltpu.VMEM((PER, 8 * TP, LANE), F32),
            pltpu.VMEM((ROWS, D), BF16),
            pltpu.SemaphoreType.DMA,
            pltpu.SemaphoreType.DMA((N_Q,)),
        ],
    )


def halves(left, right):
    return tn(left(0), right(0)) + tn(left(1), right(1))


def insert_bit(i, place, bit):
    return ((i >> place) << (place + 1)) | (bit << place) | (i & ((1 << place) - 1))


def row_pairs(values, k):
    height = values.shape[0] // 8
    for i in range(4):
        low = insert_bit(i, k, 0)
        high = low | (1 << k)
        yield i, low, high, values[height * low : height * (low + 1)], values[height * high : height * (high + 1)]


def put_down(out, i, total):
    half = MINE // 2
    out[i, :, 0:W_UP] = total[0:half]
    out[i, :, W_UP:] = total[half:]


def add_down(out, i, total, add):
    put_down(out, i, total + get_down(out[i]) if add else total)


def get_down(block):
    return jnp.concatenate([block[:, 0:W_UP], block[:, W_UP:]], axis=0)


def down_mine(bits, dd, act, recv, first, after=()):
    def body(s, l, rk, rs, gk, gs, keep, send):
        put_down(keep, 0, halves(lambda a: l[0, a], lambda a: rk[a]) + get_down(gk[0]))
        put_down(send, 0, halves(lambda a: l[0, a], lambda a: rs[a]) + get_down(gs[0]))

    def block(flip):
        return lambda i, s: insert_bit(i, first, s[1 + first] ^ flip)

    return call(
        body, (bits, dd, act, act, recv, recv),
        [pl.BlockSpec((1, 2, ROWS, MINE), lambda i, s: (s[0], 0, 0, 0))]
        + [pl.BlockSpec((2, ROWS, W_UP), lambda i, s, m=block(f): (0, 0, m(i, s))) for f in (0, 1)]
        + [pl.BlockSpec((1, *BLOCK), lambda i, s, m=block(f): (m(i, s), 0, 0)) for f in (0, 1)],
        [shape((4, *BLOCK), F32)] * 2, [pl.BlockSpec((1, *BLOCK), lambda i, s: (i, 0, 0))] * 2,
        cost(6.9), "down_mine", after, (4,), 1,
    )


def up_mine(bits, hid, da, recv, first, after=()):
    def body(s, l, r, got, keep, send):
        total = halves(lambda a: l[a], lambda a: r[a])
        mine = s[1 + first] == 0
        for i, j, k, p, q in row_pairs(total, first):
            p, q = p + got[j], q + got[k]
            keep[i] = jnp.where(mine, p, q)
            send[i] = jnp.where(mine, q, p)

    return call(
        body, (bits, hid, da, recv),
        [fixed((2, ROWS, D)), pl.BlockSpec((2, ROWS, W_UP), lambda n, s: (0, 0, 2 * s[0] + n)),
         pl.BlockSpec((8, D // 8, W_UP), lambda n, s: (0, 0, n))],
        [shape((4, *BLOCK), F32)] * 2, [pl.BlockSpec((4, D // 8, W_UP), lambda n, s: (0, 0, n))] * 2,
        cost(5.7), "up_mine", after, (2,), 1,
    )


def attn_columns(product, hid, att, r, lo, width):
    edge = 3 * MINE
    cut = edge // LANE * LANE
    parts = []
    if lo < cut:
        parts.append(product(hid, r[..., 0 : min(cut - lo, width)]))
    if lo + width > cut:
        lane = lax.broadcasted_iota(jnp.int32, (D, LANE), 1)
        right = r[..., cut - lo : cut - lo + LANE]
        parts.append(jnp.where(lane < edge - cut, product(hid, right), product(att, right)))
    if lo + width > cut + LANE:
        parts.append(product(att, r[..., cut - lo + LANE : width]))
    return parts[0] if len(parts) == 1 else jnp.concatenate(parts, axis=1)


def two_halves(left, right):
    return tn(left[0], right[0]) + tn(left[1], right[1])


def attn_mine(bits, hid, att, r3, recv, first, cols, small=None, after=()):
    extra = small is not None
    width = W_UP * len(cols)

    def body(s, h, o, r, *refs):
        gots, more, (keep, send) = refs[: len(cols)], refs[len(cols) : -2], refs[-2:]
        for k, n in enumerate(cols):

            @pl.when(pl.program_id(0) == k)
            def _():
                total = attn_columns(two_halves, h, o, r[0], n * W_UP, W_UP)
                mine = s[1 + first] == 0
                for i, j, jj, p, q in row_pairs(total, first):
                    p, q = p + gots[k][j], q + gots[k][jj]
                    keep[i] = jnp.where(mine, p, q)
                    send[i] = jnp.where(mine, q, p)
                if extra:
                    added = more[0][...] + more[1][...]
                    keep[4] = added
                    send[4] = added

    at = lambda n: n + cols[0]
    specs = [
        fixed((2, ROWS, D)),
        fixed((2, ROWS, D)),
        pl.BlockSpec((1, 2, ROWS, W_UP), lambda n, s: (s[0], 0, 0, at(n))),
    ]
    args = [bits, hid, att, r3]
    for n in cols:
        args.append(recv[n])
        specs.append(fixed((8, D // 8, W_UP)))
    if extra:
        args += small
        specs += [fixed((D // 8, W_UP))] * 2
    out = pl.BlockSpec((4 + extra, D // 8, W_UP), lambda n, s: (0, 0, n))
    return call(
        body, args, specs, [shape((4 + extra, D // 8, width), F32)] * 2, [out] * 2,
        cost(1.5 + 2.8 * len(cols)), "attn_mine", after, (len(cols),), 1,
    )


def split_sum(streams, extra, after=(), through=()):
    n = streams[0][1].shape[0]
    half = (n - extra) // 2

    def body(s, *refs):
        ins, outs = refs[: 4 * len(streams)], refs[4 * len(streams) + len(through) :]
        for k in range(len(streams)):
            ka, ra, kb, rb = ins[4 * k : 4 * k + 4]
            outs[2 * k][...] = ka[...] + ra[...]
            outs[2 * k + 1][...] = kb[...] + rb[...]

    args, specs = [jnp.stack([bit for *_, bit in streams])], []
    outs, out_specs = [shape(a.shape, a.dtype) for a in through], [ANY] * len(through)
    for k, (kept, recv, place, _) in enumerate(streams):
        block = (1, *recv.shape[1:])

        def at(flip, k=k, place=place, block=block):
            def index(i, s):
                j = insert_bit(i, place, s[k] ^ flip)
                return (jnp.where(i == half, 2 * half, j) if extra else j, 0, 0)

            return pl.BlockSpec(block, index)

        args += [kept, recv, kept, recv]
        specs += [at(0), at(0), at(1), at(1)]
        outs += [shape((half + extra, *recv.shape[1:]), F32)] * 2
        out_specs += [pl.BlockSpec(block, lambda i, s: (i, 0, 0))] * 2
    size = sum(recv.size for _, recv, *_ in streams)
    return call(
        body, args, specs, outs, out_specs, cost(1.5 + size * 5e-6), "split_sum", (*through, *after), (half + extra,), 1,
        reuse=len(through),
    )


def join_steps(joint, *pairs, after=()):
    kept = [s.kept for s, _ in pairs]
    recv = [s.recv for s, _ in pairs]

    def body(s, *refs):
        ins, (keep, send) = refs[:-2], refs[-2:]
        for k in range(len(pairs)):
            mine = s[k] == 0
            low, high = (ins[k][i] + ins[len(pairs) + k][i] for i in range(2))
            keep[k] = jnp.where(mine, low, high)
            send[k] = jnp.where(mine, high, low)

    bits = jnp.stack([s.links[name][2] for s, name in pairs])
    block = kept[0].shape
    keep, send = call(
        body, (bits, *kept, *recv), [fixed(block)] * (2 * len(pairs)),
        [shape((len(pairs), *block[1:]), F32)] * 2, [fixed((len(pairs), *block[1:]))] * 2,
        cost(2), "join_steps", after, (1,), 1,
    )
    joint.send(pairs[0][1], keep, send)
    return keep


def steps(*pairs, after=(), through=()):
    args = []
    for s, name in pairs:
        args.append((s.kept, s.recv, len(s.names) - 1 - s.names.index(name), s.links[name][2]))
    outs = split_sum(args, pairs[0][0].extra, after, through)
    passed, outs = outs[: len(through)], outs[len(through) :]
    for k, (s, name) in enumerate(pairs):
        s.send(name, outs[2 * k], outs[2 * k + 1])
    return (outs[0], *passed) if through else outs[0]


class Halving:
    def __init__(self, names, links, extra=0):
        self.names, self.links, self.extra = list(names), links, extra

    def send(self, name, kept, out):
        axis, perm, _ = self.links[name]
        if name in self.names:
            self.names.remove(name)
        self.kept, self.recv = kept, lax.ppermute(out, axis, perm)
        return kept

    def step(self, name, after=()):
        return steps((self, name), after=after)

    def pair(self):
        return self.kept, self.recv


def last_sums(mlps, att0, att1, after=()):
    pairs = [*mlps, *att0, att1]

    def body(*refs):
        ins, (qkv, out, up, down, small) = refs[: 2 * len(pairs)], refs[2 * len(pairs) :]
        for b in range(2):
            up[b] = ins[2 * b][0] + ins[2 * b + 1][0]
            down[b] = get_down(ins[2 * b][1] + ins[2 * b + 1][1])
        total = [ins[2 * i][0] + ins[2 * i + 1][0] for i in range(2, 5)]
        edge = 3 * MINE
        for b, att in enumerate((jnp.concatenate(total[0:2], axis=1), total[2])):
            qkv[b] = att[:, 0:edge]
            out[b] = att[:, edge:]
        small[...] = ins[4][1] + ins[5][1]

    rows = D // 8
    return call(
        body, [a for pair in pairs for a in pair], [VM] * (2 * len(pairs)),
        [shape((2, rows, 3 * MINE), F32), shape((2, rows, MINE), F32), shape((2, rows, D), F32),
         shape((2, MINE, W_UP), F32), shape((rows, W_UP), F32)],
        [VM] * 5, cost(4), "last_sums", after,
    )


def scatter_rest(block, dim, img, sub):
    step = sub // 2
    while step:
        bit = (img // step) % 2
        half = block.shape[dim] // 2
        keep = lax.dynamic_slice_in_dim(block, bit * half, half, dim)
        send = lax.dynamic_slice_in_dim(block, (1 - bit) * half, half, dim)
        perm = [(i, i ^ step) for i in range(8 * sub)]
        block = keep + lax.ppermute(send, "img", perm)
        step //= 2
    return block


def window_bias(table, after=()):
    pairs = 16

    def body(src, out, rolled, wide):
        l = lax.broadcasted_iota(jnp.int32, (LANE, GT), 0)
        t = lax.broadcasted_iota(jnp.int32, (LANE, GT), 1) & (TQ - 1)
        at = lax.broadcasted_iota(jnp.int32, (LANE, GT), 1) >> 6
        there = (t < T) & (l == t + 6 * row_of(t))
        wide[...] = jnp.zeros_like(wide)
        for h in range(PER):
            rows = [src[k // NG, PER * (k % NG) + h : PER * (k % NG) + h + 1] for k in range(2 * NG)]
            rows = jnp.concatenate(rows + [jnp.zeros((pairs - 2 * NG, TABLE), F32)], axis=0)
            for u in range(T):
                shift = 13 * (6 - u // SIDE) + 6 - u % SIDE
                rolled[pairs * u : pairs * (u + 1), :] = pltpu.roll(rows, (TABLE - shift) % TABLE, 1)[:, 0:LANE]
            ones = (there & (at == h)).astype(F32).astype(BF16)
            rest = rolled[...]
            for _ in range(3):
                part = rest.astype(BF16)
                moved = nn(part, ones)
                for k in range(2):
                    wide[k, 0 : pairs * T, :] += moved[:, LANE * k : LANE * (k + 1)]
                rest = rest - part.astype(F32)
        real = lax.broadcasted_iota(jnp.int32, (TP, LANE), 0) < T
        for b in range(2 * NG):
            for k in range(2):
                v = wide[k, pl.ds(b, TP, stride=pairs), :]
                out[b, :, LANE * k : LANE * (k + 1)] = jnp.where(real, v, NEG)

    return call(
        body, (table,), [VM], shape((2 * NG, TP, GT), F32), VM, cost(4), "window_bias", after,
        scratch=[pltpu.VMEM((pairs * T, LANE), F32), pltpu.VMEM((2, pairs * TP, LANE), F32)],
    )


def per_device(
    tokens, crop_count, ln1_gain, ln1_bias, w_qkv, b_query, b_value, bias_table, w_out, b_out,
    ln2_gain, ln2_bias, w_up, b_up, w_down, b_down, cotangent, *, n_img,
):
    win, img = lax.axis_index("win"), lax.axis_index("img")
    sub = n_img // 8
    x_bit, core = win // 2, win % 2
    links = {}
    for k in range(3):
        links[k] = ("img", [(i, i ^ (sub << k)) for i in range(n_img)], (img // (sub << k)) % 2)
    bits = jnp.stack([core, links[0][2], links[1][2], links[2][2]])
    at_core, at_x = jnp.reshape(core, (1,)), jnp.reshape(x_bit, (1,))
    all_valid = jnp.full((1,), C, jnp.int32)
    p = dict(
        ln1_gain=ln1_gain, ln1_bias=ln1_bias, w_qkv=w_qkv, b_query=b_query, b_value=b_value,
        w_out=w_out, b_out=b_out, ln2_gain=ln2_gain, ln2_bias=ln2_bias, w_up=w_up, b_up=b_up,
        w_down=w_down, b_down=b_down,
    )

    def over(way, a):
        return lax.ppermute(a, "win", [(i, i ^ way) for i in range(4)])

    def swap(a):
        return over(1, a)

    table = jnp.pad(bias_table.transpose(0, 2, 1), ((0, 0), (0, 0), (0, TABLE - 169)))
    bias = window_bias(table)

    mine, other = crop_rows(at_core, all_valid, tokens[:, 0].transpose(1, 0, 2))
    near, far = swap(other), (over(2, mine), over(3, other))
    ct_mine, ct_other = crop_rows(at_core, crop_count, cotangent[:, 0].transpose(1, 0, 2), (mine,))
    ct_near, ct_far = swap(ct_other), (over(2, ct_mine), over(3, ct_other))
    fwd0 = block_fwd(0, (at_x, mine, near), bias, p, 0, (ct_mine,))
    fwd0 = block_fwd(0, (at_x, *far), bias, p, 1, fwd0)
    fwd1 = block_fwd(1, (at_core, fwd0[8]), bias, p)
    z0, h0, qkvc0, o0, y0, h20, g0, gp0, _ = fwd0
    z1, h1, qkvc1, o1, y1, h21, g1, gp1, zn = fwd1

    def stream(first, extra=0):
        return Halving([k for k in (2, 1, 0) if k != first], links, extra)

    down1, up1, att1, down0, up0 = (stream(k) for k in (0, 1, 0, 1, 0))
    mlp1, mlp0 = (Halving([], links) for _ in range(2))
    att0 = [stream(0, 1), stream(0)]

    dd1, da1, dy, sv_m1, *part = mlp_back(
        1, at_x, at_core, (ct_mine, ct_near, *ct_far), y1, gp1, g1, h21, p, (zn,)
    )
    down_x, up_x = (swap(a) for a in part)
    r31, sv_a1, table1, grad1, *part = attn_back(
        1, at_x, at_core, dy, qkvc1, z1, h1, o1, bias, p, (), (part[0],)
    )
    att_x = [swap(a) for a in part]
    last = down1.send(0, *down_mine(bits, dd1, g1, down_x, 0, (sv_a1,)))
    last = up1.send(1, *up_mine(bits, h21, da1, up_x, 1, (last,)))

    dd0, da0, dy, sv_m0, *part = mlp_back(0, at_x, at_core, (grad1,), y0, gp0, g0, h20, p, (last, *att_x))
    last, *part = steps((down1, 1), (up1, 0), after=(sv_m0,), through=part)
    down_x, up_x = (swap(a) for a in part)
    last = att1.send(0, *attn_mine(bits, h1, o1, r31, att_x, 0, (0, 1), None, (last,)))
    out_mine, out_other = own_quadrants(at_x, zn, True, (last,))
    out_x = swap(out_other)
    last = join_steps(mlp1, (up1, 2), (down1, 2), after=(out_mine,))
    last = down0.send(1, *down_mine(bits, dd0, g0, down_x, 1, (last,)))
    last = up0.send(0, *up_mine(bits, h20, da0, up_x, 0, (last,)))
    r30, sv_a0, small, grad0, *part = attn_back(
        0, at_x, at_core, dy, qkvc0, z0, h0, o0, bias, p, (sv_m0, sv_a1, sv_m1, table1), (last,)
    )
    last, small, *part = steps(
        (down0, 0), (up0, 1), (att1, 1), after=(sv_a0, mlp1.recv), through=(small, *part)
    )
    att_x = [swap(a) for a in part]
    small = [small, swap(small)]
    block_out = token_major(at_core, crop_count, out_mine, out_x, (last,))
    in_mine, in_other = own_quadrants(at_x, grad0, False, (block_out,))
    in_x = swap(in_other)
    last = in_mine
    kept, out = attn_mine(bits, h0, o0, r30, att_x, 0, (0,), small, (last,))
    last = att0[0].send(0, kept, out)
    last = join_steps(mlp0, (up0, 2), (down0, 2), after=(last,))
    kept, out = attn_mine(bits, h0, o0, r30, att_x, 0, (1,), None, (last,))
    last = att0[1].send(0, kept, out)
    last = att0[0].step(1, (last,))
    last = att1.step(2, (last,))
    last = att0[1].step(1, (last,))
    last = att0[0].step(2, (last, mlp0.recv))
    last = att0[1].step(2, (last,))
    grad_tokens = crop_major(at_core, in_mine, in_x, (last,))

    g_qkv, g_out, g_up, g_down, small = last_sums(
        (mlp0.pair(), mlp1.pair()), [a.pair() for a in att0], att1.pair(), (grad_tokens,)
    )
    for k in range(sub.bit_length() - 1):
        small = small + lax.ppermute(small, "img", [(i, i ^ (1 << k)) for i in range(n_img)])
    g_qkv, g_out, g_up = (scatter_rest(g, 1, img, sub) for g in (g_qkv, g_out, g_up))
    g_down = scatter_rest(g_down, 2, img, sub).transpose(0, 2, 1)
    table = small[48:, :169].reshape(2, PER, NG, 169).transpose(0, 3, 2, 1).reshape(2, 169, HEADS)
    width = D // n_img

    vectors = jnp.concatenate([small[:24], small[24:48]], axis=1).reshape(2, 12, D)
    mine = lax.dynamic_slice_in_dim(vectors[:, :8], img * width, width, 2)
    up_bias = lax.dynamic_slice_in_dim(vectors[:, 8:].reshape(2, FF), img * (4 * width), 4 * width, 1)

    return (
        block_out.transpose(1, 0, 2)[:, None], grad_tokens.reshape(C, 1, T, D), mine[:, 0], mine[:, 1], g_qkv, mine[:, 2], mine[:, 3], table,
        g_out, mine[:, 6], mine[:, 4], mine[:, 5], g_up, up_bias, g_down, mine[:, 7],
    )


def solution(mesh):
    shard = P("img", "win", None, None)
    vec, mat = P(None, "img"), P(None, "img", "win")
    return jax.shard_map(
        functools.partial(per_device, n_img=mesh.shape["img"]),
        mesh=mesh,
        in_specs=(shard, P("img")) + (P(),) * 14 + (shard,),
        out_specs=(shard, shard, vec, vec, mat, vec, vec, P(), mat, vec, vec, vec, mat, vec, mat, vec),
        check_vma=False,
    )
```

```python
import functools

import jax
import jax.numpy as jnp
from jax import lax
from jax.experimental import pallas as pl
from jax.experimental.pallas import tpu as pltpu
from jax.sharding import PartitionSpec as P

HEADS = 24
HD = 32
SIDE = 7
T = SIDE * SIDE
TP = 56
TQ = 64
D = 768
FF = 3072
C = 8
ROWS = T * C
PAD_ROWS = TQ * C
HALF = C // 2
PIECE = T * HALF
LANE = 128
NG = D // LANE
PER = LANE // HD
GT = PER * TQ
EPSILON = 1e-05
SCALE = HD ** (-0.5)
NEG = -1e30
QCH = 768
FCH = 1536
WIN = 4
N_Q = 3 * D // QCH
N_F = FF // FCH
W_UP = D // 2
MINE = D // 4
VMEM_OF = {"forwar": 48 << 20, "mlp_ba": 48 << 20, "attn_b": 44 << 20, "attn_m": 24 << 20}
VMEM_SMALL = 24 << 20
COST = 0.4
F32 = jnp.float32
BF16 = jnp.bfloat16

TAIL_K = 0.3
TAIL = (
    0.11963200491345692,
    0.12071217642148169,
    0.10017566554041868,
    0.12769280877164998,
    -0.052036176065482394,
    0.20455934198696718,
    -0.15616004916725648,
    0.035424145900813254,
)
INV_SQRT_2PI = 0.3989422804014327

def nt(left, right):
    return lax.dot_general(left, right, (((1,), (1,)), ((), ())), preferred_element_type=F32)


def tn(left, right):
    return lax.dot_general(left, right, (((0,), (0,)), ((), ())), preferred_element_type=F32)


def nn(left, right):
    return jnp.dot(left, right, preferred_element_type=F32)


def norm_parts(values):
    average = jnp.mean(values, axis=-1, keepdims=True)
    centered = values - average
    inverse = lax.rsqrt(jnp.mean(centered * centered, axis=-1, keepdims=True) + EPSILON)
    return centered * inverse, inverse


def norm_back(grad_out, normed, inverse, gain):
    scaled = grad_out * gain
    return inverse * (
        scaled
        - jnp.mean(scaled, axis=-1, keepdims=True)
        - normed * jnp.mean(scaled * normed, axis=-1, keepdims=True)
    )


def gelu_parts(a):
    bell = jnp.exp(-0.5 * a * a)
    size = jnp.abs(a)
    t = 1.0 / (1.0 + TAIL_K * size)
    poly = jnp.full_like(t, TAIL[-1])
    for coef in TAIL[-2::-1]:
        poly = poly * t + coef
    tail = bell * (t * poly)
    phi = jnp.where(a < 0, tail, 1.0 - tail)
    return a * phi, phi + a * (INV_SQRT_2PI * bell)


def head_masks(rows):
    lanes = lax.broadcasted_iota(jnp.int32, (rows, LANE), 1)
    return [(lanes >= HD * h) & (lanes < HD * (h + 1)) for h in range(PER)]


def spread(values, ones):
    return jnp.concatenate([values * m for m in ones], axis=0)


def gather_heads(stacked, masks):
    out = stacked[(PER - 1) * TQ : (PER - 1) * TQ + TP]
    for h in range(PER - 2, -1, -1):
        out = jnp.where(masks[h], stacked[h * TQ : h * TQ + TP], out)
    return out


def soft(scores):
    e = jnp.exp(scores - jnp.max(scores, axis=0, keepdims=True))
    return e * (1.0 / jnp.sum(e, axis=0, keepdims=True))


def colsum(values):
    return jnp.sum(values, axis=0, keepdims=True)


def rows_of(w, n, stride=C):
    return pl.ds(w, n, stride=stride) if n > 1 else pl.ds(w, 1)


WHOLE = T // 8 * 8


def move_rows(dest, g, to, to_stride, src, first, stride, scale=None):
    for start, n in ((0, WHOLE), (WHOLE, T - WHOLE)):
        v = src[g, rows_of(first + stride * start, n, stride), :]
        dest[g, rows_of(to + to_stride * start, n, to_stride), :] = v if scale is None else v * scale


def lanes_at(n, width):
    return pl.ds(pl.multiple_of(n * width, width), width)


def put_rolled(dest, source, a, back):
    shift, kept = (-3, range(3, 7)) if back else (3, range(0, 4))
    for i in range(SIDE):
        for j in range(SIDE):
            half = a if i in kept else 1 - a
            tile = source[half, SIDE * ((i + shift) % SIDE) + (j + shift) % SIDE]
            if j not in kept:
                tile = pltpu.roll(tile, HALF, 0)
            t = SIDE * i + j
            dest[C * t : C * (t + 1), :] = tile


ANY = pl.BlockSpec(memory_space=pl.ANY)
VM = pl.BlockSpec(memory_space=pltpu.VMEM)
SM = pl.BlockSpec(memory_space=pltpu.SMEM)


def cost(micros):
    return pl.CostEstimate(flops=int(micros * COST * 1.15e9), bytes_accessed=0, transcendentals=0)


def shape(dims, dtype):
    return jax.ShapeDtypeStruct(dims, dtype)


def fixed(dims, single=False):
    mode = dict(pipeline_mode=pl.Buffered(1)) if single else {}
    return pl.BlockSpec(dims, lambda *_: (0,) * len(dims), **mode)


def per_half(dims):
    return pl.BlockSpec((1, *dims), lambda a, *_: (a, *(0,) * len(dims)))


def call(body, args, in_specs, outs, out_specs, estimate, name, after=(), grid=(), scalars=0, scratch=(), reuse=0):
    n_in, n_after = len(args), len(after)

    def wrapped(*refs):
        return body(*refs[:n_in], *refs[n_in + n_after :])

    return pl.pallas_call(
        wrapped,
        grid_spec=pltpu.PrefetchScalarGridSpec(
            num_scalar_prefetch=scalars,
            grid=grid,
            in_specs=list(in_specs) + [ANY] * n_after,
            out_specs=out_specs,
            scratch_shapes=list(scratch),
        ),
        out_shape=outs,
        input_output_aliases={n_in + k: k for k in range(reuse)},
        compiler_params=pltpu.CompilerParams(vmem_limit_bytes=VMEM_OF.get(name[:6], VMEM_SMALL)),
        cost_estimate=estimate,
        name=name,
    )(*args, *after)


def crop_rows(core, count, crops, after=()):
    def body(at, n, src, mine, other, s):
        wide = src[...].astype(F32).reshape(ROWS, D)
        for g in range(NG):
            s[g] = wide[:, LANE * g : LANE * (g + 1)]
        for k in range(HALF):
            for out, c in ((mine, at[0]), (other, 1 - at[0])):
                crop = HALF * c + k
                keep = jnp.where(crop < n[0], 1.0, 0.0).astype(F32)
                for g in range(NG):
                    move_rows(out, g, k, HALF, s, crop, C, keep)

    return call(
        body, (core, count, crops), [SM, SM, VM], [shape((NG, PIECE, LANE), F32)] * 2, [VM] * 2, cost(2.5), "crop_rows", after, scratch=[pltpu.VMEM((NG, ROWS, LANE), F32)],
    )


def weave(dest, pieces):
    for b, piece in enumerate(pieces):
        for k in range(HALF):
            for g in range(NG):
                move_rows(dest, g, HALF * b + k, C, piece, k, HALF)


def own_quadrants(x_at, both_halves, rolled, after=()):
    def body(x, src, mine, other, full, s):
        if rolled:
            put_rolled(full, src, x[0], True)
        else:
            full[...] = src[x[0]].reshape(ROWS, D)
        for g in range(NG):
            s[g] = full[:, LANE * g : LANE * (g + 1)]
        for b, out in enumerate((mine, other)):
            for k in range(HALF):
                for g in range(NG):
                    move_rows(out, g, k, HALF, s, HALF * b + k, C)

    return call(
        body, (x_at, both_halves), [SM, VM], [shape((NG, PIECE, LANE), F32)] * 2, [VM] * 2, cost(3), "own_quadrants", after, scratch=[pltpu.VMEM((ROWS, D), F32), pltpu.VMEM((NG, ROWS, LANE), F32)],
    )


def token_major(core, count, mine, theirs, after=()):
    def body(at, n, a, b, out, s):
        for k in range(HALF):
            for src, c in ((a, at[0]), (b, 1 - at[0])):
                crop = HALF * c + k
                keep = jnp.where(crop < n[0], 1.0, 0.0).astype(F32)
                for g in range(NG):
                    move_rows(s, g, crop, C, src, k, HALF, keep)
        for g in range(NG):
            out[:, :, LANE * g : LANE * (g + 1)] = s[g].reshape(T, C, LANE).astype(BF16)

    return call(
        body, (core, count, mine, theirs), [SM, SM, VM, VM], shape((T, C, D), BF16), VM, cost(2.5), "token_major", after, scratch=[pltpu.VMEM((NG, ROWS, LANE), F32)],
    )


def crop_major(core, mine, theirs, after=()):
    def body(at, a, b, out):
        for k in range(HALF):
            for src, c in ((a, at[0]), (b, 1 - at[0])):
                for g in range(NG):
                    for start, n in ((0, WHOLE), (WHOLE, T - WHOLE)):
                        to = (HALF * c + k) * (T * NG) + g + NG * start
                        out[rows_of(to, n, NG), :] = src[g, rows_of(k + HALF * start, n, HALF), :]

    return call(
        body, (core, mine, theirs), [SM, VM, VM], shape((C * T * NG, LANE), F32), VM, cost(2.5), "crop_major", after,
    )


def fwd_body(b, which, *refs):
    a = pl.program_id(0)
    if b == 0:
        at_x, p0, p1, *rest = refs
    else:
        core, src, *rest = refs
    (
        bias, ln1g, ln1b, bq, bv, bout, ln2g, ln2b, bup, bdown,
        wqkv_h, wout_h, wup_h, wdown_h,
        z_h, h_h, qkvc_h, o_h, y_h, h2_h, g_h, gp_h, zn_o,
        wqkv, wout, wup, wdown, qkv_s, o_s, bqkv, bias_s,
        z_o, h_o, qkvc_o, o_o, y_o, h2_o, g_o, gp_o, sem_q, sem_o, sem_u, sem_d, sem_out,
    ) = rest
    at = at_x[0] ^ which if b == 0 else a
    results = (
        (z_o, z_h), (h_o, h_h), (qkvc_o, qkvc_h), (o_o, o_h), (y_o, y_h), (h2_o, h2_h), (g_o, g_h), (gp_o, gp_h),
    )

    def out(k):
        return pltpu.make_async_copy(results[k][0].at[0], results[k][1].at[at], sem_out.at[k])

    def free(k):
        @pl.when(a > 0)
        def _():
            out(k).wait()

    def cp_q(n):
        return pltpu.make_async_copy(
            wqkv_h.at[b, :, lanes_at(n, QCH)], wqkv.at[:, lanes_at(n, QCH)], sem_q.at[n]
        )

    def cp_u(n):
        return pltpu.make_async_copy(
            wup_h.at[b, :, lanes_at(n, FCH)], wup.at[:, lanes_at(n, FCH)], sem_u.at[n]
        )

    def cp_d(n):
        return pltpu.make_async_copy(
            wdown_h.at[b, lanes_at(n, FCH), :], wdown.at[lanes_at(n, FCH), :], sem_d.at[n]
        )

    cp_o = pltpu.make_async_copy(wout_h.at[b], wout, sem_o)

    def wait(copy):
        @pl.when(a == 0)
        def _():
            copy.wait()

    @pl.when(a == 0)
    def _():
        for n in range(N_Q):
            cp_q(n).start()
        cp_o.start()
        for n in range(N_F):
            cp_u(n).start()
            cp_d(n).start()
        bqkv[:, 0:D] = bq[b : b + 1, :]
        bqkv[:, D : 2 * D] = jnp.zeros((1, D), F32)
        bqkv[:, 2 * D :] = bv[b : b + 1, :]
        qkv_s[:, ROWS:, :] = jnp.zeros((3 * NG, PAD_ROWS - ROWS, LANE), F32)

    free(0)
    if b == 0:
        weave(o_s, (p0, p1))
        for g in range(NG):
            z_o[0, :, LANE * g : LANE * (g + 1)] = o_s[g, 0:ROWS, :]
    else:
        put_rolled(z_o.at[0], src, a, False)
        for w in range(2):
            mask = shift_mask(a, core[0] ^ w)
            for g in range(NG):
                bias_s[w * NG + g] = bias[NG + g] + mask
    out(0).start()
    normed, _ = norm_parts(z_o[0])
    free(1)
    h_o[0] = (normed * ln1g[b : b + 1, :] + ln1b[b : b + 1, :]).astype(BF16)
    out(1).start()

    def qkv_step(n, _):
        wait(cp_q(n))
        joint = nn(h_o[0], wqkv[:, lanes_at(n, QCH)]) + bqkv[:, lanes_at(n, QCH)]
        joint = joint * jnp.where(n < D // QCH, SCALE, 1.0)
        joint = joint.astype(BF16).astype(F32)
        for k in range(QCH // LANE):
            qkv_s[n * (QCH // LANE) + k, 0:ROWS, :] = joint[:, LANE * k : LANE * (k + 1)]
        return 0

    lax.fori_loop(0, N_Q, qkv_step, 0)
    masks = head_masks(TP)
    ones = [m.astype(F32).astype(BF16) for m in head_masks(TQ)]

    def attend(step, _):
        items = [(step * WIN + i, g) for i in range(WIN) for g in range(NG)]
        qs = [qkv_s[g, rows_of(w, TQ), :].astype(BF16) for w, g in items]
        ks = [qkv_s[NG + g, rows_of(w, TP), :].astype(BF16) for w, g in items]
        vs = [qkv_s[2 * NG + g, rows_of(w, TP), :].astype(BF16) for w, g in items]
        for (w, g), q, k, v in zip(items, qs, ks, vs):
            qkvc_o[0, w, g] = q
            qkvc_o[0, w, NG + g, 0:TP] = k
            qkvc_o[0, w, 2 * NG + g, 0:TP] = v
        added = [bias[g] if b == 0 else bias_s[w // HALF * NG + g] for w, g in items]
        scores = [nt(k, spread(q, ones)) + extra for k, q, extra in zip(ks, qs, added)]
        probs = [soft(score).astype(BF16) for score in scores]
        for (w, g), prob, v in zip(items, probs, vs):
            o_s[g, rows_of(w, TP), :] = gather_heads(tn(prob, v), masks)
        return 0

    free(2)
    lax.fori_loop(0, C // WIN, attend, 0, unroll=2)
    out(2).start()
    free(3)
    for g in range(NG):
        o_o[0, :, LANE * g : LANE * (g + 1)] = o_s[g, 0:ROWS, :].astype(BF16)
    out(3).start()
    wait(cp_o)
    free(4)
    y_o[0] = z_o[0] + (nn(o_o[0], wout[...]) + bout[b : b + 1, :])
    out(4).start()
    normed, _ = norm_parts(y_o[0])
    free(5)
    h2_o[0] = (normed * ln2g[b : b + 1, :] + ln2b[b : b + 1, :]).astype(BF16)
    out(5).start()
    free(6)
    free(7)
    def mlp_step(n, _):
        wait(cp_u(n))
        up = nn(h2_o[0], wup[:, lanes_at(n, FCH)]) + bup[b : b + 1, lanes_at(n, FCH)]
        act, slope = gelu_parts(up)
        g_o[0, :, lanes_at(n, FCH)] = act.astype(BF16)
        gp_o[0, :, lanes_at(n, FCH)] = slope.astype(BF16)
        return 0

    lax.fori_loop(0, N_F, mlp_step, 0)
    out(6).start()
    out(7).start()
    for n in range(N_F):
        wait(cp_d(n))
    zn_o[0] = (y_o[0] + (nn(g_o[0], wdown[...]) + bdown[b : b + 1, :])).reshape(T, C, D)

    @pl.when(a == pl.num_programs(0) - 1)
    def _():
        for k in range(len(results)):
            out(k).wait()


def block_fwd(b, sources, bias, p, which=None, after=()):
    outs = [
        shape((2, ROWS, D), F32),
        shape((2, ROWS, D), BF16),
        shape((2, C, 3 * NG, TQ, LANE), BF16),
        shape((2, ROWS, D), BF16),
        shape((2, ROWS, D), F32),
        shape((2, ROWS, D), BF16),
        shape((2, ROWS, FF), BF16),
        shape((2, ROWS, FF), BF16),
        shape((2, T, C, D), F32),
    ]
    if b == 0:
        specs = [fixed((NG, PIECE, LANE), True)] * 2
        out_specs = [pl.BlockSpec((1, T, C, D), lambda a, s: (s[0] ^ which, 0, 0, 0))]
    else:
        specs = [SM, fixed((2, T, C, D), True)]
        out_specs = [per_half((T, C, D))]
    small = (bias, p["ln1_gain"], p["ln1_bias"], p["b_query"], p["b_value"], p["b_out"],
             p["ln2_gain"], p["ln2_bias"], p["b_up"], p["b_down"])
    big = (p["w_qkv"], p["w_out"], p["w_up"], p["w_down"])
    return call(
        functools.partial(fwd_body, b, which),
        (*sources, *small, *big),
        specs + [fixed(v.shape, True) for v in small] + [ANY] * 4,
        outs,
        [ANY] * 8 + out_specs,
        cost(21 if which is not None else 36),
        f"forward_{b}",
        after,
        grid=(2 if which is None else 1,),
        scalars=int(which is not None),
        reuse=len(outs) if which == 1 else 0,
        scratch=[
            pltpu.VMEM((D, 3 * D), BF16),
            pltpu.VMEM((D, D), BF16),
            pltpu.VMEM((D, FF), BF16),
            pltpu.VMEM((FF, D), BF16),
            pltpu.VMEM((3 * NG, PAD_ROWS, LANE), F32),
            pltpu.VMEM((NG, PAD_ROWS, LANE), F32),
            pltpu.VMEM((1, 3 * D), F32),
            pltpu.VMEM((2 * NG, TP, GT), F32),
            *(pltpu.VMEM((1, *o.shape[1:]), o.dtype) for o in outs[:8]),
            pltpu.SemaphoreType.DMA((N_Q,)),
            pltpu.SemaphoreType.DMA,
            pltpu.SemaphoreType.DMA((N_F,)),
            pltpu.SemaphoreType.DMA((N_F,)),
            pltpu.SemaphoreType.DMA((8,)),
        ],
    )


def mlp_back_body(b, x_at, core, *refs):
    if b == 1:
        (*pieces, y, gp, act, hid, ln2g,
         wdown_h, wup_h, dd_o, da_o, dy_o, sv_o, down_o, up_o,
         wdown, wup, dz, dd, da_s, src, woven, sem_d, sem_u) = refs
    else:
        (src, y, gp, act, hid, ln2g,
         wdown_h, wup_h, dd_o, da_o, dy_o, sv_o, down_o, up_o,
         wdown, wup, dz, dd, da_s, sem_d, sem_u) = refs
    a = pl.program_id(0)

    def cp_u(n):
        return pltpu.make_async_copy(
            wup_h.at[b, :, lanes_at(n, D)], wup.at[:, lanes_at(n, D)], sem_u.at[n]
        )

    def cp_d(n):
        return pltpu.make_async_copy(
            wdown_h.at[b, lanes_at(n, D), :], wdown.at[lanes_at(n, D), :], sem_d.at[n]
        )

    def wait(copy):
        @pl.when(a == 0)
        def _():
            copy.wait()

    @pl.when(a == 0)
    def _():
        for n in range(4):
            cp_d(n).start()
            cp_u(n).start()
        sv_o[...] = jnp.zeros_like(sv_o)
        if b == 1:
            for k in range(2):
                weave(woven, pieces[2 * k : 2 * k + 2])
                for g in range(NG):
                    src[x_at[0] ^ k, :, :, LANE * g : LANE * (g + 1)] = woven[g].reshape(T, C, LANE)

    put_rolled(dz, src, a, b == 0)
    low = dz[...].astype(BF16)
    dd[...] = low
    sv_o[3:4, :] += colsum(low.astype(F32))
    for x in range(2):

        @pl.when(x_at[0] == x)
        def _():
            for c in range(2):
                w = 2 * x + c
                dd_o[c, 0] = dd[:, MINE * w : MINE * (w + 1)]

    def step(n, _):
        wait(cp_d(n))
        grad_act = nt(dd[...], wdown[lanes_at(n, D), :])
        da = (grad_act * gp[0, :, lanes_at(n, D)].astype(F32)).astype(BF16)

        da_s[:, lanes_at(n, D)] = da

        @pl.when(n // 2 == x_at[0])
        def _():
            da_o[0, :, lanes_at(n % 2, D)] = da

        sv_o[pl.ds(4 + n, 1), :] += colsum(da.astype(F32))
        return 0

    lax.fori_loop(0, 4, step, 0)
    for n in range(4):
        wait(cp_u(n))
    dh2 = nt(da_s[...], wup[...])
    normed, inverse = norm_parts(y[0])
    sv_o[0:1, :] += colsum(dh2 * normed)
    sv_o[1:2, :] += colsum(dh2)
    dy = dz[...] + norm_back(dh2, normed, inverse, ln2g[b : b + 1, :])
    dy_o[0] = dy
    sv_o[2:3, :] += colsum(dy.astype(BF16).astype(F32))
    down = tn(dd_o[1 - core[0], 0], act[0])
    up = tn(hid[0], da_o[0, :, lanes_at(1 - core[0], D)])

    def put(add):
        for k in range(8):
            add_down(down_o, k, down[:, W_UP * k : W_UP * (k + 1)], add)
            rows = up[D // 8 * k : D // 8 * (k + 1)]
            up_o[k] = up_o[k] + rows if add else rows

    for half in range(2):
        pl.when(a == half)(functools.partial(put, half == 1))


def mlp_back(b, x_at, core, src, y, gp, act, hid, p, after=()):
    return call(
        functools.partial(mlp_back_body, b),
        (x_at, core, *src, y, gp, act, hid, p["ln2_gain"], p["w_down"], p["w_up"]),
        [SM, SM, *(fixed(v.shape, True) for v in src), per_half((ROWS, D)), per_half((ROWS, FF)), per_half((ROWS, FF)),
         per_half((ROWS, D)), fixed((2, D)), ANY, ANY],
        [
            shape((2, 2, ROWS, MINE), BF16),
            shape((2, ROWS, FF // 2), BF16),
            shape((2, ROWS, D), F32),
            shape((8, D), F32),
            shape((8, *BLOCK), F32),
            shape((8, *BLOCK), F32),
        ],
        [
            pl.BlockSpec((2, 1, ROWS, MINE), lambda a: (0, a, 0, 0)),
            per_half((ROWS, FF // 2)),
            per_half((ROWS, D)),
            fixed((8, D)),
            fixed((8, *BLOCK), True),
            fixed((8, *BLOCK), True),
        ],
        cost(22),
        f"mlp_back_{b}",
        after,
        grid=(2,),
        scratch=[
            pltpu.VMEM((FF, D), BF16),
            pltpu.VMEM((D, FF), BF16),
            pltpu.VMEM((ROWS, D), F32),
            pltpu.VMEM((ROWS, D), BF16),
            pltpu.VMEM((ROWS, FF), BF16),
            *([pltpu.VMEM((2, T, C, D), F32), pltpu.VMEM((NG, ROWS, LANE), F32)] if b else []),
            pltpu.SemaphoreType.DMA((4,)),
            pltpu.SemaphoreType.DMA((4,)),
        ],
    )


TABLE = 256
BLOCK = (D // 8, D)


def row_of(t):
    return sum((t >= SIDE * k).astype(jnp.int32) for k in range(1, 10))


def shift_mask(a, column):
    u = lax.broadcasted_iota(jnp.int32, (TP, GT), 0)
    t = lax.broadcasted_iota(jnp.int32, (TP, GT), 1) & (TQ - 1)
    iu, it = row_of(u), row_of(t)
    rows = (iu >= 4) != (it >= 4)
    cols = (u - SIDE * iu >= 4) != (t - SIDE * it >= 4)
    return jnp.where((rows & (a == 1)) | (cols & (column == 1)), -100.0, 0.0)


def table_sums(ds, moved):
    row = lax.broadcasted_iota(jnp.int32, (GT, PER * LANE), 0)
    col = lax.broadcasted_iota(jnp.int32, (GT, PER * LANE), 1)
    t = row & (TQ - 1)
    there = (row >> 6 == col >> 7) & (t < T) & ((col & (LANE - 1)) == t + 6 * row_of(t))
    onehot = there.astype(F32).astype(BF16)
    moved[:, NG * TP :, :] = jnp.zeros((PER, (8 - NG) * TP, LANE), F32)
    for g in range(NG):
        rest = ds[g]
        total = jnp.zeros((TP, PER * LANE), F32)
        for _ in range(3):
            part = rest.astype(BF16)
            total += nn(part, onehot)
            rest = rest - part.astype(F32)
        for h in range(PER):
            moved[h, TP * g : TP * (g + 1), :] = total[:, LANE * h : LANE * (h + 1)]


def sum_table(moved, put):
    for h in range(PER):
        total = jnp.zeros((8, TABLE), F32)
        for u in range(T):
            v = moved[h, pl.ds(u, 8, stride=TP), :]
            shift = 13 * (6 - u // SIDE) + 6 - u % SIDE
            total += pltpu.roll(jnp.concatenate([v, jnp.zeros_like(v)], axis=1), shift, 1)
        put(h, total)


def attn_back_body(b, x_at, core, dy, qkvc, z, hid, att, *refs):
    bias, ln1g, *refs = refs
    if b == 0:
        sv_m0, sv_a1, sv_m1, table1, *refs = refs
    (wout_h, wqkv_h, r3_o, sv_o, sum_o, grad_o, *part_o,
     wout, wqkv, do_s, dqkv_s, dq, bias_s, ds_o, moved, dyr, sem_o, sem_q) = refs
    a = pl.program_id(0)
    cp_o = pltpu.make_async_copy(wout_h.at[b], wout, sem_o)

    def cp_q(n):
        return pltpu.make_async_copy(
            wqkv_h.at[b, :, lanes_at(n, QCH)], wqkv.at[:, lanes_at(n, QCH)], sem_q.at[n]
        )

    def wait(copy):
        @pl.when(a == 0)
        def _():
            copy.wait()

    @pl.when(a == 0)
    def _():
        cp_o.start()
        for n in range(N_Q):
            cp_q(n).start()
        do_s[:, ROWS:, :] = jnp.zeros((NG, PAD_ROWS - ROWS, LANE), F32)
        ds_o[...] = jnp.zeros_like(ds_o)
        sv_o[...] = jnp.zeros_like(sv_o)

    if b == 1:
        for w in range(2):
            mask = shift_mask(a, core[0] ^ w)
            for g in range(NG):
                bias_s[w * NG + g] = bias[NG + g] + mask
    dyr[...] = dy[0].astype(BF16)
    wait(cp_o)
    do = nt(dyr[...], wout[...]).astype(BF16).astype(F32)
    for g in range(NG):
        do_s[g, 0:ROWS, :] = do[:, LANE * g : LANE * (g + 1)]
    masks = head_masks(TP)
    ones = [m.astype(F32).astype(BF16) for m in head_masks(TQ)]

    def attend(step, _):
        items = [(step * WIN + i, g) for i in range(WIN) for g in range(NG)]
        ks = [qkvc[0, w, NG + g, 0:TP] for w, g in items]
        q_wide = [spread(qkvc[0, w, g], ones) for w, g in items]
        do_wide = [spread(do_s[g, rows_of(w, TQ), :].astype(BF16), ones) for w, g in items]
        added = [bias[g] if b == 0 else bias_s[w // HALF * NG + g] for w, g in items]
        scores = [nt(k, q) + extra for k, q, extra in zip(ks, q_wide, added)]
        dprobs = [nt(qkvc[0, w, 2 * NG + g, 0:TP], d) for (w, g), d in zip(items, do_wide)]
        probs = [soft(score) for score in scores]
        weighted = [p * d for p, d in zip(probs, dprobs)]
        ds = [x - p * jnp.sum(x, axis=0, keepdims=True) for x, p in zip(weighted, probs)]
        for (w, g), d in zip(items, ds):
            ds_o[g] += d
        low = [d.astype(BF16) for d in ds]
        dks = [nn(x, q) for x, q in zip(low, q_wide)]
        dvs = [nn(p.astype(BF16), d) for p, d in zip(probs, do_wide)]
        dqs = [tn(x, k) for x, k in zip(low, ks)]
        for (w, g), d_q, d_k, d_v in zip(items, dqs, dks, dvs):
            dqkv_s[g, rows_of(w, TP), :] = gather_heads(d_q, masks) * SCALE
            dqkv_s[NG + g, rows_of(w, TP), :] = d_k
            dqkv_s[2 * NG + g, rows_of(w, TP), :] = d_v
        return 0

    lax.fori_loop(0, C // WIN, attend, 0)
    for g in range(3 * NG):
        dq[:, LANE * g : LANE * (g + 1)] = dqkv_s[g, 0:ROWS, :].astype(BF16)
    sv_o[2:3, :] += colsum(dq[:, 0:D].astype(F32))
    sv_o[3:4, :] += colsum(dq[:, 2 * D :].astype(F32))
    for n in range(N_Q):
        wait(cp_q(n))
    dh = nt(dq[...], wqkv[...])
    for x in range(2):

        @pl.when(x_at[0] == x)
        def _():
            for c in range(2):
                w = 2 * x + c
                r3_o[c, 0] = jnp.concatenate(
                    [dq[:, 3 * MINE * w : 3 * MINE * (w + 1)], dyr[:, MINE * w : MINE * (w + 1)]], axis=1
                )

    normed, inverse = norm_parts(z[0])
    sv_o[0:1, :] += colsum(dh * normed)
    sv_o[1:2, :] += colsum(dh)
    grad_o[0] = (dy[0] + norm_back(dh, normed, inverse, ln1g[b : b + 1, :])).reshape(T, C, D)
    other = r3_o[1 - core[0], 0]
    parts = [attn_columns(tn, hid[0], att[0], other[:, W_UP * n : W_UP * (n + 1)], W_UP * n, W_UP) for n in range(2)]

    def put_parts(add):
        for out, part in zip(part_o, parts):
            blocks = part.reshape(8, D // 8, W_UP)
            out[...] = out[...] + blocks if add else blocks

    for half in range(2):
        pl.when(a == half)(functools.partial(put_parts, half == 1))

    @pl.when(a == 1)
    def _():
        table_sums(ds_o, moved)
        if b == 1:
            sum_table(moved, lambda h, v: sum_o.__setitem__(h, v))
            return
        sum_o[...] = jnp.zeros_like(sum_o)
        for at, ref in ((0, sv_o), (4, sv_m0), (12, sv_a1), (16, sv_m1)):
            for k in range(2):
                sum_o[24 * k + at : 24 * k + at + ref.shape[0], :] = ref[:, W_UP * k : W_UP * (k + 1)]

        def put(h, v, at=48):
            sum_o[at + NG * h : at + NG * (h + 1), 0:TABLE] = v[0:NG]

        sum_table(moved, put)
        for h in range(PER):
            put(h, table1[h], 72)


def attn_back(b, x_at, core, dy, qkvc, z, hid, att, bias, p, sums=(), after=()):
    sum_shape = (PER, 8, TABLE) if b else (D // 8, W_UP)
    return call(
        functools.partial(attn_back_body, b),
        (x_at, core, dy, qkvc, z, hid, att, bias, p["ln1_gain"], *sums, p["w_out"], p["w_qkv"]),
        [SM, SM, per_half((ROWS, D)), per_half((C, 3 * NG, TQ, LANE))] + [per_half((ROWS, D))] * 3
        + [fixed(bias.shape, True), fixed((2, D)), *(fixed(v.shape) for v in sums), ANY, ANY],
        [shape((2, 2, ROWS, D), BF16), shape((4, D), F32), shape(sum_shape, F32), shape((2, T, C, D), F32)]
        + [shape((8, D // 8, W_UP), F32)] * 2,
        [
            pl.BlockSpec((2, 1, ROWS, D), lambda a: (0, a, 0, 0)),
            fixed((4, D)),
            fixed(sum_shape),
            per_half((T, C, D)),
        ]
        + [fixed((8, D // 8, W_UP), True)] * 2,
        cost(31),
        f"attn_back_{b}",
        after,
        grid=(2,),
        scratch=[
            pltpu.VMEM((D, D), BF16),
            pltpu.VMEM((D, 3 * D), BF16),
            pltpu.VMEM((NG, PAD_ROWS, LANE), F32),
            pltpu.VMEM((3 * NG, PAD_ROWS, LANE), F32),
            pltpu.VMEM((ROWS, 3 * D), BF16),
            pltpu.VMEM((2 * NG, TP, GT), F32),
            pltpu.VMEM((NG, TP, GT), F32),
            pltpu.VMEM((PER, 8 * TP, LANE), F32),
            pltpu.VMEM((ROWS, D), BF16),
            pltpu.SemaphoreType.DMA,
            pltpu.SemaphoreType.DMA((N_Q,)),
        ],
    )


def halves(left, right):
    return tn(left(0), right(0)) + tn(left(1), right(1))


def insert_bit(i, place, bit):
    return ((i >> place) << (place + 1)) | (bit << place) | (i & ((1 << place) - 1))


def row_pairs(values, k):
    height = values.shape[0] // 8
    for i in range(4):
        low = insert_bit(i, k, 0)
        high = low | (1 << k)
        yield i, low, high, values[height * low : height * (low + 1)], values[height * high : height * (high + 1)]


def put_down(out, i, total):
    half = MINE // 2
    out[i, :, 0:W_UP] = total[0:half]
    out[i, :, W_UP:] = total[half:]


def add_down(out, i, total, add):
    put_down(out, i, total + get_down(out[i]) if add else total)


def get_down(block):
    return jnp.concatenate([block[:, 0:W_UP], block[:, W_UP:]], axis=0)


def down_mine(bits, dd, act, recv, first, after=()):
    def body(s, l, rk, rs, gk, gs, keep, send):
        put_down(keep, 0, halves(lambda a: l[0, a], lambda a: rk[a]) + get_down(gk[0]))
        put_down(send, 0, halves(lambda a: l[0, a], lambda a: rs[a]) + get_down(gs[0]))

    def block(flip):
        return lambda i, s: insert_bit(i, first, s[1 + first] ^ flip)

    return call(
        body, (bits, dd, act, act, recv, recv),
        [pl.BlockSpec((1, 2, ROWS, MINE), lambda i, s: (s[0], 0, 0, 0))]
        + [pl.BlockSpec((2, ROWS, W_UP), lambda i, s, m=block(f): (0, 0, m(i, s))) for f in (0, 1)]
        + [pl.BlockSpec((1, *BLOCK), lambda i, s, m=block(f): (m(i, s), 0, 0)) for f in (0, 1)],
        [shape((4, *BLOCK), F32)] * 2, [pl.BlockSpec((1, *BLOCK), lambda i, s: (i, 0, 0))] * 2,
        cost(6.9), "down_mine", after, (4,), 1,
    )


def up_mine(bits, hid, da, recv, first, after=()):
    def body(s, l, r, got, keep, send):
        total = halves(lambda a: l[a], lambda a: r[a])
        mine = s[1 + first] == 0
        for i, j, k, p, q in row_pairs(total, first):
            p, q = p + got[j], q + got[k]
            keep[i] = jnp.where(mine, p, q)
            send[i] = jnp.where(mine, q, p)

    return call(
        body, (bits, hid, da, recv),
        [fixed((2, ROWS, D)), pl.BlockSpec((2, ROWS, W_UP), lambda n, s: (0, 0, 2 * s[0] + n)),
         pl.BlockSpec((8, D // 8, W_UP), lambda n, s: (0, 0, n))],
        [shape((4, *BLOCK), F32)] * 2, [pl.BlockSpec((4, D // 8, W_UP), lambda n, s: (0, 0, n))] * 2,
        cost(5.7), "up_mine", after, (2,), 1,
    )


def attn_columns(product, hid, att, r, lo, width):
    edge = 3 * MINE
    cut = edge // LANE * LANE
    parts = []
    if lo < cut:
        parts.append(product(hid, r[..., 0 : min(cut - lo, width)]))
    if lo + width > cut:
        lane = lax.broadcasted_iota(jnp.int32, (D, LANE), 1)
        right = r[..., cut - lo : cut - lo + LANE]
        parts.append(jnp.where(lane < edge - cut, product(hid, right), product(att, right)))
    if lo + width > cut + LANE:
        parts.append(product(att, r[..., cut - lo + LANE : width]))
    return parts[0] if len(parts) == 1 else jnp.concatenate(parts, axis=1)


def two_halves(left, right):
    return tn(left[0], right[0]) + tn(left[1], right[1])


def attn_mine(bits, hid, att, r3, recv, first, cols, small=None, after=()):
    extra = small is not None
    width = W_UP * len(cols)

    def body(s, h, o, r, *refs):
        gots, more, (keep, send) = refs[: len(cols)], refs[len(cols) : -2], refs[-2:]
        for k, n in enumerate(cols):

            @pl.when(pl.program_id(0) == k)
            def _():
                total = attn_columns(two_halves, h, o, r[0], n * W_UP, W_UP)
                mine = s[1 + first] == 0
                for i, j, jj, p, q in row_pairs(total, first):
                    p, q = p + gots[k][j], q + gots[k][jj]
                    keep[i] = jnp.where(mine, p, q)
                    send[i] = jnp.where(mine, q, p)
                if extra:
                    added = more[0][...] + more[1][...]
                    keep[4] = added
                    send[4] = added

    at = lambda n: n + cols[0]
    specs = [
        fixed((2, ROWS, D)),
        fixed((2, ROWS, D)),
        pl.BlockSpec((1, 2, ROWS, W_UP), lambda n, s: (s[0], 0, 0, at(n))),
    ]
    args = [bits, hid, att, r3]
    for n in cols:
        args.append(recv[n])
        specs.append(fixed((8, D // 8, W_UP)))
    if extra:
        args += small
        specs += [fixed((D // 8, W_UP))] * 2
    out = pl.BlockSpec((4 + extra, D // 8, W_UP), lambda n, s: (0, 0, n))
    return call(
        body, args, specs, [shape((4 + extra, D // 8, width), F32)] * 2, [out] * 2,
        cost(1.5 + 2.8 * len(cols)), "attn_mine", after, (len(cols),), 1,
    )


def split_sum(streams, extra, after=(), through=()):
    n = streams[0][1].shape[0]
    half = (n - extra) // 2

    def body(s, *refs):
        ins, outs = refs[: 4 * len(streams)], refs[4 * len(streams) + len(through) :]
        for k in range(len(streams)):
            ka, ra, kb, rb = ins[4 * k : 4 * k + 4]
            outs[2 * k][...] = ka[...] + ra[...]
            outs[2 * k + 1][...] = kb[...] + rb[...]

    args, specs = [jnp.stack([bit for *_, bit in streams])], []
    outs, out_specs = [shape(a.shape, a.dtype) for a in through], [ANY] * len(through)
    for k, (kept, recv, place, _) in enumerate(streams):
        block = (1, *recv.shape[1:])

        def at(flip, k=k, place=place, block=block):
            def index(i, s):
                j = insert_bit(i, place, s[k] ^ flip)
                return (jnp.where(i == half, 2 * half, j) if extra else j, 0, 0)

            return pl.BlockSpec(block, index)

        args += [kept, recv, kept, recv]
        specs += [at(0), at(0), at(1), at(1)]
        outs += [shape((half + extra, *recv.shape[1:]), F32)] * 2
        out_specs += [pl.BlockSpec(block, lambda i, s: (i, 0, 0))] * 2
    size = sum(recv.size for _, recv, *_ in streams)
    return call(
        body, args, specs, outs, out_specs, cost(1.5 + size * 5e-6), "split_sum", (*through, *after), (half + extra,), 1,
        reuse=len(through),
    )


def join_steps(joint, *pairs, after=()):
    kept = [s.kept for s, _ in pairs]
    recv = [s.recv for s, _ in pairs]

    def body(s, *refs):
        ins, (keep, send) = refs[:-2], refs[-2:]
        for k in range(len(pairs)):
            mine = s[k] == 0
            low, high = (ins[k][i] + ins[len(pairs) + k][i] for i in range(2))
            keep[k] = jnp.where(mine, low, high)
            send[k] = jnp.where(mine, high, low)

    bits = jnp.stack([s.links[name][2] for s, name in pairs])
    block = kept[0].shape
    keep, send = call(
        body, (bits, *kept, *recv), [fixed(block)] * (2 * len(pairs)),
        [shape((len(pairs), *block[1:]), F32)] * 2, [fixed((len(pairs), *block[1:]))] * 2,
        cost(2), "join_steps", after, (1,), 1,
    )
    joint.send(pairs[0][1], keep, send)
    return keep


def steps(*pairs, after=(), through=()):
    args = []
    for s, name in pairs:
        args.append((s.kept, s.recv, len(s.names) - 1 - s.names.index(name), s.links[name][2]))
    outs = split_sum(args, pairs[0][0].extra, after, through)
    passed, outs = outs[: len(through)], outs[len(through) :]
    for k, (s, name) in enumerate(pairs):
        s.send(name, outs[2 * k], outs[2 * k + 1])
    return (outs[0], *passed) if through else outs[0]


class Halving:
    def __init__(self, names, links, extra=0):
        self.names, self.links, self.extra = list(names), links, extra

    def send(self, name, kept, out):
        axis, perm, _ = self.links[name]
        if name in self.names:
            self.names.remove(name)
        self.kept, self.recv = kept, lax.ppermute(out, axis, perm)
        return kept

    def step(self, name, after=()):
        return steps((self, name), after=after)

    def pair(self):
        return self.kept, self.recv


def last_sums(mlps, att0, att1, after=()):
    pairs = [*mlps, *att0, att1]

    def body(*refs):
        ins, (qkv, out, up, down, small) = refs[: 2 * len(pairs)], refs[2 * len(pairs) :]
        for b in range(2):
            up[b] = ins[2 * b][0] + ins[2 * b + 1][0]
            down[b] = get_down(ins[2 * b][1] + ins[2 * b + 1][1])
        total = [ins[2 * i][0] + ins[2 * i + 1][0] for i in range(2, 5)]
        edge = 3 * MINE
        for b, att in enumerate((jnp.concatenate(total[0:2], axis=1), total[2])):
            qkv[b] = att[:, 0:edge]
            out[b] = att[:, edge:]
        small[...] = ins[4][1] + ins[5][1]

    rows = D // 8
    return call(
        body, [a for pair in pairs for a in pair], [VM] * (2 * len(pairs)),
        [shape((2, rows, 3 * MINE), F32), shape((2, rows, MINE), F32), shape((2, rows, D), F32),
         shape((2, MINE, W_UP), F32), shape((rows, W_UP), F32)],
        [VM] * 5, cost(4), "last_sums", after,
    )


def scatter_rest(block, dim, img, sub):
    step = sub // 2
    while step:
        bit = (img // step) % 2
        half = block.shape[dim] // 2
        keep = lax.dynamic_slice_in_dim(block, bit * half, half, dim)
        send = lax.dynamic_slice_in_dim(block, (1 - bit) * half, half, dim)
        perm = [(i, i ^ step) for i in range(8 * sub)]
        block = keep + lax.ppermute(send, "img", perm)
        step //= 2
    return block


def window_bias(table, after=()):
    pairs = 16

    def body(src, out, rolled, wide):
        l = lax.broadcasted_iota(jnp.int32, (LANE, GT), 0)
        t = lax.broadcasted_iota(jnp.int32, (LANE, GT), 1) & (TQ - 1)
        at = lax.broadcasted_iota(jnp.int32, (LANE, GT), 1) >> 6
        there = (t < T) & (l == t + 6 * row_of(t))
        wide[...] = jnp.zeros_like(wide)
        for h in range(PER):
            rows = [src[k // NG, PER * (k % NG) + h : PER * (k % NG) + h + 1] for k in range(2 * NG)]
            rows = jnp.concatenate(rows + [jnp.zeros((pairs - 2 * NG, TABLE), F32)], axis=0)
            for u in range(T):
                shift = 13 * (6 - u // SIDE) + 6 - u % SIDE
                rolled[pairs * u : pairs * (u + 1), :] = pltpu.roll(rows, (TABLE - shift) % TABLE, 1)[:, 0:LANE]
            ones = (there & (at == h)).astype(F32).astype(BF16)
            rest = rolled[...]
            for _ in range(3):
                part = rest.astype(BF16)
                moved = nn(part, ones)
                for k in range(2):
                    wide[k, 0 : pairs * T, :] += moved[:, LANE * k : LANE * (k + 1)]
                rest = rest - part.astype(F32)
        real = lax.broadcasted_iota(jnp.int32, (TP, LANE), 0) < T
        for b in range(2 * NG):
            for k in range(2):
                v = wide[k, pl.ds(b, TP, stride=pairs), :]
                out[b, :, LANE * k : LANE * (k + 1)] = jnp.where(real, v, NEG)

    return call(
        body, (table,), [VM], shape((2 * NG, TP, GT), F32), VM, cost(4), "window_bias", after,
        scratch=[pltpu.VMEM((pairs * T, LANE), F32), pltpu.VMEM((2, pairs * TP, LANE), F32)],
    )


def per_device(
    tokens, crop_count, ln1_gain, ln1_bias, w_qkv, b_query, b_value, bias_table, w_out, b_out,
    ln2_gain, ln2_bias, w_up, b_up, w_down, b_down, cotangent, *, n_img,
):
    win, img = lax.axis_index("win"), lax.axis_index("img")
    sub = n_img // 8
    x_bit, core = win // 2, win % 2
    links = {}
    for k in range(3):
        links[k] = ("img", [(i, i ^ (sub << k)) for i in range(n_img)], (img // (sub << k)) % 2)
    bits = jnp.stack([core, links[0][2], links[1][2], links[2][2]])
    at_core, at_x = jnp.reshape(core, (1,)), jnp.reshape(x_bit, (1,))
    all_valid = jnp.full((1,), C, jnp.int32)
    p = dict(
        ln1_gain=ln1_gain, ln1_bias=ln1_bias, w_qkv=w_qkv, b_query=b_query, b_value=b_value,
        w_out=w_out, b_out=b_out, ln2_gain=ln2_gain, ln2_bias=ln2_bias, w_up=w_up, b_up=b_up,
        w_down=w_down, b_down=b_down,
    )

    def over(way, a):
        return lax.ppermute(a, "win", [(i, i ^ way) for i in range(4)])

    def swap(a):
        return over(1, a)

    table = jnp.pad(bias_table.transpose(0, 2, 1), ((0, 0), (0, 0), (0, TABLE - 169)))
    bias = window_bias(table)

    mine, other = crop_rows(at_core, all_valid, tokens[:, 0].transpose(1, 0, 2))
    near, far = swap(other), (over(2, mine), over(3, other))
    ct_mine, ct_other = crop_rows(at_core, crop_count, cotangent[:, 0].transpose(1, 0, 2), (mine,))
    ct_near, ct_far = swap(ct_other), (over(2, ct_mine), over(3, ct_other))
    fwd0 = block_fwd(0, (at_x, mine, near), bias, p, 0, (ct_mine,))
    fwd0 = block_fwd(0, (at_x, *far), bias, p, 1, fwd0)
    fwd1 = block_fwd(1, (at_core, fwd0[8]), bias, p)
    z0, h0, qkvc0, o0, y0, h20, g0, gp0, _ = fwd0
    z1, h1, qkvc1, o1, y1, h21, g1, gp1, zn = fwd1

    def stream(first, extra=0):
        return Halving([k for k in (2, 1, 0) if k != first], links, extra)

    down1, up1, att1, down0, up0 = (stream(k) for k in (0, 1, 0, 1, 0))
    mlp1, mlp0 = (Halving([], links) for _ in range(2))
    att0 = [stream(0, 1), stream(0)]

    dd1, da1, dy, sv_m1, *part = mlp_back(
        1, at_x, at_core, (ct_mine, ct_near, *ct_far), y1, gp1, g1, h21, p, (zn,)
    )
    down_x, up_x = (swap(a) for a in part)
    r31, sv_a1, table1, grad1, *part = attn_back(
        1, at_x, at_core, dy, qkvc1, z1, h1, o1, bias, p, (), (part[0],)
    )
    att_x = [swap(a) for a in part]
    last = down1.send(0, *down_mine(bits, dd1, g1, down_x, 0, (sv_a1,)))
    last = up1.send(1, *up_mine(bits, h21, da1, up_x, 1, (last,)))

    dd0, da0, dy, sv_m0, *part = mlp_back(0, at_x, at_core, (grad1,), y0, gp0, g0, h20, p, (last, *att_x))
    last, *part = steps((down1, 1), (up1, 0), after=(sv_m0,), through=part)
    down_x, up_x = (swap(a) for a in part)
    last = att1.send(0, *attn_mine(bits, h1, o1, r31, att_x, 0, (0, 1), None, (last,)))
    out_mine, out_other = own_quadrants(at_x, zn, True, (last,))
    out_x = swap(out_other)
    last = join_steps(mlp1, (up1, 2), (down1, 2), after=(out_mine,))
    last = down0.send(1, *down_mine(bits, dd0, g0, down_x, 1, (last,)))
    last = up0.send(0, *up_mine(bits, h20, da0, up_x, 0, (last,)))
    r30, sv_a0, small, grad0, *part = attn_back(
        0, at_x, at_core, dy, qkvc0, z0, h0, o0, bias, p, (sv_m0, sv_a1, sv_m1, table1), (last,)
    )
    last, small, *part = steps(
        (down0, 0), (up0, 1), (att1, 1), after=(sv_a0, mlp1.recv), through=(small, *part)
    )
    att_x = [swap(a) for a in part]
    small = [small, swap(small)]
    block_out = token_major(at_core, crop_count, out_mine, out_x, (last,))
    in_mine, in_other = own_quadrants(at_x, grad0, False, (block_out,))
    in_x = swap(in_other)
    last = in_mine
    kept, out = attn_mine(bits, h0, o0, r30, att_x, 0, (0,), small, (last,))
    last = att0[0].send(0, kept, out)
    last = join_steps(mlp0, (up0, 2), (down0, 2), after=(last,))
    kept, out = attn_mine(bits, h0, o0, r30, att_x, 0, (1,), None, (last,))
    last = att0[1].send(0, kept, out)
    last = att0[0].step(1, (last,))
    last = att1.step(2, (last,))
    last = att0[1].step(1, (last,))
    last = att0[0].step(2, (last, mlp0.recv))
    last = att0[1].step(2, (last,))
    grad_tokens = crop_major(at_core, in_mine, in_x, (last,))

    g_qkv, g_out, g_up, g_down, small = last_sums(
        (mlp0.pair(), mlp1.pair()), [a.pair() for a in att0], att1.pair(), (grad_tokens,)
    )
    for k in range(sub.bit_length() - 1):
        small = small + lax.ppermute(small, "img", [(i, i ^ (1 << k)) for i in range(n_img)])
    g_qkv, g_out, g_up = (scatter_rest(g, 1, img, sub) for g in (g_qkv, g_out, g_up))
    g_down = scatter_rest(g_down, 2, img, sub).transpose(0, 2, 1)
    table = small[48:, :169].reshape(2, PER, NG, 169).transpose(0, 3, 2, 1).reshape(2, 169, HEADS)
    width = D // n_img

    vectors = jnp.concatenate([small[:24], small[24:48]], axis=1).reshape(2, 12, D)
    mine = lax.dynamic_slice_in_dim(vectors[:, :8], img * width, width, 2)
    up_bias = lax.dynamic_slice_in_dim(vectors[:, 8:].reshape(2, FF), img * (4 * width), 4 * width, 1)

    return (
        block_out.transpose(1, 0, 2)[:, None], grad_tokens.reshape(C, 1, T, D), mine[:, 0], mine[:, 1], g_qkv, mine[:, 2], mine[:, 3], table,
        g_out, mine[:, 6], mine[:, 4], mine[:, 5], g_up, up_bias, g_down, mine[:, 7],
    )


def solution(mesh):
    shard = P("img", "win", None, None)
    vec, mat = P(None, "img"), P(None, "img", "win")
    return jax.shard_map(
        functools.partial(per_device, n_img=mesh.shape["img"]),
        mesh=mesh,
        in_specs=(shard, P("img")) + (P(),) * 14 + (shard,),
        out_specs=(shard, shard, vec, vec, mat, vec, vec, P(), mat, vec, vec, vec, mat, vec, mat, vec),
        check_vma=False,
    )
```

```python
import functools

import jax
import jax.numpy as jnp
from jax import lax
from jax.experimental import pallas as pl
from jax.experimental.pallas import tpu as pltpu
from jax.sharding import PartitionSpec as P

HEADS = 24
HD = 32
SIDE = 7
T = SIDE * SIDE
TP = 56
TQ = 64
D = 768
FF = 3072
C = 8
ROWS = T * C
PAD_ROWS = TQ * C
HALF = C // 2
PIECE = T * HALF
LANE = 128
NG = D // LANE
PER = LANE // HD
GT = PER * TQ
EPSILON = 1e-05
SCALE = HD ** (-0.5)
NEG = -1e30
QCH = 768
FCH = 1536
WIN = 4
N_Q = 3 * D // QCH
N_F = FF // FCH
W_UP = D // 2
MINE = D // 4
VMEM_OF = {"forwar": 48 << 20, "mlp_ba": 48 << 20, "attn_b": 44 << 20, "attn_m": 24 << 20}
VMEM_SMALL = 24 << 20
COST = 0.4
F32 = jnp.float32
BF16 = jnp.bfloat16

TAIL_K = 0.3
TAIL = (
    0.11963200491345692,
    0.12071217642148169,
    0.10017566554041868,
    0.12769280877164998,
    -0.052036176065482394,
    0.20455934198696718,
    -0.15616004916725648,
    0.035424145900813254,
)
INV_SQRT_2PI = 0.3989422804014327

def nt(left, right):
    return lax.dot_general(left, right, (((1,), (1,)), ((), ())), preferred_element_type=F32)


def tn(left, right):
    return lax.dot_general(left, right, (((0,), (0,)), ((), ())), preferred_element_type=F32)


def nn(left, right):
    return jnp.dot(left, right, preferred_element_type=F32)


def norm_parts(values):
    average = jnp.mean(values, axis=-1, keepdims=True)
    centered = values - average
    inverse = lax.rsqrt(jnp.mean(centered * centered, axis=-1, keepdims=True) + EPSILON)
    return centered * inverse, inverse


def norm_back(grad_out, normed, inverse, gain):
    scaled = grad_out * gain
    return inverse * (
        scaled
        - jnp.mean(scaled, axis=-1, keepdims=True)
        - normed * jnp.mean(scaled * normed, axis=-1, keepdims=True)
    )


def gelu_parts(a):
    bell = jnp.exp(-0.5 * a * a)
    size = jnp.abs(a)
    t = 1.0 / (1.0 + TAIL_K * size)
    poly = jnp.full_like(t, TAIL[-1])
    for coef in TAIL[-2::-1]:
        poly = poly * t + coef
    tail = bell * (t * poly)
    phi = jnp.where(a < 0, tail, 1.0 - tail)
    return a * phi, phi + a * (INV_SQRT_2PI * bell)


def head_masks(rows):
    lanes = lax.broadcasted_iota(jnp.int32, (rows, LANE), 1)
    return [(lanes >= HD * h) & (lanes < HD * (h + 1)) for h in range(PER)]


def spread(values, ones):
    return jnp.concatenate([values * m for m in ones], axis=0)


def gather_heads(stacked, masks):
    out = stacked[(PER - 1) * TQ : (PER - 1) * TQ + TP]
    for h in range(PER - 2, -1, -1):
        out = jnp.where(masks[h], stacked[h * TQ : h * TQ + TP], out)
    return out


def soft(scores):
    e = jnp.exp(scores - jnp.max(scores, axis=0, keepdims=True))
    return e * (1.0 / jnp.sum(e, axis=0, keepdims=True))


def colsum(values):
    return jnp.sum(values, axis=0, keepdims=True)


def rows_of(w, n, stride=C):
    return pl.ds(w, n, stride=stride) if n > 1 else pl.ds(w, 1)


WHOLE = T // 8 * 8


def move_rows(dest, g, to, to_stride, src, first, stride, scale=None):
    for start, n in ((0, WHOLE), (WHOLE, T - WHOLE)):
        v = src[g, rows_of(first + stride * start, n, stride), :]
        dest[g, rows_of(to + to_stride * start, n, to_stride), :] = v if scale is None else v * scale


def lanes_at(n, width):
    return pl.ds(pl.multiple_of(n * width, width), width)


def put_rolled(dest, source, a, back):
    shift, kept = (-3, range(3, 7)) if back else (3, range(0, 4))
    for i in range(SIDE):
        for j in range(SIDE):
            half = a if i in kept else 1 - a
            tile = source[half, SIDE * ((i + shift) % SIDE) + (j + shift) % SIDE]
            if j not in kept:
                tile = pltpu.roll(tile, HALF, 0)
            t = SIDE * i + j
            dest[C * t : C * (t + 1), :] = tile


ANY = pl.BlockSpec(memory_space=pl.ANY)
VM = pl.BlockSpec(memory_space=pltpu.VMEM)
SM = pl.BlockSpec(memory_space=pltpu.SMEM)


def cost(micros):
    return pl.CostEstimate(flops=int(micros * COST * 1.15e9), bytes_accessed=0, transcendentals=0)


def shape(dims, dtype):
    return jax.ShapeDtypeStruct(dims, dtype)


def fixed(dims, single=False):
    mode = dict(pipeline_mode=pl.Buffered(1)) if single else {}
    return pl.BlockSpec(dims, lambda *_: (0,) * len(dims), **mode)


def per_half(dims):
    return pl.BlockSpec((1, *dims), lambda a, *_: (a, *(0,) * len(dims)))


def call(body, args, in_specs, outs, out_specs, estimate, name, after=(), grid=(), scalars=0, scratch=(), reuse=0):
    n_in, n_after = len(args), len(after)

    def wrapped(*refs):
        return body(*refs[:n_in], *refs[n_in + n_after :])

    return pl.pallas_call(
        wrapped,
        grid_spec=pltpu.PrefetchScalarGridSpec(
            num_scalar_prefetch=scalars,
            grid=grid,
            in_specs=list(in_specs) + [ANY] * n_after,
            out_specs=out_specs,
            scratch_shapes=list(scratch),
        ),
        out_shape=outs,
        input_output_aliases={n_in + k: k for k in range(reuse)},
        compiler_params=pltpu.CompilerParams(vmem_limit_bytes=VMEM_OF.get(name[:6], VMEM_SMALL)),
        cost_estimate=estimate,
        name=name,
    )(*args, *after)


def crop_rows(core, count, crops, after=()):
    def body(at, n, src, mine, other, s):
        wide = src[...].astype(F32).reshape(ROWS, D)
        for g in range(NG):
            s[g] = wide[:, LANE * g : LANE * (g + 1)]
        for k in range(HALF):
            for out, c in ((mine, at[0]), (other, 1 - at[0])):
                crop = HALF * c + k
                keep = jnp.where(crop < n[0], 1.0, 0.0).astype(F32)
                for g in range(NG):
                    move_rows(out, g, k, HALF, s, crop, C, keep)

    return call(
        body, (core, count, crops), [SM, SM, VM], [shape((NG, PIECE, LANE), F32)] * 2, [VM] * 2, cost(2.5), "crop_rows", after, scratch=[pltpu.VMEM((NG, ROWS, LANE), F32)],
    )


def weave(dest, pieces):
    for b, piece in enumerate(pieces):
        for k in range(HALF):
            for g in range(NG):
                move_rows(dest, g, HALF * b + k, C, piece, k, HALF)


def own_quadrants(x_at, both_halves, rolled, after=()):
    def body(x, src, mine, other, full, s):
        if rolled:
            put_rolled(full, src, x[0], True)
        else:
            full[...] = src[x[0]].reshape(ROWS, D)
        for g in range(NG):
            s[g] = full[:, LANE * g : LANE * (g + 1)]
        for b, out in enumerate((mine, other)):
            for k in range(HALF):
                for g in range(NG):
                    move_rows(out, g, k, HALF, s, HALF * b + k, C)

    return call(
        body, (x_at, both_halves), [SM, VM], [shape((NG, PIECE, LANE), F32)] * 2, [VM] * 2, cost(3), "own_quadrants", after, scratch=[pltpu.VMEM((ROWS, D), F32), pltpu.VMEM((NG, ROWS, LANE), F32)],
    )


def token_major(core, count, mine, theirs, after=()):
    def body(at, n, a, b, out, s):
        for k in range(HALF):
            for src, c in ((a, at[0]), (b, 1 - at[0])):
                crop = HALF * c + k
                keep = jnp.where(crop < n[0], 1.0, 0.0).astype(F32)
                for g in range(NG):
                    move_rows(s, g, crop, C, src, k, HALF, keep)
        for g in range(NG):
            out[:, :, LANE * g : LANE * (g + 1)] = s[g].reshape(T, C, LANE).astype(BF16)

    return call(
        body, (core, count, mine, theirs), [SM, SM, VM, VM], shape((T, C, D), BF16), VM, cost(2.5), "token_major", after, scratch=[pltpu.VMEM((NG, ROWS, LANE), F32)],
    )


def crop_major(core, mine, theirs, after=()):
    def body(at, a, b, out):
        for k in range(HALF):
            for src, c in ((a, at[0]), (b, 1 - at[0])):
                for g in range(NG):
                    for start, n in ((0, WHOLE), (WHOLE, T - WHOLE)):
                        to = (HALF * c + k) * (T * NG) + g + NG * start
                        out[rows_of(to, n, NG), :] = src[g, rows_of(k + HALF * start, n, HALF), :]

    return call(
        body, (core, mine, theirs), [SM, VM, VM], shape((C * T * NG, LANE), F32), VM, cost(2.5), "crop_major", after,
    )


def fwd_body(b, which, *refs):
    a = pl.program_id(0)
    if b == 0:
        at_x, p0, p1, *rest = refs
    else:
        core, src, *rest = refs
    (
        bias, ln1g, ln1b, bq, bv, bout, ln2g, ln2b, bup, bdown,
        wqkv_h, wout_h, wup_h, wdown_h,
        z_h, h_h, qkvc_h, o_h, y_h, h2_h, g_h, gp_h, zn_o,
        wqkv, wout, wup, wdown, qkv_s, o_s, bqkv, bias_s,
        z_o, h_o, qkvc_o, o_o, y_o, h2_o, g_o, gp_o, sem_q, sem_o, sem_u, sem_d, sem_out,
    ) = rest
    at = at_x[0] ^ which if b == 0 else a
    results = (
        (z_o, z_h), (h_o, h_h), (qkvc_o, qkvc_h), (o_o, o_h), (y_o, y_h), (h2_o, h2_h), (g_o, g_h), (gp_o, gp_h),
    )

    def out(k):
        return pltpu.make_async_copy(results[k][0].at[0], results[k][1].at[at], sem_out.at[k])

    def free(k):
        @pl.when(a > 0)
        def _():
            out(k).wait()

    def cp_q(n):
        return pltpu.make_async_copy(
            wqkv_h.at[b, :, lanes_at(n, QCH)], wqkv.at[:, lanes_at(n, QCH)], sem_q.at[n]
        )

    def cp_u(n):
        return pltpu.make_async_copy(
            wup_h.at[b, :, lanes_at(n, FCH)], wup.at[:, lanes_at(n, FCH)], sem_u.at[n]
        )

    def cp_d(n):
        return pltpu.make_async_copy(
            wdown_h.at[b, lanes_at(n, FCH), :], wdown.at[lanes_at(n, FCH), :], sem_d.at[n]
        )

    cp_o = pltpu.make_async_copy(wout_h.at[b], wout, sem_o)

    def wait(copy):
        @pl.when(a == 0)
        def _():
            copy.wait()

    @pl.when(a == 0)
    def _():
        for n in range(N_Q):
            cp_q(n).start()
        cp_o.start()
        for n in range(N_F):
            cp_u(n).start()
            cp_d(n).start()
        bqkv[:, 0:D] = bq[b : b + 1, :]
        bqkv[:, D : 2 * D] = jnp.zeros((1, D), F32)
        bqkv[:, 2 * D :] = bv[b : b + 1, :]
        qkv_s[:, ROWS:, :] = jnp.zeros((3 * NG, PAD_ROWS - ROWS, LANE), F32)

    free(0)
    if b == 0:
        weave(o_s, (p0, p1))
        for g in range(NG):
            z_o[0, :, LANE * g : LANE * (g + 1)] = o_s[g, 0:ROWS, :]
    else:
        put_rolled(z_o.at[0], src, a, False)
        for w in range(2):
            mask = shift_mask(a, core[0] ^ w)
            for g in range(NG):
                bias_s[w * NG + g] = bias[NG + g] + mask
    out(0).start()
    normed, _ = norm_parts(z_o[0])
    free(1)
    h_o[0] = (normed * ln1g[b : b + 1, :] + ln1b[b : b + 1, :]).astype(BF16)
    out(1).start()

    def qkv_step(n, _):
        wait(cp_q(n))
        joint = nn(h_o[0], wqkv[:, lanes_at(n, QCH)]) + bqkv[:, lanes_at(n, QCH)]
        joint = joint * jnp.where(n < D // QCH, SCALE, 1.0)
        joint = joint.astype(BF16).astype(F32)
        for k in range(QCH // LANE):
            qkv_s[n * (QCH // LANE) + k, 0:ROWS, :] = joint[:, LANE * k : LANE * (k + 1)]
        return 0

    lax.fori_loop(0, N_Q, qkv_step, 0)
    masks = head_masks(TP)
    ones = [m.astype(F32).astype(BF16) for m in head_masks(TQ)]

    def attend(step, _):
        items = [(step * WIN + i, g) for i in range(WIN) for g in range(NG)]
        qs = [qkv_s[g, rows_of(w, TQ), :].astype(BF16) for w, g in items]
        ks = [qkv_s[NG + g, rows_of(w, TP), :].astype(BF16) for w, g in items]
        vs = [qkv_s[2 * NG + g, rows_of(w, TP), :].astype(BF16) for w, g in items]
        for (w, g), q, k, v in zip(items, qs, ks, vs):
            qkvc_o[0, w, g] = q
            qkvc_o[0, w, NG + g, 0:TP] = k
            qkvc_o[0, w, 2 * NG + g, 0:TP] = v
        added = [bias[g] if b == 0 else bias_s[w // HALF * NG + g] for w, g in items]
        scores = [nt(k, spread(q, ones)) + extra for k, q, extra in zip(ks, qs, added)]
        probs = [soft(score).astype(BF16) for score in scores]
        for (w, g), prob, v in zip(items, probs, vs):
            o_s[g, rows_of(w, TP), :] = gather_heads(tn(prob, v), masks)
        return 0

    free(2)
    lax.fori_loop(0, C // WIN, attend, 0, unroll=2)
    out(2).start()
    free(3)
    for g in range(NG):
        o_o[0, :, LANE * g : LANE * (g + 1)] = o_s[g, 0:ROWS, :].astype(BF16)
    out(3).start()
    wait(cp_o)
    free(4)
    y_o[0] = z_o[0] + (nn(o_o[0], wout[...]) + bout[b : b + 1, :])
    out(4).start()
    normed, _ = norm_parts(y_o[0])
    free(5)
    h2_o[0] = (normed * ln2g[b : b + 1, :] + ln2b[b : b + 1, :]).astype(BF16)
    out(5).start()
    free(6)
    free(7)
    def mlp_step(n, _):
        wait(cp_u(n))
        up = nn(h2_o[0], wup[:, lanes_at(n, FCH)]) + bup[b : b + 1, lanes_at(n, FCH)]
        act, slope = gelu_parts(up)
        g_o[0, :, lanes_at(n, FCH)] = act.astype(BF16)
        gp_o[0, :, lanes_at(n, FCH)] = slope.astype(BF16)
        return 0

    lax.fori_loop(0, N_F, mlp_step, 0)
    out(6).start()
    out(7).start()
    for n in range(N_F):
        wait(cp_d(n))
    zn_o[0] = (y_o[0] + (nn(g_o[0], wdown[...]) + bdown[b : b + 1, :])).reshape(T, C, D)

    @pl.when(a == pl.num_programs(0) - 1)
    def _():
        for k in range(len(results)):
            out(k).wait()


def block_fwd(b, sources, bias, p, which=None, after=()):
    outs = [
        shape((2, ROWS, D), F32),
        shape((2, ROWS, D), BF16),
        shape((2, C, 3 * NG, TQ, LANE), BF16),
        shape((2, ROWS, D), BF16),
        shape((2, ROWS, D), F32),
        shape((2, ROWS, D), BF16),
        shape((2, ROWS, FF), BF16),
        shape((2, ROWS, FF), BF16),
        shape((2, T, C, D), F32),
    ]
    if b == 0:
        specs = [fixed((NG, PIECE, LANE), True)] * 2
        out_specs = [pl.BlockSpec((1, T, C, D), lambda a, s: (s[0] ^ which, 0, 0, 0))]
    else:
        specs = [SM, fixed((2, T, C, D), True)]
        out_specs = [per_half((T, C, D))]
    small = (bias, p["ln1_gain"], p["ln1_bias"], p["b_query"], p["b_value"], p["b_out"],
             p["ln2_gain"], p["ln2_bias"], p["b_up"], p["b_down"])
    big = (p["w_qkv"], p["w_out"], p["w_up"], p["w_down"])
    return call(
        functools.partial(fwd_body, b, which),
        (*sources, *small, *big),
        specs + [fixed(v.shape, True) for v in small] + [ANY] * 4,
        outs,
        [ANY] * 8 + out_specs,
        cost(21 if which is not None else 36),
        f"forward_{b}",
        after,
        grid=(2 if which is None else 1,),
        scalars=int(which is not None),
        reuse=len(outs) if which == 1 else 0,
        scratch=[
            pltpu.VMEM((D, 3 * D), BF16),
            pltpu.VMEM((D, D), BF16),
            pltpu.VMEM((D, FF), BF16),
            pltpu.VMEM((FF, D), BF16),
            pltpu.VMEM((3 * NG, PAD_ROWS, LANE), F32),
            pltpu.VMEM((NG, PAD_ROWS, LANE), F32),
            pltpu.VMEM((1, 3 * D), F32),
            pltpu.VMEM((2 * NG, TP, GT), F32),
            *(pltpu.VMEM((1, *o.shape[1:]), o.dtype) for o in outs[:8]),
            pltpu.SemaphoreType.DMA((N_Q,)),
            pltpu.SemaphoreType.DMA,
            pltpu.SemaphoreType.DMA((N_F,)),
            pltpu.SemaphoreType.DMA((N_F,)),
            pltpu.SemaphoreType.DMA((8,)),
        ],
    )


def mlp_back_body(b, x_at, core, *refs):
    if b == 1:
        (*pieces, y, gp, act, hid, ln2g,
         wdown_h, wup_h, dd_o, da_o, dy_o, sv_o, down_o, up_o,
         wdown, wup, dz, dd, da_s, src, woven, sem_d, sem_u) = refs
    else:
        (src, y, gp, act, hid, ln2g,
         wdown_h, wup_h, dd_o, da_o, dy_o, sv_o, down_o, up_o,
         wdown, wup, dz, dd, da_s, sem_d, sem_u) = refs
    a = pl.program_id(0)

    def cp_u(n):
        return pltpu.make_async_copy(
            wup_h.at[b, :, lanes_at(n, D)], wup.at[:, lanes_at(n, D)], sem_u.at[n]
        )

    def cp_d(n):
        return pltpu.make_async_copy(
            wdown_h.at[b, lanes_at(n, D), :], wdown.at[lanes_at(n, D), :], sem_d.at[n]
        )

    def wait(copy):
        @pl.when(a == 0)
        def _():
            copy.wait()

    @pl.when(a == 0)
    def _():
        for n in range(4):
            cp_d(n).start()
            cp_u(n).start()
        sv_o[...] = jnp.zeros_like(sv_o)
        if b == 1:
            for k in range(2):
                weave(woven, pieces[2 * k : 2 * k + 2])
                for g in range(NG):
                    src[x_at[0] ^ k, :, :, LANE * g : LANE * (g + 1)] = woven[g].reshape(T, C, LANE)

    put_rolled(dz, src, a, b == 0)
    low = dz[...].astype(BF16)
    dd[...] = low
    sv_o[3:4, :] += colsum(low.astype(F32))
    for x in range(2):

        @pl.when(x_at[0] == x)
        def _():
            for c in range(2):
                w = 2 * x + c
                dd_o[c, 0] = dd[:, MINE * w : MINE * (w + 1)]

    def step(n, _):
        wait(cp_d(2 * n))
        wait(cp_d(2 * n + 1))
        grad_act = nt(dd[...], wdown[lanes_at(n, 2 * D), :])
        da = (grad_act * gp[0, :, lanes_at(n, 2 * D)].astype(F32)).astype(BF16)
        da_s[:, lanes_at(n, 2 * D)] = da

        @pl.when(n == x_at[0])
        def _():
            da_o[0] = da

        sums = colsum(da.astype(F32))
        for k in range(2):
            sv_o[pl.ds(4 + 2 * n + k, 1), :] += sums[:, D * k : D * (k + 1)]
        return 0

    lax.fori_loop(0, 2, step, 0)
    for n in range(4):
        wait(cp_u(n))
    dh2 = nt(da_s[...], wup[...])
    normed, inverse = norm_parts(y[0])
    sv_o[0:1, :] += colsum(dh2 * normed)
    sv_o[1:2, :] += colsum(dh2)
    dy = dz[...] + norm_back(dh2, normed, inverse, ln2g[b : b + 1, :])
    dy_o[0] = dy
    sv_o[2:3, :] += colsum(dy.astype(BF16).astype(F32))
    down = tn(dd_o[1 - core[0], 0], act[0])
    up = tn(hid[0], da_o[0, :, lanes_at(1 - core[0], D)])

    def put(add):
        for k in range(8):
            add_down(down_o, k, down[:, W_UP * k : W_UP * (k + 1)], add)
            rows = up[D // 8 * k : D // 8 * (k + 1)]
            up_o[k] = up_o[k] + rows if add else rows

    for half in range(2):
        pl.when(a == half)(functools.partial(put, half == 1))


def mlp_back(b, x_at, core, src, y, gp, act, hid, p, after=()):
    return call(
        functools.partial(mlp_back_body, b),
        (x_at, core, *src, y, gp, act, hid, p["ln2_gain"], p["w_down"], p["w_up"]),
        [SM, SM, *(fixed(v.shape, True) for v in src), per_half((ROWS, D)), per_half((ROWS, FF)), per_half((ROWS, FF)),
         per_half((ROWS, D)), fixed((2, D)), ANY, ANY],
        [
            shape((2, 2, ROWS, MINE), BF16),
            shape((2, ROWS, FF // 2), BF16),
            shape((2, ROWS, D), F32),
            shape((8, D), F32),
            shape((8, *BLOCK), F32),
            shape((8, *BLOCK), F32),
        ],
        [
            pl.BlockSpec((2, 1, ROWS, MINE), lambda a: (0, a, 0, 0)),
            per_half((ROWS, FF // 2)),
            per_half((ROWS, D)),
            fixed((8, D)),
            fixed((8, *BLOCK), True),
            fixed((8, *BLOCK), True),
        ],
        cost(22),
        f"mlp_back_{b}",
        after,
        grid=(2,),
        scratch=[
            pltpu.VMEM((FF, D), BF16),
            pltpu.VMEM((D, FF), BF16),
            pltpu.VMEM((ROWS, D), F32),
            pltpu.VMEM((ROWS, D), BF16),
            pltpu.VMEM((ROWS, FF), BF16),
            *([pltpu.VMEM((2, T, C, D), F32), pltpu.VMEM((NG, ROWS, LANE), F32)] if b else []),
            pltpu.SemaphoreType.DMA((4,)),
            pltpu.SemaphoreType.DMA((4,)),
        ],
    )


TABLE = 256
BLOCK = (D // 8, D)


def row_of(t):
    return sum((t >= SIDE * k).astype(jnp.int32) for k in range(1, 10))


def shift_mask(a, column):
    u = lax.broadcasted_iota(jnp.int32, (TP, GT), 0)
    t = lax.broadcasted_iota(jnp.int32, (TP, GT), 1) & (TQ - 1)
    iu, it = row_of(u), row_of(t)
    rows = (iu >= 4) != (it >= 4)
    cols = (u - SIDE * iu >= 4) != (t - SIDE * it >= 4)
    return jnp.where((rows & (a == 1)) | (cols & (column == 1)), -100.0, 0.0)


def table_sums(ds, moved):
    row = lax.broadcasted_iota(jnp.int32, (GT, PER * LANE), 0)
    col = lax.broadcasted_iota(jnp.int32, (GT, PER * LANE), 1)
    t = row & (TQ - 1)
    there = (row >> 6 == col >> 7) & (t < T) & ((col & (LANE - 1)) == t + 6 * row_of(t))
    onehot = there.astype(F32).astype(BF16)
    moved[:, NG * TP :, :] = jnp.zeros((PER, (8 - NG) * TP, LANE), F32)
    for g in range(NG):
        rest = ds[g]
        total = jnp.zeros((TP, PER * LANE), F32)
        for _ in range(3):
            part = rest.astype(BF16)
            total += nn(part, onehot)
            rest = rest - part.astype(F32)
        for h in range(PER):
            moved[h, TP * g : TP * (g + 1), :] = total[:, LANE * h : LANE * (h + 1)]


def sum_table(moved, put):
    for h in range(PER):
        total = jnp.zeros((8, TABLE), F32)
        for u in range(T):
            v = moved[h, pl.ds(u, 8, stride=TP), :]
            shift = 13 * (6 - u // SIDE) + 6 - u % SIDE
            total += pltpu.roll(jnp.concatenate([v, jnp.zeros_like(v)], axis=1), shift, 1)
        put(h, total)


def attn_back_body(b, x_at, core, dy, qkvc, z, hid, att, *refs):
    bias, ln1g, *refs = refs
    if b == 0:
        sv_m0, sv_a1, sv_m1, table1, *refs = refs
    (wout_h, wqkv_h, r3_o, sv_o, sum_o, grad_o, *part_o,
     wout, wqkv, do_s, dqkv_s, dq, bias_s, ds_o, moved, dyr, sem_o, sem_q) = refs
    a = pl.program_id(0)
    cp_o = pltpu.make_async_copy(wout_h.at[b], wout, sem_o)

    def cp_q(n):
        return pltpu.make_async_copy(
            wqkv_h.at[b, :, lanes_at(n, QCH)], wqkv.at[:, lanes_at(n, QCH)], sem_q.at[n]
        )

    def wait(copy):
        @pl.when(a == 0)
        def _():
            copy.wait()

    @pl.when(a == 0)
    def _():
        cp_o.start()
        for n in range(N_Q):
            cp_q(n).start()
        do_s[:, ROWS:, :] = jnp.zeros((NG, PAD_ROWS - ROWS, LANE), F32)
        ds_o[...] = jnp.zeros_like(ds_o)
        sv_o[...] = jnp.zeros_like(sv_o)

    if b == 1:
        for w in range(2):
            mask = shift_mask(a, core[0] ^ w)
            for g in range(NG):
                bias_s[w * NG + g] = bias[NG + g] + mask
    dyr[...] = dy[0].astype(BF16)
    wait(cp_o)
    do = nt(dyr[...], wout[...]).astype(BF16).astype(F32)
    for g in range(NG):
        do_s[g, 0:ROWS, :] = do[:, LANE * g : LANE * (g + 1)]
    masks = head_masks(TP)
    ones = [m.astype(F32).astype(BF16) for m in head_masks(TQ)]

    def attend(step, _):
        items = [(step * WIN + i, g) for i in range(WIN) for g in range(NG)]
        ks = [qkvc[0, w, NG + g, 0:TP] for w, g in items]
        q_wide = [spread(qkvc[0, w, g], ones) for w, g in items]
        do_wide = [spread(do_s[g, rows_of(w, TQ), :].astype(BF16), ones) for w, g in items]
        added = [bias[g] if b == 0 else bias_s[w // HALF * NG + g] for w, g in items]
        scores = [nt(k, q) + extra for k, q, extra in zip(ks, q_wide, added)]
        dprobs = [nt(qkvc[0, w, 2 * NG + g, 0:TP], d) for (w, g), d in zip(items, do_wide)]
        probs = [soft(score) for score in scores]
        weighted = [p * d for p, d in zip(probs, dprobs)]
        ds = [x - p * jnp.sum(x, axis=0, keepdims=True) for x, p in zip(weighted, probs)]
        for (w, g), d in zip(items, ds):
            ds_o[g] += d
        low = [d.astype(BF16) for d in ds]
        dks = [nn(x, q) for x, q in zip(low, q_wide)]
        dvs = [nn(p.astype(BF16), d) for p, d in zip(probs, do_wide)]
        dqs = [tn(x, k) for x, k in zip(low, ks)]
        for (w, g), d_q, d_k, d_v in zip(items, dqs, dks, dvs):
            dqkv_s[g, rows_of(w, TP), :] = gather_heads(d_q, masks) * SCALE
            dqkv_s[NG + g, rows_of(w, TP), :] = d_k
            dqkv_s[2 * NG + g, rows_of(w, TP), :] = d_v
        return 0

    lax.fori_loop(0, C // WIN, attend, 0)
    for g in range(3 * NG):
        dq[:, LANE * g : LANE * (g + 1)] = dqkv_s[g, 0:ROWS, :].astype(BF16)
    sv_o[2:3, :] += colsum(dq[:, 0:D].astype(F32))
    sv_o[3:4, :] += colsum(dq[:, 2 * D :].astype(F32))
    for n in range(N_Q):
        wait(cp_q(n))
    dh = nt(dq[...], wqkv[...])
    for x in range(2):

        @pl.when(x_at[0] == x)
        def _():
            for c in range(2):
                w = 2 * x + c
                r3_o[c, 0] = jnp.concatenate(
                    [dq[:, 3 * MINE * w : 3 * MINE * (w + 1)], dyr[:, MINE * w : MINE * (w + 1)]], axis=1
                )

    normed, inverse = norm_parts(z[0])
    sv_o[0:1, :] += colsum(dh * normed)
    sv_o[1:2, :] += colsum(dh)
    grad_o[0] = (dy[0] + norm_back(dh, normed, inverse, ln1g[b : b + 1, :])).reshape(T, C, D)
    other = r3_o[1 - core[0], 0]
    parts = [attn_columns(tn, hid[0], att[0], other[:, W_UP * n : W_UP * (n + 1)], W_UP * n, W_UP) for n in range(2)]

    def put_parts(add):
        for out, part in zip(part_o, parts):
            blocks = part.reshape(8, D // 8, W_UP)
            out[...] = out[...] + blocks if add else blocks

    for half in range(2):
        pl.when(a == half)(functools.partial(put_parts, half == 1))

    @pl.when(a == 1)
    def _():
        table_sums(ds_o, moved)
        if b == 1:
            sum_table(moved, lambda h, v: sum_o.__setitem__(h, v))
            return
        sum_o[...] = jnp.zeros_like(sum_o)
        for at, ref in ((0, sv_o), (4, sv_m0), (12, sv_a1), (16, sv_m1)):
            for k in range(2):
                sum_o[24 * k + at : 24 * k + at + ref.shape[0], :] = ref[:, W_UP * k : W_UP * (k + 1)]

        def put(h, v, at=48):
            sum_o[at + NG * h : at + NG * (h + 1), 0:TABLE] = v[0:NG]

        sum_table(moved, put)
        for h in range(PER):
            put(h, table1[h], 72)


def attn_back(b, x_at, core, dy, qkvc, z, hid, att, bias, p, sums=(), after=()):
    sum_shape = (PER, 8, TABLE) if b else (D // 8, W_UP)
    return call(
        functools.partial(attn_back_body, b),
        (x_at, core, dy, qkvc, z, hid, att, bias, p["ln1_gain"], *sums, p["w_out"], p["w_qkv"]),
        [SM, SM, per_half((ROWS, D)), per_half((C, 3 * NG, TQ, LANE))] + [per_half((ROWS, D))] * 3
        + [fixed(bias.shape, True), fixed((2, D)), *(fixed(v.shape) for v in sums), ANY, ANY],
        [shape((2, 2, ROWS, D), BF16), shape((4, D), F32), shape(sum_shape, F32), shape((2, T, C, D), F32)]
        + [shape((8, D // 8, W_UP), F32)] * 2,
        [
            pl.BlockSpec((2, 1, ROWS, D), lambda a: (0, a, 0, 0)),
            fixed((4, D)),
            fixed(sum_shape),
            per_half((T, C, D)),
        ]
        + [fixed((8, D // 8, W_UP), True)] * 2,
        cost(31),
        f"attn_back_{b}",
        after,
        grid=(2,),
        scratch=[
            pltpu.VMEM((D, D), BF16),
            pltpu.VMEM((D, 3 * D), BF16),
            pltpu.VMEM((NG, PAD_ROWS, LANE), F32),
            pltpu.VMEM((3 * NG, PAD_ROWS, LANE), F32),
            pltpu.VMEM((ROWS, 3 * D), BF16),
            pltpu.VMEM((2 * NG, TP, GT), F32),
            pltpu.VMEM((NG, TP, GT), F32),
            pltpu.VMEM((PER, 8 * TP, LANE), F32),
            pltpu.VMEM((ROWS, D), BF16),
            pltpu.SemaphoreType.DMA,
            pltpu.SemaphoreType.DMA((N_Q,)),
        ],
    )


def halves(left, right):
    return tn(left(0), right(0)) + tn(left(1), right(1))


def insert_bit(i, place, bit):
    return ((i >> place) << (place + 1)) | (bit << place) | (i & ((1 << place) - 1))


def row_pairs(values, k):
    height = values.shape[0] // 8
    for i in range(4):
        low = insert_bit(i, k, 0)
        high = low | (1 << k)
        yield i, low, high, values[height * low : height * (low + 1)], values[height * high : height * (high + 1)]


def put_down(out, i, total):
    half = MINE // 2
    out[i, :, 0:W_UP] = total[0:half]
    out[i, :, W_UP:] = total[half:]


def add_down(out, i, total, add):
    put_down(out, i, total + get_down(out[i]) if add else total)


def get_down(block):
    return jnp.concatenate([block[:, 0:W_UP], block[:, W_UP:]], axis=0)


def down_mine(bits, dd, act, recv, first, after=()):
    def body(s, l, rk, rs, gk, gs, keep, send):
        put_down(keep, 0, halves(lambda a: l[0, a], lambda a: rk[a]) + get_down(gk[0]))
        put_down(send, 0, halves(lambda a: l[0, a], lambda a: rs[a]) + get_down(gs[0]))

    def block(flip):
        return lambda i, s: insert_bit(i, first, s[1 + first] ^ flip)

    return call(
        body, (bits, dd, act, act, recv, recv),
        [pl.BlockSpec((1, 2, ROWS, MINE), lambda i, s: (s[0], 0, 0, 0))]
        + [pl.BlockSpec((2, ROWS, W_UP), lambda i, s, m=block(f): (0, 0, m(i, s))) for f in (0, 1)]
        + [pl.BlockSpec((1, *BLOCK), lambda i, s, m=block(f): (m(i, s), 0, 0)) for f in (0, 1)],
        [shape((4, *BLOCK), F32)] * 2, [pl.BlockSpec((1, *BLOCK), lambda i, s: (i, 0, 0))] * 2,
        cost(6.9), "down_mine", after, (4,), 1,
    )


def up_mine(bits, hid, da, recv, first, after=()):
    def body(s, l, r, got, keep, send):
        total = halves(lambda a: l[a], lambda a: r[a])
        mine = s[1 + first] == 0
        for i, j, k, p, q in row_pairs(total, first):
            p, q = p + got[j], q + got[k]
            keep[i] = jnp.where(mine, p, q)
            send[i] = jnp.where(mine, q, p)

    return call(
        body, (bits, hid, da, recv),
        [fixed((2, ROWS, D)), pl.BlockSpec((2, ROWS, W_UP), lambda n, s: (0, 0, 2 * s[0] + n)),
         pl.BlockSpec((8, D // 8, W_UP), lambda n, s: (0, 0, n))],
        [shape((4, *BLOCK), F32)] * 2, [pl.BlockSpec((4, D // 8, W_UP), lambda n, s: (0, 0, n))] * 2,
        cost(5.7), "up_mine", after, (2,), 1,
    )


def attn_columns(product, hid, att, r, lo, width):
    edge = 3 * MINE
    cut = edge // LANE * LANE
    parts = []
    if lo < cut:
        parts.append(product(hid, r[..., 0 : min(cut - lo, width)]))
    if lo + width > cut:
        lane = lax.broadcasted_iota(jnp.int32, (D, LANE), 1)
        right = r[..., cut - lo : cut - lo + LANE]
        parts.append(jnp.where(lane < edge - cut, product(hid, right), product(att, right)))
    if lo + width > cut + LANE:
        parts.append(product(att, r[..., cut - lo + LANE : width]))
    return parts[0] if len(parts) == 1 else jnp.concatenate(parts, axis=1)


def two_halves(left, right):
    return tn(left[0], right[0]) + tn(left[1], right[1])


def attn_mine(bits, hid, att, r3, recv, first, cols, small=None, after=()):
    extra = small is not None
    width = W_UP * len(cols)

    def body(s, h, o, r, *refs):
        gots, more, (keep, send) = refs[: len(cols)], refs[len(cols) : -2], refs[-2:]
        for k, n in enumerate(cols):

            @pl.when(pl.program_id(0) == k)
            def _():
                total = attn_columns(two_halves, h, o, r[0], n * W_UP, W_UP)
                mine = s[1 + first] == 0
                for i, j, jj, p, q in row_pairs(total, first):
                    p, q = p + gots[k][j], q + gots[k][jj]
                    keep[i] = jnp.where(mine, p, q)
                    send[i] = jnp.where(mine, q, p)
                if extra:
                    added = more[0][...] + more[1][...]
                    keep[4] = added
                    send[4] = added

    at = lambda n: n + cols[0]
    specs = [
        fixed((2, ROWS, D)),
        fixed((2, ROWS, D)),
        pl.BlockSpec((1, 2, ROWS, W_UP), lambda n, s: (s[0], 0, 0, at(n))),
    ]
    args = [bits, hid, att, r3]
    for n in cols:
        args.append(recv[n])
        specs.append(fixed((8, D // 8, W_UP)))
    if extra:
        args += small
        specs += [fixed((D // 8, W_UP))] * 2
    out = pl.BlockSpec((4 + extra, D // 8, W_UP), lambda n, s: (0, 0, n))
    return call(
        body, args, specs, [shape((4 + extra, D // 8, width), F32)] * 2, [out] * 2,
        cost(1.5 + 2.8 * len(cols)), "attn_mine", after, (len(cols),), 1,
    )


def split_sum(streams, extra, after=(), through=()):
    n = streams[0][1].shape[0]
    half = (n - extra) // 2

    def body(s, *refs):
        ins, outs = refs[: 4 * len(streams)], refs[4 * len(streams) + len(through) :]
        for k in range(len(streams)):
            ka, ra, kb, rb = ins[4 * k : 4 * k + 4]
            outs[2 * k][...] = ka[...] + ra[...]
            outs[2 * k + 1][...] = kb[...] + rb[...]

    args, specs = [jnp.stack([bit for *_, bit in streams])], []
    outs, out_specs = [shape(a.shape, a.dtype) for a in through], [ANY] * len(through)
    for k, (kept, recv, place, _) in enumerate(streams):
        block = (1, *recv.shape[1:])

        def at(flip, k=k, place=place, block=block):
            def index(i, s):
                j = insert_bit(i, place, s[k] ^ flip)
                return (jnp.where(i == half, 2 * half, j) if extra else j, 0, 0)

            return pl.BlockSpec(block, index)

        args += [kept, recv, kept, recv]
        specs += [at(0), at(0), at(1), at(1)]
        outs += [shape((half + extra, *recv.shape[1:]), F32)] * 2
        out_specs += [pl.BlockSpec(block, lambda i, s: (i, 0, 0))] * 2
    size = sum(recv.size for _, recv, *_ in streams)
    return call(
        body, args, specs, outs, out_specs, cost(1.5 + size * 5e-6), "split_sum", (*through, *after), (half + extra,), 1,
        reuse=len(through),
    )


def join_steps(joint, *pairs, after=()):
    kept = [s.kept for s, _ in pairs]
    recv = [s.recv for s, _ in pairs]

    def body(s, *refs):
        ins, (keep, send) = refs[:-2], refs[-2:]
        for k in range(len(pairs)):
            mine = s[k] == 0
            low, high = (ins[k][i] + ins[len(pairs) + k][i] for i in range(2))
            keep[k] = jnp.where(mine, low, high)
            send[k] = jnp.where(mine, high, low)

    bits = jnp.stack([s.links[name][2] for s, name in pairs])
    block = kept[0].shape
    keep, send = call(
        body, (bits, *kept, *recv), [fixed(block)] * (2 * len(pairs)),
        [shape((len(pairs), *block[1:]), F32)] * 2, [fixed((len(pairs), *block[1:]))] * 2,
        cost(2), "join_steps", after, (1,), 1,
    )
    joint.send(pairs[0][1], keep, send)
    return keep


def steps(*pairs, after=(), through=()):
    args = []
    for s, name in pairs:
        args.append((s.kept, s.recv, len(s.names) - 1 - s.names.index(name), s.links[name][2]))
    outs = split_sum(args, pairs[0][0].extra, after, through)
    passed, outs = outs[: len(through)], outs[len(through) :]
    for k, (s, name) in enumerate(pairs):
        s.send(name, outs[2 * k], outs[2 * k + 1])
    return (outs[0], *passed) if through else outs[0]


class Halving:
    def __init__(self, names, links, extra=0):
        self.names, self.links, self.extra = list(names), links, extra

    def send(self, name, kept, out):
        axis, perm, _ = self.links[name]
        if name in self.names:
            self.names.remove(name)
        self.kept, self.recv = kept, lax.ppermute(out, axis, perm)
        return kept

    def step(self, name, after=()):
        return steps((self, name), after=after)

    def pair(self):
        return self.kept, self.recv


def last_sums(mlps, att0, att1, after=()):
    pairs = [*mlps, *att0, att1]

    def body(*refs):
        ins, (qkv, out, up, down, small) = refs[: 2 * len(pairs)], refs[2 * len(pairs) :]
        for b in range(2):
            up[b] = ins[2 * b][0] + ins[2 * b + 1][0]
            down[b] = get_down(ins[2 * b][1] + ins[2 * b + 1][1])
        total = [ins[2 * i][0] + ins[2 * i + 1][0] for i in range(2, 5)]
        edge = 3 * MINE
        for b, att in enumerate((jnp.concatenate(total[0:2], axis=1), total[2])):
            qkv[b] = att[:, 0:edge]
            out[b] = att[:, edge:]
        small[...] = ins[4][1] + ins[5][1]

    rows = D // 8
    return call(
        body, [a for pair in pairs for a in pair], [VM] * (2 * len(pairs)),
        [shape((2, rows, 3 * MINE), F32), shape((2, rows, MINE), F32), shape((2, rows, D), F32),
         shape((2, MINE, W_UP), F32), shape((rows, W_UP), F32)],
        [VM] * 5, cost(4), "last_sums", after,
    )


def scatter_rest(block, dim, img, sub):
    step = sub // 2
    while step:
        bit = (img // step) % 2
        half = block.shape[dim] // 2
        keep = lax.dynamic_slice_in_dim(block, bit * half, half, dim)
        send = lax.dynamic_slice_in_dim(block, (1 - bit) * half, half, dim)
        perm = [(i, i ^ step) for i in range(8 * sub)]
        block = keep + lax.ppermute(send, "img", perm)
        step //= 2
    return block


def window_bias(table, after=()):
    pairs = 16

    def body(src, out, rolled, wide):
        l = lax.broadcasted_iota(jnp.int32, (LANE, GT), 0)
        t = lax.broadcasted_iota(jnp.int32, (LANE, GT), 1) & (TQ - 1)
        at = lax.broadcasted_iota(jnp.int32, (LANE, GT), 1) >> 6
        there = (t < T) & (l == t + 6 * row_of(t))
        wide[...] = jnp.zeros_like(wide)
        for h in range(PER):
            rows = [src[k // NG, PER * (k % NG) + h : PER * (k % NG) + h + 1] for k in range(2 * NG)]
            rows = jnp.concatenate(rows + [jnp.zeros((pairs - 2 * NG, TABLE), F32)], axis=0)
            for u in range(T):
                shift = 13 * (6 - u // SIDE) + 6 - u % SIDE
                rolled[pairs * u : pairs * (u + 1), :] = pltpu.roll(rows, (TABLE - shift) % TABLE, 1)[:, 0:LANE]
            ones = (there & (at == h)).astype(F32).astype(BF16)
            rest = rolled[...]
            for _ in range(3):
                part = rest.astype(BF16)
                moved = nn(part, ones)
                for k in range(2):
                    wide[k, 0 : pairs * T, :] += moved[:, LANE * k : LANE * (k + 1)]
                rest = rest - part.astype(F32)
        real = lax.broadcasted_iota(jnp.int32, (TP, LANE), 0) < T
        for b in range(2 * NG):
            for k in range(2):
                v = wide[k, pl.ds(b, TP, stride=pairs), :]
                out[b, :, LANE * k : LANE * (k + 1)] = jnp.where(real, v, NEG)

    return call(
        body, (table,), [VM], shape((2 * NG, TP, GT), F32), VM, cost(4), "window_bias", after,
        scratch=[pltpu.VMEM((pairs * T, LANE), F32), pltpu.VMEM((2, pairs * TP, LANE), F32)],
    )


def per_device(
    tokens, crop_count, ln1_gain, ln1_bias, w_qkv, b_query, b_value, bias_table, w_out, b_out,
    ln2_gain, ln2_bias, w_up, b_up, w_down, b_down, cotangent, *, n_img,
):
    win, img = lax.axis_index("win"), lax.axis_index("img")
    sub = n_img // 8
    x_bit, core = win // 2, win % 2
    links = {}
    for k in range(3):
        links[k] = ("img", [(i, i ^ (sub << k)) for i in range(n_img)], (img // (sub << k)) % 2)
    bits = jnp.stack([core, links[0][2], links[1][2], links[2][2]])
    at_core, at_x = jnp.reshape(core, (1,)), jnp.reshape(x_bit, (1,))
    all_valid = jnp.full((1,), C, jnp.int32)
    p = dict(
        ln1_gain=ln1_gain, ln1_bias=ln1_bias, w_qkv=w_qkv, b_query=b_query, b_value=b_value,
        w_out=w_out, b_out=b_out, ln2_gain=ln2_gain, ln2_bias=ln2_bias, w_up=w_up, b_up=b_up,
        w_down=w_down, b_down=b_down,
    )

    def over(way, a):
        return lax.ppermute(a, "win", [(i, i ^ way) for i in range(4)])

    def swap(a):
        return over(1, a)

    table = jnp.pad(bias_table.transpose(0, 2, 1), ((0, 0), (0, 0), (0, TABLE - 169)))
    bias = window_bias(table)

    mine, other = crop_rows(at_core, all_valid, tokens[:, 0].transpose(1, 0, 2))
    near, far = swap(other), (over(2, mine), over(3, other))
    ct_mine, ct_other = crop_rows(at_core, crop_count, cotangent[:, 0].transpose(1, 0, 2), (mine,))
    ct_near, ct_far = swap(ct_other), (over(2, ct_mine), over(3, ct_other))
    fwd0 = block_fwd(0, (at_x, mine, near), bias, p, 0, (ct_mine,))
    fwd0 = block_fwd(0, (at_x, *far), bias, p, 1, fwd0)
    fwd1 = block_fwd(1, (at_core, fwd0[8]), bias, p)
    z0, h0, qkvc0, o0, y0, h20, g0, gp0, _ = fwd0
    z1, h1, qkvc1, o1, y1, h21, g1, gp1, zn = fwd1

    def stream(first, extra=0):
        return Halving([k for k in (2, 1, 0) if k != first], links, extra)

    down1, up1, att1, down0, up0 = (stream(k) for k in (0, 1, 0, 1, 0))
    mlp1, mlp0 = (Halving([], links) for _ in range(2))
    att0 = [stream(0, 1), stream(0)]

    dd1, da1, dy, sv_m1, *part = mlp_back(
        1, at_x, at_core, (ct_mine, ct_near, *ct_far), y1, gp1, g1, h21, p, (zn,)
    )
    down_x, up_x = (swap(a) for a in part)
    r31, sv_a1, table1, grad1, *part = attn_back(
        1, at_x, at_core, dy, qkvc1, z1, h1, o1, bias, p, (), (part[0],)
    )
    att_x = [swap(a) for a in part]
    last = down1.send(0, *down_mine(bits, dd1, g1, down_x, 0, (sv_a1,)))
    last = up1.send(1, *up_mine(bits, h21, da1, up_x, 1, (last,)))

    dd0, da0, dy, sv_m0, *part = mlp_back(0, at_x, at_core, (grad1,), y0, gp0, g0, h20, p, (last, *att_x))
    last, *part = steps((down1, 1), (up1, 0), after=(sv_m0,), through=part)
    down_x, up_x = (swap(a) for a in part)
    last = att1.send(0, *attn_mine(bits, h1, o1, r31, att_x, 0, (0, 1), None, (last,)))
    out_mine, out_other = own_quadrants(at_x, zn, True, (last,))
    out_x = swap(out_other)
    last = join_steps(mlp1, (up1, 2), (down1, 2), after=(out_mine,))
    last = down0.send(1, *down_mine(bits, dd0, g0, down_x, 1, (last,)))
    last = up0.send(0, *up_mine(bits, h20, da0, up_x, 0, (last,)))
    r30, sv_a0, small, grad0, *part = attn_back(
        0, at_x, at_core, dy, qkvc0, z0, h0, o0, bias, p, (sv_m0, sv_a1, sv_m1, table1), (last,)
    )
    last, small, *part = steps(
        (down0, 0), (up0, 1), (att1, 1), after=(sv_a0, mlp1.recv), through=(small, *part)
    )
    att_x = [swap(a) for a in part]
    small = [small, swap(small)]
    block_out = token_major(at_core, crop_count, out_mine, out_x, (last,))
    in_mine, in_other = own_quadrants(at_x, grad0, False, (block_out,))
    in_x = swap(in_other)
    last = in_mine
    kept, out = attn_mine(bits, h0, o0, r30, att_x, 0, (0,), small, (last,))
    last = att0[0].send(0, kept, out)
    last = join_steps(mlp0, (up0, 2), (down0, 2), after=(last,))
    kept, out = attn_mine(bits, h0, o0, r30, att_x, 0, (1,), None, (last,))
    last = att0[1].send(0, kept, out)
    last = att0[0].step(1, (last,))
    last = att1.step(2, (last,))
    last = att0[1].step(1, (last,))
    last = att0[0].step(2, (last, mlp0.recv))
    last = att0[1].step(2, (last,))
    grad_tokens = crop_major(at_core, in_mine, in_x, (last,))

    g_qkv, g_out, g_up, g_down, small = last_sums(
        (mlp0.pair(), mlp1.pair()), [a.pair() for a in att0], att1.pair(), (grad_tokens,)
    )
    for k in range(sub.bit_length() - 1):
        small = small + lax.ppermute(small, "img", [(i, i ^ (1 << k)) for i in range(n_img)])
    g_qkv, g_out, g_up = (scatter_rest(g, 1, img, sub) for g in (g_qkv, g_out, g_up))
    g_down = scatter_rest(g_down, 2, img, sub).transpose(0, 2, 1)
    table = small[48:, :169].reshape(2, PER, NG, 169).transpose(0, 3, 2, 1).reshape(2, 169, HEADS)
    width = D // n_img

    vectors = jnp.concatenate([small[:24], small[24:48]], axis=1).reshape(2, 12, D)
    mine = lax.dynamic_slice_in_dim(vectors[:, :8], img * width, width, 2)
    up_bias = lax.dynamic_slice_in_dim(vectors[:, 8:].reshape(2, FF), img * (4 * width), 4 * width, 1)

    return (
        block_out.transpose(1, 0, 2)[:, None], grad_tokens.reshape(C, 1, T, D), mine[:, 0], mine[:, 1], g_qkv, mine[:, 2], mine[:, 3], table,
        g_out, mine[:, 6], mine[:, 4], mine[:, 5], g_up, up_bias, g_down, mine[:, 7],
    )


def solution(mesh):
    shard = P("img", "win", None, None)
    vec, mat = P(None, "img"), P(None, "img", "win")
    return jax.shard_map(
        functools.partial(per_device, n_img=mesh.shape["img"]),
        mesh=mesh,
        in_specs=(shard, P("img")) + (P(),) * 14 + (shard,),
        out_specs=(shard, shard, vec, vec, mat, vec, vec, P(), mat, vec, vec, vec, mat, vec, mat, vec),
        check_vma=False,
    )
```
